256 devices in a mesh: quad: 16 (over z_lo, x), sx: 4 (over z_hi, core), sy: 4 (over y).
Axes of the slice: x: 4, y: 4, z: 8 (z_hi: 2, z_lo: 4; z = z_hi * 4 + z_lo), core: 2. Of those that a mesh axis runs over, the one named last changes fastest.
Arguments:
- probes: bfloat16 [64, 64, 32, 128], P(None, 'sx', 'sy'), may hold values from -6 to 6
- quad_index: int32 [16], P('quad'), may hold values from 0 to 63
- region_label: int32 [64, 64, 32], replicated, may hold values from 0 to 7
- gain_label: int32 [64, 64, 32], replicated, may hold values from 0 to 7
- region_eps: float32 [8], replicated, may hold values from 1 to 3
- gain_rate: float32 [8], replicated, may hold values from 1 to 8
Outputs:
- moment0: float32 [64, 64, 32, 128], P('quad', 'sx', 'sy')
- moment1: float32 [64, 64, 32, 128], P('quad', 'sx', 'sy')
- projections: float32 [2, 2, 64, 64], replicated
The draws below stay inside these ranges and needn't reach their ends.
All inputs are finite; a program needn't handle non-finite values.
Results may differ from the reference program's by a relative error of at most 0.0003.
Values may be sent and summed in bfloat16 or wider, within the bound.
No kernel may reach another device: no remote copies, remote signals or barrier semaphores. Data moves between devices by JAX's collectives and lax.ppermute only.
A program may use at most 128 MiB of HBM per device.

```python
import math
import jax
import jax.numpy as jnp
from jax import lax

PROBE_COUNT = 64
QUAD = 16
NREG = 8
NGAIN = 8
NZ = 64
NX = 64
NY = 32
CELLS = 131072


def draw_probes(key, part):
    key = jax.random.fold_in(key, 11)
    rough_key, amp_key, first_key, second_key = jax.random.split(key, 4)
    shape = (NZ, NX, NY, 2 * PROBE_COUNT)
    columns = 2 * PROBE_COUNT
    rough = jax.random.truncated_normal(rough_key, -3.0, 3.0, shape, jnp.float32)
    amplitude = jax.random.uniform(amp_key, (columns,), jnp.float32, -2.0, 2.0)
    first_phase = jax.random.uniform(first_key, (columns,), jnp.float32, -math.pi, math.pi)
    second_phase = jax.random.uniform(second_key, (columns,), jnp.float32, -math.pi, math.pi)
    along_x = 2.0 * math.pi / NX * jnp.arange(NX, dtype=jnp.float32)
    along_y = 2.0 * math.pi / NY * jnp.arange(NY, dtype=jnp.float32)
    wave = jnp.sin(along_x[:, None, None] + first_phase) * jnp.sin(along_y[None, :, None] + second_phase)
    smooth = amplitude * (1.0 + 0.5 * wave)
    return (rough + smooth[None]).astype(jnp.bfloat16)


def set_ends(drawn, rng, smallest, largest):
    longest = drawn.shape.index(max(drawn.shape))
    spots = []
    for shift in (0, 1):
        where = [jax.random.randint(jax.random.fold_in(rng, axis), (), 0, length) for axis, length in enumerate(drawn.shape)]
        where[longest] = (where[longest] + shift) % drawn.shape[longest]
        spots.append(tuple(where))
    return drawn.at[spots[0]].set(smallest).at[spots[1]].set(largest)


def setup_inputs(seed: int = 0) -> dict:
    seeds = jax.random.split(jax.random.key(seed), 7)
    return {
        "probes": draw_probes(jax.random.fold_in(seeds[6], 71), 0),
        "quad_index": set_ends(jax.random.randint(seeds[1], (QUAD,), 0, 4 * QUAD), jax.random.fold_in(seeds[1], 1), 0, (4 * QUAD) - 1).astype(jnp.int32),
        "region_label": set_ends(jax.random.randint(seeds[2], (NZ, NX, NY), 0, NREG), jax.random.fold_in(seeds[2], 1), 0, NREG - 1).astype(jnp.int32),
        "gain_label": set_ends(jax.random.randint(seeds[3], (NZ, NX, NY), 0, NGAIN), jax.random.fold_in(seeds[3], 1), 0, NGAIN - 1).astype(jnp.int32),
        "region_eps": jnp.clip(jnp.exp(jax.random.uniform(seeds[4], (NREG,), jnp.float32, math.log(1.0), math.log(3.0))), 1.0, 3.0),
        "gain_rate": jnp.clip(jax.random.uniform(seeds[5], (NGAIN,), jnp.float32, 1.0, 8.0), 1.0, 8.0),
    }


def multiply_by(coef_real, coef_imag, field):
    half = field.shape[-1] // 2
    field_real = field[..., :half]
    field_imag = field[..., half:]
    return jnp.concatenate([coef_real * field_real - coef_imag * field_imag, coef_real * field_imag + coef_imag * field_real], axis=-1)


def neighbour_sum(field):
    padded = jnp.pad(field, ((1, 1), (1, 1), (1, 1), (0, 0)))
    total = padded[2:, 1:-1, 1:-1] + padded[:-2, 1:-1, 1:-1]
    total = total + padded[1:-1, 2:, 1:-1] + padded[1:-1, :-2, 1:-1]
    return total + padded[1:-1, 1:-1, 2:] + padded[1:-1, 1:-1, :-2]


def assemble(cross, half):
    blocks = []
    for moment in range(2):
        first_col = 2 * half * moment
        real_cols = cross[:, first_col:first_col + half]
        imag_cols = cross[:, first_col + half:first_col + 2 * half]
        blocks.append(jnp.stack([real_cols[:half] + imag_cols[half:], imag_cols[:half] - real_cols[half:]]))
    return jnp.stack(blocks)


def reference(probes, quad_index, region_label, gain_label, region_eps, gain_rate):
    mat_real = region_eps[region_label][..., None]
    mat_imag = gain_rate[gain_label][..., None]
    source = probes.astype(jnp.float32)

    def one_node(carry, node_index):
        angle_node = (2.0 * math.pi) * (node_index.astype(jnp.float32) + 0.5) / (4 * QUAD)
        weight_real = jnp.cos(angle_node)
        weight_imag = jnp.sin(angle_node)
        node_real = 2.0 + weight_real
        node_imag = weight_imag
        diag_real = 6.0 + node_real * mat_real - node_imag * mat_imag
        diag_imag = node_real * mat_imag + node_imag * mat_real
        modulus = diag_real * diag_real + diag_imag * diag_imag
        inverse_real = diag_real / modulus
        inverse_imag = -diag_imag / modulus
        iterate = multiply_by(inverse_real, inverse_imag, source)
        for sweep in range(2):
            iterate = multiply_by(inverse_real, inverse_imag, source + neighbour_sum(iterate))
        scaled_real = weight_real * node_real - weight_imag * node_imag
        scaled_imag = weight_real * node_imag + weight_imag * node_real
        first = carry[0] + multiply_by(weight_real, weight_imag, iterate)
        second = carry[1] + multiply_by(scaled_real, scaled_imag, iterate)
        return (first, second), None

    zeros = jnp.zeros(probes.shape, jnp.float32)
    (moment0, moment1), _ = lax.scan(one_node, (zeros, zeros), quad_index)
    columns = probes.shape[-1]
    flat_source = source.reshape(-1, columns)
    both = jnp.concatenate([moment0, moment1], axis=-1).reshape(-1, 2 * columns)
    cross = jnp.dot(flat_source.T, both, precision=lax.Precision.HIGHEST, preferred_element_type=jnp.float32)
    projections = assemble(cross, columns // 2) / CELLS
    return moment0, moment1, projections
```

```python
import functools
import math

import jax
import jax.numpy as jnp
import numpy as np
from jax import lax
from jax.experimental import pallas as pl
from jax.experimental.pallas import tpu as pltpu
from jax.sharding import PartitionSpec as P

QUAD = 16
SLAB = 4
CX = 16
CY = 8
LANES = CX * CY
OUTSIDE = 64

OFFSETS = sorted(
    [(dx, dy) for dx in range(-2, 3) for dy in range(-2, 3) if abs(dx) + abs(dy) <= 2],
    key=lambda o: (abs(o[0]) + abs(o[1]), o),
)
REACH = {0: 13, 1: 5, 2: 1}
TAPS = [(dz, off) for dz in range(-2, 3) for off in range(REACH[abs(dz)])]
TAP_AT = {(dz,) + OFFSETS[off]: i for i, (dz, off) in enumerate(TAPS)}
UNITS = [(1, 0, 0), (-1, 0, 0), (0, 1, 0), (0, -1, 0), (0, 0, 1), (0, 0, -1)]
WIDE = len(OFFSETS) * LANES


def selector(cells):
    row_of = {cell: row for row, cell in enumerate(cells) if cell is not None}
    pick = np.zeros((256, WIDE), np.float32)
    for o, (dx, dy) in enumerate(OFFSETS):
        for x in range(CX):
            for y in range(CY):
                row = row_of.get((x + dx, y + dy))
                if row is not None:
                    pick[row, o * LANES + x * CY + y] = 1.0
    return pick.astype(jnp.bfloat16)


def source_cells():
    cells = [(x, y) for x in range(CX) for y in range(CY)]
    cells += [(x, y) for x in range(CX) for y in (-2, -1)]
    cells += [(x, y) for x in range(CX) for y in (CY, CY + 1)]
    for xs in ((-2, -1), (CX, CX + 1)):
        cells += [(x, y) for x in xs for y in range(CY)]
        cells += [(x, y) for x in xs for y in (-2, -1)]
        cells += [(x, y) for x in xs for y in (CY, CY + 1)]
        cells += [None] * 8
    return cells


def window_cells():
    return [(x, y) for x in range(-2, CX + 2) for y in range(-2, CY + 2)]


def material_kernel(eps_ref, gain_ref, code_ref, pick_ref, real_ref, imag_ref, inside_ref):
    codes = jnp.dot(code_ref[...], pick_ref[...], preferred_element_type=jnp.float32)
    for t, (dz, off) in enumerate(TAPS):
        row = (dz + 2) * 8
        code = codes[row : row + 8, off * LANES : (off + 1) * LANES].astype(jnp.int32)
        region = lax.shift_right_logical(code, 3)
        level = code & 7
        real = jnp.zeros((8, LANES), jnp.float32)
        imag = jnp.zeros((8, LANES), jnp.float32)
        for value in range(8):
            real = jnp.where(region == value, eps_ref[value], real)
            imag = jnp.where(level == value, gain_ref[value], imag)
        real_ref[t] = real
        imag_ref[t] = imag
        inside_ref[t] = jnp.where(code < OUTSIDE, 1.0, 0.0)


def cmul(a, b):
    return (a[0] * b[0] - a[1] * b[1], a[0] * b[1] + a[1] * b[0])


def cadd(a, b):
    return (a[0] + b[0], a[1] + b[1])


def moment_kernel(
    weight_ref,
    real_ref,
    imag_ref,
    inside_ref,
    own_ref,
    ylo_ref,
    yhi_ref,
    xlo_ref,
    xhi_ref,
    pick_ref,
    moments_ref,
    cross_ref,
    shifted,
    coef,
):
    for plane in range(SLAB + 4):
        reach = 13 if 2 <= plane < SLAB + 2 else (5 if plane in (1, SLAB + 2) else 1)
        rows = jnp.concatenate(
            [own_ref[plane], ylo_ref[plane], yhi_ref[plane], xlo_ref[plane], xhi_ref[plane]], axis=0
        )
        picked = lax.dot_general(
            rows,
            pick_ref[:, : reach * LANES],
            (((0,), (0,)), ((), ())),
            preferred_element_type=jnp.float32,
        )
        for off in range(reach):
            shifted[plane, off] = picked[:, off * LANES : (off + 1) * LANES]

    coef[...] = jnp.zeros(coef.shape, jnp.float32)
    first_half = lax.broadcasted_iota(jnp.int32, (8, LANES), 0) < SLAB

    def one_pair(pair, carry):
        weight = (
            jnp.where(first_half, weight_ref[0, 2 * pair], weight_ref[0, 2 * pair + 1]),
            jnp.where(
                first_half, weight_ref[0, QUAD + 2 * pair], weight_ref[0, QUAD + 2 * pair + 1]
            ),
        )
        node = (2.0 + weight[0], weight[1])
        inv = []
        for t in range(len(TAPS)):
            diag_real = 6.0 + node[0] * real_ref[t] - node[1] * imag_ref[t]
            diag_imag = node[0] * imag_ref[t] + node[1] * real_ref[t]
            scale = inside_ref[t] / (diag_real * diag_real + diag_imag * diag_imag)
            inv.append((diag_real * scale, -(diag_imag * scale)))
        centre = inv[TAP_AT[(0, 0, 0)]]
        lead0 = cmul(weight, centre)
        lead1 = cmul(node, lead0)
        for t, (dz, off) in enumerate(TAPS):
            step = (dz,) + OFFSETS[off]
            size = sum(abs(d) for d in step)
            if size == 0:
                near = functools.reduce(cadd, [inv[TAP_AT[u]] for u in UNITS])
                term = cmul(centre, near)
                term = (1.0 + term[0], term[1])
            elif size == 1:
                term = inv[t]
            else:
                mids = [
                    inv[TAP_AT[u]]
                    for u in UNITS
                    if sum(abs(s - d) for s, d in zip(step, u)) == 1
                ]
                term = cmul(inv[t], functools.reduce(cadd, mids))
            for k, lead in enumerate((lead0, lead1)):
                real, imag = cmul(lead, term)
                coef[4 * t + 2 * k] += real
                coef[4 * t + 2 * k + 1] += imag
        return carry

    lax.fori_loop(0, QUAD // 2, one_pair, 0)
    for i in range(4 * len(TAPS)):
        both = coef[i]
        coef[i] = both + pltpu.roll(both, SLAB, axis=0)

    half = 64
    part = 32

    def one_chunk(step, carry):
        z = step // 2
        col = pl.multiple_of((step % 2) * part, part)
        sums = [jnp.zeros((part, LANES), jnp.float32) for _ in range(4)]
        for t, (dz, off) in enumerate(TAPS):
            real = shifted[z + 2 + dz, off, pl.ds(col, part), :]
            imag = shifted[z + 2 + dz, off, pl.ds(half + col, part), :]
            for k in range(2):
                coef_real = coef[4 * t + 2 * k, pl.ds(z, 1), :]
                coef_imag = coef[4 * t + 2 * k + 1, pl.ds(z, 1), :]
                sums[2 * k] += coef_real * real - coef_imag * imag
                sums[2 * k + 1] += coef_real * imag + coef_imag * real
        for k in range(2):
            moments_ref[k, z, pl.ds(col, part), :] = sums[2 * k]
            moments_ref[k, z, pl.ds(half + col, part), :] = sums[2 * k + 1]
        return carry

    lax.fori_loop(0, 2 * SLAB, one_chunk, 0)

    cross = jnp.zeros((half, 4 * half), jnp.float32)
    for z in range(SLAB):
        left = jnp.concatenate([shifted[z + 2, 0, :half], shifted[z + 2, 0, half:]], axis=1)
        left = left.astype(jnp.bfloat16)
        rows = []
        for k in range(2):
            real = moments_ref[k, z, :half]
            imag = moments_ref[k, z, half:]
            rows.append(jnp.concatenate([real, imag], axis=1))
            rows.append(jnp.concatenate([imag, -real], axis=1))
        right = jnp.concatenate(rows, axis=0)
        high = right.astype(jnp.bfloat16)
        low = (right - high.astype(jnp.float32)).astype(jnp.bfloat16)
        for piece in (high, low):
            cross += lax.dot_general(
                left, piece, (((1,), (1,)), ((), ())), preferred_element_type=jnp.float32
            )
    cross_ref[...] = cross * (1.0 / 131072)


def turn_kernel(moments_ref, first_ref, second_ref):
    for k, out_ref in enumerate((first_ref, second_ref)):
        for z in range(SLAB):
            out_ref[z] = moments_ref[k, z].T


def swap(block, axis, bit):
    count = lax.axis_size(axis)
    return lax.ppermute(block, axis, [(i, i ^ bit) for i in range(count)])


def sum_of_four(block, axis, bits):
    first, second, third = (swap(block, axis, bit) for bit in bits)
    return (block + first) + (second + third)


def reduce_cross(cross):
    width = cross.shape[1] // 2
    core = lax.axis_index("sx") & 1
    low, high = cross[:, :width], cross[:, width:]
    mine = jnp.where(core == 0, low, high)
    block = mine + swap(jnp.where(core == 0, high, low), "sx", 1)
    block = sum_of_four(block, "sy", (1, 2, 3))
    block = sum_of_four(block, "quad", (1, 2, 3))
    block = sum_of_four(block, "quad", (4, 8, 12))
    block = block + swap(block, "sx", 2)
    other = swap(block, "sx", 1)
    return jnp.where(core == 0, block, other), jnp.where(core == 0, other, block)


def beside(block, axis, forward):
    count = lax.axis_size(axis)
    pairs = [(i, i + 1) for i in range(count - 1)]
    return lax.ppermute(block, axis, pairs if forward else [(b, a) for a, b in pairs])


def body(probes, quad_index, region_label, gain_label, region_eps, gain_rate):
    depth, cells_x, cells_y, columns = probes.shape
    me = lax.axis_index("quad")
    start_z = me * SLAB
    start_x = lax.axis_index("sx") * cells_x
    start_y = lax.axis_index("sy") * cells_y

    angle = 2.0 * math.pi * (quad_index.astype(jnp.float32) + 0.5) / (4 * QUAD)
    lane = lax.broadcasted_iota(jnp.int32, (1, 128), 1)
    weight = jnp.where(lane == me, jnp.cos(angle), 0.0)
    weight = jnp.where(lane == me + QUAD, jnp.sin(angle), weight)

    flat = probes.reshape(depth, cells_x * cells_y, columns)
    own = jnp.concatenate(
        [
            lax.dynamic_slice_in_dim(flat, jnp.maximum(start_z - 2, 0), 2, 0),
            lax.dynamic_slice_in_dim(flat, start_z, SLAB, 0),
            lax.dynamic_slice_in_dim(flat, jnp.minimum(start_z + SLAB, depth - 2), 2, 0),
        ],
        axis=0,
    )
    planes = SLAB + 4
    cube = own.reshape(planes, cells_x, cells_y, columns)
    ylo = beside(cube[:, :, -2:, :].reshape(planes, -1, columns), "sy", True)
    yhi = beside(cube[:, :, :2, :].reshape(planes, -1, columns), "sy", False)
    weight = sum_of_four(weight, "quad", (1, 2, 3))

    def edge(first):
        at = 0 if first else (cells_x - 2)
        pieces = [
            own[:, at * cells_y : (at + 2) * cells_y],
            ylo[:, at * 2 : (at + 2) * 2],
            yhi[:, at * 2 : (at + 2) * 2],
        ]
        return jnp.pad(jnp.concatenate(pieces, axis=1), ((0, 0), (0, 8), (0, 0)))

    xlo = beside(edge(False), "sx", True)
    xhi = beside(edge(True), "sx", False)
    weight = sum_of_four(weight, "quad", (4, 8, 12))

    code = jnp.pad(region_label * 8 + gain_label, 2, constant_values=OUTSIDE)
    code = lax.dynamic_slice(
        code, (start_z, start_x, start_y), (planes, cells_x + 4, cells_y + 4)
    ).astype(jnp.bfloat16)
    code = jnp.pad(code.reshape(planes, -1), ((0, 0), (0, 16)))
    code = jnp.concatenate([code[d : d + SLAB] for d in range(5) for _ in range(2)], axis=0)
    code = jnp.pad(code, ((0, 8), (0, 0)))

    smem = pl.BlockSpec(memory_space=pltpu.SMEM)
    vmem = pl.BlockSpec(memory_space=pltpu.VMEM)
    taps = len(TAPS)
    per_tap = jax.ShapeDtypeStruct((taps, 8, LANES), jnp.float32)
    real, imag, inside = pl.pallas_call(
        material_kernel,
        out_shape=[per_tap] * 3,
        in_specs=[smem, smem, vmem, vmem],
        out_specs=[vmem] * 3,
        cost_estimate=pl.CostEstimate(flops=40000000, bytes_accessed=1200000, transcendentals=0),
        name="material",
    )(region_eps, gain_rate, code, jnp.asarray(selector(window_cells())))

    moments, cross = pl.pallas_call(
        moment_kernel,
        out_shape=[
            jax.ShapeDtypeStruct((2, SLAB, columns, LANES), jnp.float32),
            jax.ShapeDtypeStruct((64, 256), jnp.float32),
        ],
        in_specs=[smem] + [vmem] * 9,
        out_specs=[vmem] * 2,
        scratch_shapes=[
            pltpu.VMEM((planes, len(OFFSETS), columns, LANES), jnp.float32),
            pltpu.VMEM((4 * taps, 8, LANES), jnp.float32),
        ],
        compiler_params=pltpu.CompilerParams(vmem_limit_bytes=32 * 1024 * 1024),
        cost_estimate=pl.CostEstimate(flops=600000000, bytes_accessed=3000000, transcendentals=0),
        name="moments",
    )(weight, real, imag, inside, own, ylo, yhi, xlo, xhi, jnp.asarray(selector(source_cells())))

    out = jax.ShapeDtypeStruct((SLAB, LANES, columns), jnp.float32)
    first, second = pl.pallas_call(
        turn_kernel,
        out_shape=[out] * 2,
        in_specs=[vmem],
        out_specs=[vmem] * 2,
        cost_estimate=pl.CostEstimate(flops=1000000, bytes_accessed=1000000, transcendentals=0),
        name="turn",
    )(moments)
    shape = (SLAB, cells_x, cells_y, columns)

    halves = reduce_cross(cross)
    projections = jnp.stack(
        [jnp.stack([half[:, :64], half[:, 64:]], axis=0) for half in halves], axis=0
    )
    return (first.reshape(shape), second.reshape(shape), projections)


def solution(mesh):
    placed = (P(None, "sx", "sy", None), P("quad"), P(), P(), P(), P())
    return jax.shard_map(
        body,
        mesh=mesh,
        in_specs=placed,
        out_specs=(P("quad", "sx", "sy", None), P("quad", "sx", "sy", None), P()),
        check_vma=False,
    )
```

```python
import functools
import math

import jax
import jax.numpy as jnp
import numpy as np
from jax import lax
from jax.experimental import pallas as pl
from jax.experimental.pallas import tpu as pltpu
from jax.sharding import PartitionSpec as P

QUAD = 16
SLAB = 4
CX = 16
CY = 8
LANES = CX * CY

OFFSETS = sorted(
    [(dx, dy) for dx in range(-2, 3) for dy in range(-2, 3) if abs(dx) + abs(dy) <= 2],
    key=lambda o: (abs(o[0]) + abs(o[1]), o),
)
REACH = {0: 13, 1: 5, 2: 1}
TAPS = [(dz, off) for dz in range(-2, 3) for off in range(REACH[abs(dz)])]
TAP_AT = {(dz,) + OFFSETS[off]: i for i, (dz, off) in enumerate(TAPS)}
UNITS = [(1, 0, 0), (-1, 0, 0), (0, 1, 0), (0, -1, 0), (0, 0, 1), (0, 0, -1)]
WIDE = len(OFFSETS) * LANES


def source_cells():
    cells = [(x, y) for x in range(CX) for y in range(CY)]
    for y in (-1, -2, CY, CY + 1):
        cells += [(x, y) for x in range(CX)]
    for xs, near in (((-2, -1), -1), ((CX, CX + 1), CX)):
        cells += [(x, y) for x in xs for y in range(CY)]
        cells += [(near, -1), (near, CY)] + [None] * 14
    return cells


def selector():
    row_of = {cell: row for row, cell in enumerate(source_cells()) if cell is not None}
    pick = np.zeros((256, WIDE), np.float32)
    for o, (dx, dy) in enumerate(OFFSETS):
        for x in range(CX):
            for y in range(CY):
                pick[row_of[(x + dx, y + dy)], o * LANES + x * CY + y] = 1.0
    return pick.astype(jnp.bfloat16)


def material_kernel(place_ref, eps_ref, gain_ref, region_ref, level_ref, out_ref, labels, codes, sems):
    planes = SLAB + 4
    first, ahead = place_ref[0], place_ref[1]
    copies = [
        pltpu.make_async_copy(ref.at[pl.ds(first, planes)], labels.at[i], sems.at[i])
        for i, ref in enumerate((region_ref, level_ref))
    ]
    for copy in copies:
        copy.start()
    depth_y, depth_x = labels.shape[2:]
    lane = lax.broadcasted_iota(jnp.int32, (depth_x, LANES), 1)
    x_row = lax.broadcasted_iota(jnp.int32, (depth_x, LANES), 0) - place_ref[2]
    picks = [
        jnp.where(x_row == lax.shift_right_logical(lane, 3) + dx, 1.0, 0.0) for dx in range(-2, 3)
    ]
    pick = jnp.concatenate(picks, axis=1).astype(jnp.bfloat16)
    y_lane = lax.broadcasted_iota(jnp.int32, (depth_y, LANES), 1) & 7
    y_row = lax.broadcasted_iota(jnp.int32, (depth_y, LANES), 0) - place_ref[3]
    for copy in copies:
        copy.wait()
    code = labels[0] * 8 + labels[1] + 1
    code = code.astype(jnp.float32).astype(jnp.bfloat16).reshape(planes * depth_y, depth_x)
    spread = jnp.dot(code, pick, preferred_element_type=jnp.float32)
    codes[...] = jnp.zeros(codes.shape, jnp.float32)
    for off, (dx, dy) in enumerate(OFFSETS):
        block = spread[:, (dx + 2) * LANES : (dx + 3) * LANES].reshape(planes, depth_y, LANES)
        picked = jnp.sum(jnp.where((y_row == y_lane + dy)[None], block, 0.0), axis=1)
        codes[off, pl.ds(ahead, planes), :] = picked
    for t, (dz, off) in enumerate(TAPS):
        row = dz + 4
        code = codes[off, row : row + SLAB, :]
        code = jnp.concatenate([code, code], axis=0).astype(jnp.int32)
        inside = code > 0
        code = code - 1
        region = lax.shift_right_logical(code, 3)
        level = code & 7
        real = jnp.zeros((8, LANES), jnp.float32)
        imag = jnp.zeros((8, LANES), jnp.float32)
        for value in range(8):
            real = jnp.where(region == value, eps_ref[value], real)
            imag = jnp.where(level == value, gain_ref[value], imag)
        out_ref[t] = real
        out_ref[len(TAPS) + t] = imag
        out_ref[2 * len(TAPS) + t] = jnp.where(inside, 1.0, 0.0)


def cmul(a, b):
    return (a[0] * b[0] - a[1] * b[1], a[0] * b[1] + a[1] * b[0])


def cadd(a, b):
    return (a[0] + b[0], a[1] + b[1])


def moment_kernel(
    weight_ref,
    material_ref,
    own_ref,
    ylo_ref,
    yhi_ref,
    xlo_ref,
    xhi_ref,
    pick_ref,
    moments_ref,
    cross_ref,
    shifted,
    coef,
):
    for plane in range(SLAB + 4):
        near, far = (plane - 1) * 16, 96 + (plane - 2) * 16
        sides = (ylo_ref, yhi_ref, xlo_ref, xhi_ref)
        if 2 <= plane < SLAB + 2:
            reach, starts = 13, (near, far)
        elif plane in (1, SLAB + 2):
            reach, starts = 5, (near, near)
        else:
            reach, starts = 1, ()
        rows = [own_ref[plane]] + [ref[i : i + 16] for ref in sides for i in starts]
        rows = jnp.concatenate(rows, axis=0) if starts else rows[0]
        picked = lax.dot_general(
            rows,
            pick_ref[: rows.shape[0], : reach * LANES],
            (((0,), (0,)), ((), ())),
            preferred_element_type=jnp.float32,
        )
        for off in range(reach):
            shifted[plane, off] = picked[:, off * LANES : (off + 1) * LANES]

    coef[...] = jnp.zeros(coef.shape, jnp.float32)
    first_half = lax.broadcasted_iota(jnp.int32, (8, LANES), 0) < SLAB

    def one_pair(pair, carry):
        weight = (
            jnp.where(first_half, weight_ref[0, 2 * pair], weight_ref[0, 2 * pair + 1]),
            jnp.where(
                first_half, weight_ref[0, QUAD + 2 * pair], weight_ref[0, QUAD + 2 * pair + 1]
            ),
        )
        node = (2.0 + weight[0], weight[1])
        inv = []
        for t in range(len(TAPS)):
            real, imag = material_ref[t], material_ref[len(TAPS) + t]
            diag_real = 6.0 + node[0] * real - node[1] * imag
            diag_imag = node[0] * imag + node[1] * real
            scale = material_ref[2 * len(TAPS) + t] / (diag_real * diag_real + diag_imag * diag_imag)
            inv.append((diag_real * scale, -(diag_imag * scale)))
        centre = inv[TAP_AT[(0, 0, 0)]]
        lead0 = cmul(weight, centre)
        lead1 = cmul(node, lead0)
        for t, (dz, off) in enumerate(TAPS):
            step = (dz,) + OFFSETS[off]
            size = sum(abs(d) for d in step)
            if size == 0:
                near = functools.reduce(cadd, [inv[TAP_AT[u]] for u in UNITS])
                term = cmul(centre, near)
                term = (1.0 + term[0], term[1])
            elif size == 1:
                term = inv[t]
            else:
                mids = [
                    inv[TAP_AT[u]]
                    for u in UNITS
                    if sum(abs(s - d) for s, d in zip(step, u)) == 1
                ]
                term = cmul(inv[t], functools.reduce(cadd, mids))
            for k, lead in enumerate((lead0, lead1)):
                real, imag = cmul(lead, term)
                coef[4 * t + 2 * k] += real
                coef[4 * t + 2 * k + 1] += imag
        return carry

    lax.fori_loop(0, QUAD // 2, one_pair, 0)
    for i in range(4 * len(TAPS)):
        both = coef[i]
        coef[i] = both + pltpu.roll(both, SLAB, axis=0)

    half = 64
    part = 32

    def one_chunk(step, carry):
        z = step // 2
        col = pl.multiple_of((step % 2) * part, part)
        sums = [jnp.zeros((part, LANES), jnp.float32) for _ in range(4)]
        for t, (dz, off) in enumerate(TAPS):
            real = shifted[z + 2 + dz, off, pl.ds(col, part), :]
            imag = shifted[z + 2 + dz, off, pl.ds(half + col, part), :]
            for k in range(2):
                coef_real = coef[4 * t + 2 * k, pl.ds(z, 1), :]
                coef_imag = coef[4 * t + 2 * k + 1, pl.ds(z, 1), :]
                sums[2 * k] += coef_real * real - coef_imag * imag
                sums[2 * k + 1] += coef_real * imag + coef_imag * real
        for k in range(2):
            moments_ref[k, z, pl.ds(col, part), :] = sums[2 * k]
            moments_ref[k, z, pl.ds(half + col, part), :] = sums[2 * k + 1]
        return carry

    lax.fori_loop(0, 2 * SLAB, one_chunk, 0)

    cross = jnp.zeros((half, 4 * half), jnp.float32)
    for z in range(SLAB):
        left = jnp.concatenate([shifted[z + 2, 0, :half], shifted[z + 2, 0, half:]], axis=1)
        left = left.astype(jnp.bfloat16)
        rows = []
        for k in range(2):
            real = moments_ref[k, z, :half]
            imag = moments_ref[k, z, half:]
            rows.append(jnp.concatenate([real, imag], axis=1))
            rows.append(jnp.concatenate([imag, -real], axis=1))
        right = jnp.concatenate(rows, axis=0)
        high = right.astype(jnp.bfloat16)
        low = (right - high.astype(jnp.float32)).astype(jnp.bfloat16)
        for piece in (high, low):
            cross += lax.dot_general(
                left, piece, (((1,), (1,)), ((), ())), preferred_element_type=jnp.float32
            )
    cross_ref[...] = cross * (1.0 / 131072)


def turn_kernel(moments_ref, first_ref, second_ref):
    for k, out_ref in enumerate((first_ref, second_ref)):
        for z in range(SLAB):
            out_ref[z] = moments_ref[k, z].T


def swap(block, **bits):
    axes = tuple(bits)
    sizes = [lax.axis_size(axis) for axis in axes]
    pairs = []
    for place in np.ndindex(*sizes):
        other = tuple(i ^ bit for i, bit in zip(place, bits.values()))
        pairs.append((int(np.ravel_multi_index(place, sizes)), int(np.ravel_multi_index(other, sizes))))
    return lax.ppermute(block, axes, pairs)


def beside(block, axis, forward):
    count = lax.axis_size(axis)
    pairs = [(i, i + 1) for i in range(count - 1)]
    return lax.ppermute(block, axis, pairs if forward else [(b, a) for a, b in pairs])


def body(probes, quad_index, region_label, gain_label, region_eps, gain_rate):
    depth, cells_x, cells_y, columns = probes.shape
    planes = SLAB + 4
    me = lax.axis_index("quad")
    start_z = me * SLAB
    start_x = lax.axis_index("sx") * cells_x
    start_y = lax.axis_index("sy") * cells_y
    core = lax.axis_index("sx") & 1

    angle = 2.0 * math.pi * (quad_index.astype(jnp.float32) + 0.5) / (4 * QUAD)
    lane = lax.broadcasted_iota(jnp.int32, (1, 128), 1)
    weight = jnp.where(lane == me, jnp.cos(angle), 0.0)
    weight = jnp.where(lane == me + QUAD, jnp.sin(angle), weight)
    weight = weight + swap(weight, quad=1)

    flat = probes.reshape(depth, cells_x * cells_y, columns)
    own = jnp.concatenate(
        [
            lax.dynamic_slice_in_dim(flat, jnp.maximum(start_z - 2, 0), 2, 0),
            lax.dynamic_slice_in_dim(flat, start_z, SLAB, 0),
            lax.dynamic_slice_in_dim(flat, jnp.minimum(start_z + SLAB, depth - 2), 2, 0),
        ],
        axis=0,
    )
    cube = own.reshape(planes, cells_x, cells_y, columns)

    def layers(near, far):
        pieces = [cube[1 : planes - 1, :, near], cube[2 : planes - 2, :, far]]
        return jnp.concatenate(pieces, axis=0).reshape(-1, columns)

    ylo = beside(layers(cells_y - 1, cells_y - 2), "sy", True)
    yhi = beside(layers(0, 1), "sy", False)
    weight = weight + swap(weight, quad=3)

    def edge(at, x):
        rows = own[1 : planes - 1, at * cells_y : (at + 2) * cells_y].reshape(-1, columns)
        corners = [
            side[16 : 16 + SLAB * 16].reshape(SLAB, 16, columns)[:, x : x + 1] for side in (ylo, yhi)
        ]
        corners = jnp.pad(jnp.concatenate(corners, axis=1), ((0, 0), (0, 14), (0, 0)))
        return jnp.concatenate([rows, corners.reshape(-1, columns)], axis=0)

    low, high = edge(0, 0), edge(cells_x - 2, cells_x - 1)
    inner = jnp.where(core == 0, high, low)
    outer = jnp.where(core == 0, low, high)
    weight, inner, outer = lax.optimization_barrier((weight, inner, outer))
    outer = lax.ppermute(outer, "sx", [(1, 2), (2, 1)])
    inner = swap(inner, sx=1)
    weight = weight + swap(weight, quad=4)
    weight, region_label, gain_label = lax.optimization_barrier((weight, region_label, gain_label))
    weight = weight + swap(weight, quad=8)

    first_plane = jnp.clip(start_z - 2, 0, depth - planes)
    place = jnp.stack([first_plane, first_plane - start_z + 4, start_x, start_y]).astype(jnp.int32)
    smem = pl.BlockSpec(memory_space=pltpu.SMEM)
    vmem = pl.BlockSpec(memory_space=pltpu.VMEM)
    anywhere = pl.BlockSpec(memory_space=pl.ANY)
    taps = len(TAPS)
    mib = 1024 * 1024
    material = pl.pallas_call(
        material_kernel,
        out_shape=jax.ShapeDtypeStruct((3 * taps, 8, LANES), jnp.float32),
        in_specs=[smem, smem, smem, anywhere, anywhere],
        out_specs=vmem,
        scratch_shapes=[
            pltpu.VMEM((2, planes) + region_label.shape[:0:-1], jnp.int32),
            pltpu.VMEM((len(OFFSETS), 16, LANES), jnp.float32),
            pltpu.SemaphoreType.DMA((2,)),
        ],
        compiler_params=pltpu.CompilerParams(vmem_limit_bytes=8 * mib),
        cost_estimate=pl.CostEstimate(flops=40000000, bytes_accessed=1200000, transcendentals=0),
        name="material",
    )(place, region_eps, gain_rate, region_label.swapaxes(1, 2), gain_label.swapaxes(1, 2))

    xlo = jnp.where(core == 0, outer, inner)
    xhi = jnp.where(core == 0, inner, outer)
    moments, cross = pl.pallas_call(
        moment_kernel,
        out_shape=[
            jax.ShapeDtypeStruct((2, SLAB, columns, LANES), jnp.float32),
            jax.ShapeDtypeStruct((64, 256), jnp.float32),
        ],
        in_specs=[smem] + [vmem] * 7,
        out_specs=[vmem] * 2,
        scratch_shapes=[
            pltpu.VMEM((planes, len(OFFSETS), columns, LANES), jnp.float32),
            pltpu.VMEM((4 * taps, 8, LANES), jnp.float32),
        ],
        compiler_params=pltpu.CompilerParams(vmem_limit_bytes=24 * mib),
        cost_estimate=pl.CostEstimate(flops=600000000, bytes_accessed=3000000, transcendentals=0),
        name="moments",
    )(weight, material, own, ylo, yhi, xlo, xhi, jnp.asarray(selector()))

    width = cross.shape[1] // 2
    block = jnp.where(core == 0, cross[:, :width], cross[:, width:])
    block = block + swap(jnp.where(core == 0, cross[:, width:], cross[:, :width]), sx=1)
    block = block + swap(block, sy=1)
    block = block + swap(block, sy=3)
    block = block + swap(block, quad=1)
    block = block + swap(block, quad=3)
    block = block + swap(block, quad=4)
    block = block + swap(block, quad=8)
    block, moments = lax.optimization_barrier((block, moments))
    block = block + swap(block, quad=8, sx=2)

    out = jax.ShapeDtypeStruct((SLAB, LANES, columns), jnp.float32)
    first, second = pl.pallas_call(
        turn_kernel,
        out_shape=[out] * 2,
        in_specs=[vmem],
        out_specs=[vmem] * 2,
        compiler_params=pltpu.CompilerParams(vmem_limit_bytes=8 * mib),
        cost_estimate=pl.CostEstimate(flops=1000000, bytes_accessed=1000000, transcendentals=0),
        name="turn",
    )(moments)
    block, first, second = lax.optimization_barrier((block, first, second))
    other = swap(block, sx=1)
    halves = (jnp.where(core == 0, block, other), jnp.where(core == 0, other, block))
    projections = jnp.stack(
        [jnp.stack([half[:, :64], half[:, 64:]], axis=0) for half in halves], axis=0
    )
    shape = (SLAB, cells_x, cells_y, columns)
    return (first.reshape(shape), second.reshape(shape), projections)


def solution(mesh):
    placed = (P(None, "sx", "sy", None), P("quad"), P(), P(), P(), P())
    return jax.shard_map(
        body,
        mesh=mesh,
        in_specs=placed,
        out_specs=(P("quad", "sx", "sy", None), P("quad", "sx", "sy", None), P()),
        check_vma=False,
    )
```

```python
import functools
import math

import jax
import jax.numpy as jnp
import numpy as np
from jax import lax
from jax.experimental import pallas as pl
from jax.experimental.pallas import tpu as pltpu
from jax.sharding import PartitionSpec as P

QUAD = 16
SLAB = 4
CX = 16
CY = 8
LANES = CX * CY

OFFSETS = sorted(
    [(dx, dy) for dx in range(-2, 3) for dy in range(-2, 3) if abs(dx) + abs(dy) <= 2],
    key=lambda o: (abs(o[0]) + abs(o[1]), o),
)
REACH = {0: 13, 1: 5, 2: 1}
TAPS = [(dz, off) for dz in range(-2, 3) for off in range(REACH[abs(dz)])]
TAP_AT = {(dz,) + OFFSETS[off]: i for i, (dz, off) in enumerate(TAPS)}
UNITS = [(1, 0, 0), (-1, 0, 0), (0, 1, 0), (0, -1, 0), (0, 0, 1), (0, 0, -1)]
WIDE = len(OFFSETS) * LANES


def source_cells():
    cells = [(x, y) for x in range(CX) for y in range(CY)]
    for y in (-1, -2, CY, CY + 1):
        cells += [(x, y) for x in range(CX)]
    for xs, near in (((-2, -1), -1), ((CX, CX + 1), CX)):
        cells += [(x, y) for x in xs for y in range(CY)]
        cells += [(near, -1), (near, CY)] + [None] * 14
    return cells


def selector():
    row_of = {cell: row for row, cell in enumerate(source_cells()) if cell is not None}
    pick = np.zeros((256, WIDE), np.float32)
    for o, (dx, dy) in enumerate(OFFSETS):
        for x in range(CX):
            for y in range(CY):
                pick[row_of[(x + dx, y + dy)], o * LANES + x * CY + y] = 1.0
    return pick.astype(jnp.bfloat16)


def slab_kernel(quad_ref, probes_ref, weight_ref, own_ref, inner_ref, outer_ref, sems):
    depth = probes_ref.shape[0]
    start = lax.axis_index("quad") * SLAB
    spans = (
        (jnp.maximum(start - 2, 0), 0, 2),
        (start, 2, SLAB),
        (jnp.minimum(start + SLAB, depth - 2), SLAB + 2, 2),
    )
    copies = [
        pltpu.make_async_copy(probes_ref.at[pl.ds(a, n)], own_ref.at[b : b + n], sems.at[i])
        for i, (a, b, n) in enumerate(spans)
    ]
    for copy in copies:
        copy.start()
    me = lax.axis_index("quad")
    index = jnp.full((1, LANES), quad_ref[0], jnp.int32).astype(jnp.float32)
    angle = 2.0 * math.pi * (index + 0.5) / (4 * QUAD)
    lane = lax.broadcasted_iota(jnp.int32, (1, LANES), 1)
    weight = jnp.where(lane == me, jnp.cos(angle), 0.0)
    weight_ref[...] = jnp.where(lane == me + QUAD, jnp.sin(angle), weight)
    row = lax.broadcasted_iota(jnp.int32, (32, LANES), 0)
    cell = lax.broadcasted_iota(jnp.int32, (32, LANES), 1)
    even = (lax.axis_index("sy") & 1) == 0
    deep = jnp.where(row < CX, 0, 1)
    picks = []
    for high in (even, jnp.logical_not(even)):
        y = jnp.where(high, CY - 1 - deep, deep)
        picks.append(jnp.where(cell == (row & (CX - 1)) * CY + y, 1.0, 0.0).astype(jnp.bfloat16))
    for copy in copies:
        copy.wait()
    for pick, out_ref in zip(picks, (inner_ref, outer_ref)):
        for plane in range(1, SLAB + 3):
            layers = jnp.dot(pick, own_ref[plane], preferred_element_type=jnp.float32)
            layers = layers.astype(jnp.bfloat16)
            out_ref[(plane - 1) * CX : plane * CX] = layers[:CX]
            if 2 <= plane < SLAB + 2:
                at = (SLAB + 2 + plane - 2) * CX
                out_ref[at : at + CX] = layers[CX:]


def material_kernel(eps_ref, gain_ref, region_ref, level_ref, out_ref, labels, codes, sems):
    planes = SLAB + 4
    start = lax.axis_index("quad") * SLAB
    first = jnp.clip(start - 2, 0, region_ref.shape[0] - planes)
    ahead = first - start + 4
    copies = [
        pltpu.make_async_copy(ref.at[pl.ds(first, planes)], labels.at[i], sems.at[i])
        for i, ref in enumerate((region_ref, level_ref))
    ]
    for copy in copies:
        copy.start()
    depth_y, depth_x = labels.shape[2:]
    lane = lax.broadcasted_iota(jnp.int32, (depth_x, LANES), 1)
    x_row = lax.broadcasted_iota(jnp.int32, (depth_x, LANES), 0) - lax.axis_index("sx") * CX
    picks = [
        jnp.where(x_row == lax.shift_right_logical(lane, 3) + dx, 1.0, 0.0) for dx in range(-2, 3)
    ]
    pick = jnp.concatenate(picks, axis=1).astype(jnp.bfloat16)
    y_lane = lax.broadcasted_iota(jnp.int32, (depth_y, LANES), 1) & 7
    y_row = lax.broadcasted_iota(jnp.int32, (depth_y, LANES), 0) - lax.axis_index("sy") * CY
    for copy in copies:
        copy.wait()
    code = labels[0] * 8 + labels[1] + 1
    code = code.astype(jnp.float32).astype(jnp.bfloat16).reshape(planes * depth_y, depth_x)
    spread = jnp.dot(code, pick, preferred_element_type=jnp.float32)
    codes[...] = jnp.zeros(codes.shape, jnp.float32)
    for off, (dx, dy) in enumerate(OFFSETS):
        block = spread[:, (dx + 2) * LANES : (dx + 3) * LANES].reshape(planes, depth_y, LANES)
        picked = jnp.sum(jnp.where((y_row == y_lane + dy)[None], block, 0.0), axis=1)
        codes[off, pl.ds(ahead, planes), :] = picked
    for t, (dz, off) in enumerate(TAPS):
        row = dz + 4
        code = codes[off, row : row + SLAB, :]
        code = jnp.concatenate([code, code], axis=0).astype(jnp.int32)
        inside = code > 0
        code = code - 1
        region = lax.shift_right_logical(code, 3)
        level = code & 7
        real = jnp.zeros((8, LANES), jnp.float32)
        imag = jnp.zeros((8, LANES), jnp.float32)
        for value in range(8):
            real = jnp.where(region == value, eps_ref[value], real)
            imag = jnp.where(level == value, gain_ref[value], imag)
        out_ref[t] = real
        out_ref[len(TAPS) + t] = imag
        out_ref[2 * len(TAPS) + t] = jnp.where(inside, 1.0, 0.0)


def cmul(a, b):
    return (a[0] * b[0] - a[1] * b[1], a[0] * b[1] + a[1] * b[0])


def cadd(a, b):
    return (a[0] + b[0], a[1] + b[1])


def moment_kernel(
    weight_ref,
    material_ref,
    own_ref,
    ylo_ref,
    yhi_ref,
    xlo_ref,
    xhi_ref,
    pick_ref,
    moments_ref,
    cross_ref,
    shifted,
    coef,
    folded,
):
    for plane in range(SLAB + 4):
        near, far = (plane - 1) * 16, 96 + (plane - 2) * 16
        sides = (ylo_ref, yhi_ref, xlo_ref, xhi_ref)
        if 2 <= plane < SLAB + 2:
            reach, starts = 13, (near, far)
        elif plane in (1, SLAB + 2):
            reach, starts = 5, (near, near)
        else:
            reach, starts = 1, ()
        rows = [own_ref[plane]] + [ref[i : i + 16] for ref in sides for i in starts]
        rows = jnp.concatenate(rows, axis=0) if starts else rows[0]
        picked = lax.dot_general(
            rows,
            pick_ref[: rows.shape[0], : reach * LANES],
            (((0,), (0,)), ((), ())),
            preferred_element_type=jnp.float32,
        )
        for off in range(reach):
            shifted[plane, off] = picked[:, off * LANES : (off + 1) * LANES]

    coef[...] = jnp.zeros(coef.shape, jnp.float32)
    first_half = lax.broadcasted_iota(jnp.int32, (8, LANES), 0) < SLAB

    def one_pair(pair, carry):
        weight = (
            jnp.where(first_half, weight_ref[0, 2 * pair], weight_ref[0, 2 * pair + 1]),
            jnp.where(
                first_half, weight_ref[0, QUAD + 2 * pair], weight_ref[0, QUAD + 2 * pair + 1]
            ),
        )
        node = (2.0 + weight[0], weight[1])
        inv = []
        for t in range(len(TAPS)):
            real, imag = material_ref[t], material_ref[len(TAPS) + t]
            diag_real = 6.0 + node[0] * real - node[1] * imag
            diag_imag = node[0] * imag + node[1] * real
            scale = material_ref[2 * len(TAPS) + t] / (diag_real * diag_real + diag_imag * diag_imag)
            inv.append((diag_real * scale, -(diag_imag * scale)))
        centre = inv[TAP_AT[(0, 0, 0)]]
        lead0 = cmul(weight, centre)
        lead1 = cmul(node, lead0)
        for t, (dz, off) in enumerate(TAPS):
            step = (dz,) + OFFSETS[off]
            size = sum(abs(d) for d in step)
            if size == 0:
                near = functools.reduce(cadd, [inv[TAP_AT[u]] for u in UNITS])
                term = cmul(centre, near)
                term = (1.0 + term[0], term[1])
            elif size == 1:
                term = inv[t]
            else:
                mids = [
                    inv[TAP_AT[u]]
                    for u in UNITS
                    if sum(abs(s - d) for s, d in zip(step, u)) == 1
                ]
                term = cmul(inv[t], functools.reduce(cadd, mids))
            for k, lead in enumerate((lead0, lead1)):
                real, imag = cmul(lead, term)
                coef[4 * t + 2 * k] += real
                coef[4 * t + 2 * k + 1] += imag
        return carry

    lax.fori_loop(0, QUAD // 2, one_pair, 0)
    for i in range(2 * len(TAPS)):
        real, imag = coef[2 * i], coef[2 * i + 1]
        real = real + pltpu.roll(real, SLAB, axis=0)
        imag = imag + pltpu.roll(imag, SLAB, axis=0)
        folded[3 * i] = real
        folded[3 * i + 1] = imag - real
        folded[3 * i + 2] = real + imag

    half = 64
    part = 32

    def one_chunk(step, carry):
        z = step // 2
        col = pl.multiple_of((step % 2) * part, part)
        sums = [jnp.zeros((part, LANES), jnp.float32) for _ in range(6)]
        for t, (dz, off) in enumerate(TAPS):
            real = shifted[z + 2 + dz, off, pl.ds(col, part), :]
            imag = shifted[z + 2 + dz, off, pl.ds(half + col, part), :]
            factors = (real + imag, real, imag)
            for i in range(6):
                sums[i] += folded[6 * t + i, pl.ds(z, 1), :] * factors[i % 3]
        for k in range(2):
            both, minus, plus = sums[3 * k : 3 * k + 3]
            moments_ref[k, z, pl.ds(col, part), :] = both - plus
            moments_ref[k, z, pl.ds(half + col, part), :] = both + minus
        return carry

    lax.fori_loop(0, 2 * SLAB, one_chunk, 0)

    cross = jnp.zeros((half, 4 * half), jnp.float32)
    for z in range(SLAB):
        left = jnp.concatenate([shifted[z + 2, 0, :half], shifted[z + 2, 0, half:]], axis=1)
        left = left.astype(jnp.bfloat16)
        rows = []
        for k in range(2):
            real = moments_ref[k, z, :half]
            imag = moments_ref[k, z, half:]
            rows.append(jnp.concatenate([real, imag], axis=1))
            rows.append(jnp.concatenate([imag, -real], axis=1))
        right = jnp.concatenate(rows, axis=0)
        high = right.astype(jnp.bfloat16)
        low = (right - high.astype(jnp.float32)).astype(jnp.bfloat16)
        for piece in (high, low):
            cross += lax.dot_general(
                left, piece, (((1,), (1,)), ((), ())), preferred_element_type=jnp.float32
            )
    cross_ref[...] = cross * (1.0 / 131072)


def turn_kernel(moments_ref, first_ref, second_ref):
    for k, out_ref in enumerate((first_ref, second_ref)):
        for z in range(SLAB):
            out_ref[z] = moments_ref[k, z].T


def turn(moments, columns):
    out = jax.ShapeDtypeStruct((SLAB, LANES, columns), jnp.float32)
    vmem = pl.BlockSpec(memory_space=pltpu.VMEM)
    return pl.pallas_call(
        turn_kernel,
        out_shape=[out] * 2,
        in_specs=[vmem],
        out_specs=[vmem] * 2,
        compiler_params=pltpu.CompilerParams(vmem_limit_bytes=8 * 1024 * 1024),
        cost_estimate=pl.CostEstimate(flops=1000000, bytes_accessed=1000000, transcendentals=0),
        name="turn",
    )(moments)


def swap(block, **bits):
    axes = tuple(bits)
    sizes = [lax.axis_size(axis) for axis in axes]
    pairs = []
    for place in np.ndindex(*sizes):
        other = tuple(i ^ bit for i, bit in zip(place, bits.values()))
        pairs.append((int(np.ravel_multi_index(place, sizes)), int(np.ravel_multi_index(other, sizes))))
    return lax.ppermute(block, axes, pairs)


def body(probes, quad_index, region_label, gain_label, region_eps, gain_rate):
    depth, cells_x, cells_y, columns = probes.shape
    planes = SLAB + 4
    core = lax.axis_index("sx") & 1

    smem = pl.BlockSpec(memory_space=pltpu.SMEM)
    vmem = pl.BlockSpec(memory_space=pltpu.VMEM)
    hbm = pl.BlockSpec(memory_space=pltpu.HBM)
    mib = 1024 * 1024
    layers = jax.ShapeDtypeStruct(((2 * SLAB + 2) * CX, columns), probes.dtype)
    weight, own, inner, outer = pl.pallas_call(
        slab_kernel,
        out_shape=[
            jax.ShapeDtypeStruct((1, LANES), jnp.float32),
            jax.ShapeDtypeStruct((planes, cells_x * cells_y, columns), probes.dtype),
            layers,
            layers,
        ],
        in_specs=[smem, hbm],
        out_specs=[vmem] * 4,
        scratch_shapes=[pltpu.SemaphoreType.DMA((3,))],
        compiler_params=pltpu.CompilerParams(vmem_limit_bytes=4 * mib),
        cost_estimate=pl.CostEstimate(flops=10000000, bytes_accessed=600000, transcendentals=0),
        name="slab",
    )(quad_index, probes.reshape(depth, cells_x * cells_y, columns))

    def sides(axis, inner, outer):
        even = (lax.axis_index(axis) & 1) == 0
        return jnp.where(even, outer, inner), jnp.where(even, inner, outer)

    middle = [(1, 2), (2, 1)]
    ylo, yhi = sides("sy", swap(inner, sy=1), lax.ppermute(outer, "sy", middle))

    weight = weight + swap(weight, quad=1)

    def edge(at, x):
        rows = own[1 : planes - 1, at * cells_y : (at + 2) * cells_y].reshape(-1, columns)
        corners = [
            side[16 : 16 + SLAB * 16].reshape(SLAB, 16, columns)[:, x : x + 1] for side in (ylo, yhi)
        ]
        corners = jnp.pad(jnp.concatenate(corners, axis=1), ((0, 0), (0, 14), (0, 0)))
        return jnp.concatenate([rows, corners.reshape(-1, columns)], axis=0)

    low, high = edge(0, 0), edge(cells_x - 2, cells_x - 1)
    inner = jnp.where(core == 0, high, low)
    outer = jnp.where(core == 0, low, high)
    weight, inner, outer, region_label, gain_label = lax.optimization_barrier(
        (weight, inner, outer, region_label, gain_label)
    )
    outer = lax.ppermute(outer, "sx", middle)
    inner = swap(inner, sx=1)
    xlo, xhi = sides("sx", inner, outer)
    weight = weight + swap(weight, quad=3)
    weight = weight + swap(weight, quad=4)
    weight = weight + swap(weight, quad=8)

    taps = len(TAPS)
    material = pl.pallas_call(
        material_kernel,
        out_shape=jax.ShapeDtypeStruct((3 * taps, 8, LANES), jnp.float32),
        in_specs=[smem, smem, hbm, hbm],
        out_specs=vmem,
        scratch_shapes=[
            pltpu.VMEM((2, planes) + region_label.shape[:0:-1], jnp.int32),
            pltpu.VMEM((len(OFFSETS), 16, LANES), jnp.float32),
            pltpu.SemaphoreType.DMA((2,)),
        ],
        compiler_params=pltpu.CompilerParams(vmem_limit_bytes=8 * mib),
        cost_estimate=pl.CostEstimate(flops=40000000, bytes_accessed=1200000, transcendentals=0),
        name="material",
    )(region_eps, gain_rate, region_label.swapaxes(1, 2), gain_label.swapaxes(1, 2))

    moments, cross = pl.pallas_call(
        moment_kernel,
        out_shape=[
            jax.ShapeDtypeStruct((2, SLAB, columns, LANES), jnp.float32),
            jax.ShapeDtypeStruct((64, 256), jnp.float32),
        ],
        in_specs=[smem] + [vmem] * 7,
        out_specs=[vmem] * 2,
        scratch_shapes=[
            pltpu.VMEM((planes, len(OFFSETS), columns, LANES), jnp.float32),
            pltpu.VMEM((4 * taps, 8, LANES), jnp.float32),
            pltpu.VMEM((6 * taps, 8, LANES), jnp.float32),
        ],
        compiler_params=pltpu.CompilerParams(vmem_limit_bytes=24 * mib),
        cost_estimate=pl.CostEstimate(flops=600000000, bytes_accessed=3000000, transcendentals=0),
        name="moments",
    )(weight, material, own, ylo, yhi, xlo, xhi, jnp.asarray(selector()))

    width = cross.shape[1] // 2
    block = jnp.where(core == 0, cross[:, :width], cross[:, width:])
    block = block + swap(jnp.where(core == 0, cross[:, width:], cross[:, :width]), sx=1)
    along_y = [dict(sy=1), dict(sy=3)]
    along_x = [dict(quad=1), dict(quad=3)]
    along_z = [dict(quad=4), dict(quad=8), dict(quad=8, sx=2)]
    rows = block.shape[0] // 2
    upper, lower = block[:rows], block[rows:]
    orders = zip(along_y + along_x + along_z, along_z + along_y + along_x)
    for i, (upper_step, lower_step) in enumerate(orders):
        if i == 3:
            upper, moments = lax.optimization_barrier((upper, moments))
        if i == 6:
            first, second = turn(moments, columns)
            upper, first, second = lax.optimization_barrier((upper, first, second))
        upper_in, lower_in = swap(upper, **upper_step), swap(lower, **lower_step)
        upper, lower = upper + upper_in, lower + lower_in
    block = jnp.concatenate([upper, lower], axis=0)
    other = swap(block, sx=1)
    halves = (jnp.where(core == 0, block, other), jnp.where(core == 0, other, block))
    projections = jnp.stack(
        [jnp.stack([half[:, :64], half[:, 64:]], axis=0) for half in halves], axis=0
    )
    shape = (SLAB, cells_x, cells_y, columns)
    return (first.reshape(shape), second.reshape(shape), projections)


def solution(mesh):
    placed = (P(None, "sx", "sy", None), P("quad"), P(), P(), P(), P())
    return jax.shard_map(
        body,
        mesh=mesh,
        in_specs=placed,
        out_specs=(P("quad", "sx", "sy", None), P("quad", "sx", "sy", None), P()),
        check_vma=False,
    )
```

```python
import functools
import math

import jax
import jax.numpy as jnp
import numpy as np
from jax import lax
from jax.experimental import pallas as pl
from jax.experimental.pallas import tpu as pltpu
from jax.sharding import PartitionSpec as P

QUAD = 16
SLAB = 4
CX = 16
CY = 8
LANES = CX * CY

OFFSETS = sorted(
    [(dx, dy) for dx in range(-2, 3) for dy in range(-2, 3) if abs(dx) + abs(dy) <= 2],
    key=lambda o: (abs(o[0]) + abs(o[1]), o),
)
REACH = {0: 13, 1: 5, 2: 1}
TAPS = [(dz, off) for dz in range(-2, 3) for off in range(REACH[abs(dz)])]
TAP_AT = {(dz,) + OFFSETS[off]: i for i, (dz, off) in enumerate(TAPS)}
UNITS = [(1, 0, 0), (-1, 0, 0), (0, 1, 0), (0, -1, 0), (0, 0, 1), (0, 0, -1)]
WIDE = len(OFFSETS) * LANES
FAR = (SLAB + 2) * CX
CORNERS = FAR + SLAB * CX
PARTS = CORNERS + 16


def source_cells():
    cells = [(x, y) for x in range(CX) for y in range(CY)]
    for y in (-1, -2, CY, CY + 1):
        cells += [(x, y) for x in range(CX)]
    for xs, near in (((-2, -1), -1), ((CX, CX + 1), CX)):
        cells += [(x, y) for x in xs for y in range(CY)]
        cells += [(near, -1), (near, CY)] + [None] * 14
    return cells


def selector():
    row_of = {cell: row for row, cell in enumerate(source_cells()) if cell is not None}
    pick = np.zeros((256, WIDE), np.float32)
    for o, (dx, dy) in enumerate(OFFSETS):
        for x in range(CX):
            for y in range(CY):
                pick[row_of[(x + dx, y + dy)], o * LANES + x * CY + y] = 1.0
    return pick.astype(jnp.bfloat16)


def slab_kernel(quad_ref, probes_ref, own_ref, first_ref, second_ref, third_ref, fourth_ref, *whole):
    depth = probes_ref.shape[0]
    me = lax.axis_index("quad")
    even_x = (lax.axis_index("sx") & 1) == 0
    even_y = (lax.axis_index("sy") & 1) == 0

    def plane(slab, p):
        return probes_ref[jnp.clip(slab * SLAB + (p - 2), 0, depth - 1)]

    def x_edge(slab, p, high):
        block = plane(slab, p)
        return jnp.where(high, block[LANES - 16 :].astype(jnp.float32), block[:16].astype(jnp.float32))

    index = jnp.full((1, LANES), quad_ref[0], jnp.int32).astype(jnp.float32)
    angle = 2.0 * math.pi * (index + 0.5) / (4 * QUAD)
    lane = lax.broadcasted_iota(jnp.int32, (1, LANES), 1)
    weight = jnp.where(lane == me, jnp.cos(angle), 0.0)
    weight = jnp.where(lane == me + QUAD, jnp.sin(angle), weight)
    row = lax.broadcasted_iota(jnp.int32, (16, LANES), 0)
    parts = jnp.zeros((16, LANES), jnp.float32)
    for i in range(3):
        part = weight.astype(jnp.bfloat16).astype(jnp.float32)
        parts = jnp.where(row == i, part, parts)
        weight = weight - part
    first_ref[PARTS : PARTS + 16] = parts.astype(jnp.bfloat16)

    for out_ref, scratch, step, high in (
        (first_ref, whole[0], 1, even_y),
        (second_ref, whole[1], 3, jnp.logical_not(even_y)),
    ):
        target = me ^ step
        for p in range(1, SLAB + 3):
            scratch[(p - 1) * LANES : p * LANES] = plane(target, p).astype(jnp.float32)
        for at, start, count, deep in ((0, 0, SLAB + 2, 0), (FAR, LANES, SLAB, 1)):
            low = scratch[pl.ds(start + deep, count * CX, stride=CY), :]
            top = scratch[pl.ds(start + CY - 1 - deep, count * CX, stride=CY), :]
            out_ref[at : at + count * CX] = jnp.where(high, top, low).astype(jnp.bfloat16)
        corners = jnp.zeros((16, LANES), jnp.float32)
        for i, (bit, edge) in enumerate(((4, even_x), (8, jnp.logical_not(even_x)))):
            cell = jnp.where(edge, CY, 0) + jnp.where(high, CY - 1, 0)
            for p in range(SLAB):
                picked = jnp.where(row == cell, x_edge(target ^ bit, p + 2, edge), 0.0)
                picked = jnp.sum(picked, axis=0, keepdims=True)
                corners = jnp.where(row == i * SLAB + p, picked, corners)
        out_ref[CORNERS : CORNERS + 16] = corners.astype(jnp.bfloat16)

    for out_ref, bit, high in ((third_ref, 4, even_x), (fourth_ref, 8, jnp.logical_not(even_x))):
        for p in range(1, SLAB + 3):
            out_ref[(p - 1) * 16 : p * 16] = x_edge(me ^ bit, p, high).astype(jnp.bfloat16)
    for p in range(SLAB + 4):
        own_ref[p] = plane(me, p)


def material_kernel(eps_ref, gain_ref, region_ref, level_ref, out_ref, labels, codes, sems):
    planes = SLAB + 4
    start = lax.axis_index("quad") * SLAB
    first = jnp.clip(start - 2, 0, region_ref.shape[0] - planes)
    ahead = first - start + 4
    copies = [
        pltpu.make_async_copy(ref.at[pl.ds(first, planes)], labels.at[i], sems.at[i])
        for i, ref in enumerate((region_ref, level_ref))
    ]
    for copy in copies:
        copy.start()
    depth_y, depth_x = labels.shape[2:]
    lane = lax.broadcasted_iota(jnp.int32, (depth_x, LANES), 1)
    x_row = lax.broadcasted_iota(jnp.int32, (depth_x, LANES), 0) - lax.axis_index("sx") * CX
    picks = [
        jnp.where(x_row == lax.shift_right_logical(lane, 3) + dx, 1.0, 0.0) for dx in range(-2, 3)
    ]
    pick = jnp.concatenate(picks, axis=1).astype(jnp.bfloat16)
    y_lane = lax.broadcasted_iota(jnp.int32, (depth_y, LANES), 1) & 7
    y_row = lax.broadcasted_iota(jnp.int32, (depth_y, LANES), 0) - lax.axis_index("sy") * CY
    for copy in copies:
        copy.wait()
    code = labels[0] * 8 + labels[1] + 1
    code = code.astype(jnp.float32).astype(jnp.bfloat16).reshape(planes * depth_y, depth_x)
    spread = jnp.dot(code, pick, preferred_element_type=jnp.float32)
    codes[...] = jnp.zeros(codes.shape, jnp.float32)
    for off, (dx, dy) in enumerate(OFFSETS):
        block = spread[:, (dx + 2) * LANES : (dx + 3) * LANES].reshape(planes, depth_y, LANES)
        picked = jnp.sum(jnp.where((y_row == y_lane + dy)[None], block, 0.0), axis=1)
        codes[off, pl.ds(ahead, planes), :] = picked
    for t, (dz, off) in enumerate(TAPS):
        row = dz + 4
        code = codes[off, row : row + SLAB, :]
        code = jnp.concatenate([code, code], axis=0).astype(jnp.int32)
        inside = code > 0
        code = code - 1
        region = lax.shift_right_logical(code, 3)
        level = code & 7
        real = jnp.zeros((8, LANES), jnp.float32)
        imag = jnp.zeros((8, LANES), jnp.float32)
        for value in range(8):
            real = jnp.where(region == value, eps_ref[value], real)
            imag = jnp.where(level == value, gain_ref[value], imag)
        out_ref[t] = real
        out_ref[len(TAPS) + t] = imag
        out_ref[2 * len(TAPS) + t] = jnp.where(inside, 1.0, 0.0)


def cmul(a, b):
    return (a[0] * b[0] - a[1] * b[1], a[0] * b[1] + a[1] * b[0])


def cadd(a, b):
    return (a[0] + b[0], a[1] + b[1])


def moment_kernel(
    weight_ref,
    material_ref,
    own_ref,
    ylo_ref,
    yhi_ref,
    xlo_ref,
    xhi_ref,
    pick_ref,
    moments_ref,
    cross_ref,
    shifted,
    coef,
    folded,
):
    for plane in range(SLAB + 4):
        near, far = (plane - 1) * 16, 96 + (plane - 2) * 16
        sides = (ylo_ref, yhi_ref, xlo_ref, xhi_ref)
        if 2 <= plane < SLAB + 2:
            reach, starts = 13, (near, far)
        elif plane in (1, SLAB + 2):
            reach, starts = 5, (near, near)
        else:
            reach, starts = 1, ()
        rows = [own_ref[plane]] + [ref[i : i + 16] for ref in sides for i in starts]
        rows = jnp.concatenate(rows, axis=0) if starts else rows[0]
        picked = lax.dot_general(
            rows,
            pick_ref[: rows.shape[0], : reach * LANES],
            (((0,), (0,)), ((), ())),
            preferred_element_type=jnp.float32,
        )
        for off in range(reach):
            shifted[plane, off] = picked[:, off * LANES : (off + 1) * LANES]

    coef[...] = jnp.zeros(coef.shape, jnp.float32)
    first_half = lax.broadcasted_iota(jnp.int32, (8, LANES), 0) < SLAB

    def one_pair(pair, carry):
        weight = (
            jnp.where(first_half, weight_ref[0, 2 * pair], weight_ref[0, 2 * pair + 1]),
            jnp.where(
                first_half, weight_ref[0, QUAD + 2 * pair], weight_ref[0, QUAD + 2 * pair + 1]
            ),
        )
        node = (2.0 + weight[0], weight[1])
        inv = []
        for t in range(len(TAPS)):
            real, imag = material_ref[t], material_ref[len(TAPS) + t]
            diag_real = 6.0 + node[0] * real - node[1] * imag
            diag_imag = node[0] * imag + node[1] * real
            scale = material_ref[2 * len(TAPS) + t] / (diag_real * diag_real + diag_imag * diag_imag)
            inv.append((diag_real * scale, -(diag_imag * scale)))
        centre = inv[TAP_AT[(0, 0, 0)]]
        lead0 = cmul(weight, centre)
        lead1 = cmul(node, lead0)
        for t, (dz, off) in enumerate(TAPS):
            step = (dz,) + OFFSETS[off]
            size = sum(abs(d) for d in step)
            if size == 0:
                near = functools.reduce(cadd, [inv[TAP_AT[u]] for u in UNITS])
                term = cmul(centre, near)
                term = (1.0 + term[0], term[1])
            elif size == 1:
                term = inv[t]
            else:
                mids = [
                    inv[TAP_AT[u]]
                    for u in UNITS
                    if sum(abs(s - d) for s, d in zip(step, u)) == 1
                ]
                term = cmul(inv[t], functools.reduce(cadd, mids))
            for k, lead in enumerate((lead0, lead1)):
                real, imag = cmul(lead, term)
                coef[4 * t + 2 * k] += real
                coef[4 * t + 2 * k + 1] += imag
        return carry

    lax.fori_loop(0, QUAD // 2, one_pair, 0)
    for i in range(2 * len(TAPS)):
        real, imag = coef[2 * i], coef[2 * i + 1]
        real = real + pltpu.roll(real, SLAB, axis=0)
        imag = imag + pltpu.roll(imag, SLAB, axis=0)
        folded[3 * i] = real
        folded[3 * i + 1] = imag - real
        folded[3 * i + 2] = real + imag

    half = 64
    part = 32

    def one_chunk(step, carry):
        z = step // 2
        col = pl.multiple_of((step % 2) * part, part)
        sums = [jnp.zeros((part, LANES), jnp.float32) for _ in range(6)]
        for t, (dz, off) in enumerate(TAPS):
            real = shifted[z + 2 + dz, off, pl.ds(col, part), :]
            imag = shifted[z + 2 + dz, off, pl.ds(half + col, part), :]
            factors = (real + imag, real, imag)
            for i in range(6):
                sums[i] += folded[6 * t + i, pl.ds(z, 1), :] * factors[i % 3]
        for k in range(2):
            both, minus, plus = sums[3 * k : 3 * k + 3]
            moments_ref[k, z, pl.ds(col, part), :] = both - plus
            moments_ref[k, z, pl.ds(half + col, part), :] = both + minus
        return carry

    lax.fori_loop(0, 2 * SLAB, one_chunk, 0)

    cross = jnp.zeros((half, 4 * half), jnp.float32)
    for z in range(SLAB):
        left = jnp.concatenate([shifted[z + 2, 0, :half], shifted[z + 2, 0, half:]], axis=1)
        left = left.astype(jnp.bfloat16)
        rows = []
        for k in range(2):
            real = moments_ref[k, z, :half]
            imag = moments_ref[k, z, half:]
            rows.append(jnp.concatenate([real, imag], axis=1))
            rows.append(jnp.concatenate([imag, -real], axis=1))
        right = jnp.concatenate(rows, axis=0)
        high = right.astype(jnp.bfloat16)
        low = (right - high.astype(jnp.float32)).astype(jnp.bfloat16)
        for piece in (high, low):
            cross += lax.dot_general(
                left, piece, (((1,), (1,)), ((), ())), preferred_element_type=jnp.float32
            )
    cross_ref[...] = cross * (1.0 / 131072)


def turn_kernel(moments_ref, first_ref, second_ref):
    for k, out_ref in enumerate((first_ref, second_ref)):
        for z in range(SLAB):
            out_ref[z] = moments_ref[k, z].T


def turn(moments, columns):
    out = jax.ShapeDtypeStruct((SLAB, LANES, columns), jnp.float32)
    vmem = pl.BlockSpec(memory_space=pltpu.VMEM)
    return pl.pallas_call(
        turn_kernel,
        out_shape=[out] * 2,
        in_specs=[vmem],
        out_specs=[vmem] * 2,
        compiler_params=pltpu.CompilerParams(vmem_limit_bytes=8 * 1024 * 1024),
        cost_estimate=pl.CostEstimate(flops=1000000, bytes_accessed=1000000, transcendentals=0),
        name="turn",
    )(moments)


def swap(block, bits):
    axes = tuple(bits)
    sizes = [lax.axis_size(axis) for axis in axes]
    pairs = []
    for place in np.ndindex(*sizes):
        other = tuple(i ^ bit for i, bit in zip(place, bits.values()))
        pairs.append((int(np.ravel_multi_index(place, sizes)), int(np.ravel_multi_index(other, sizes))))
    return lax.ppermute(block, axes, pairs)


def body(probes, quad_index, region_label, gain_label, region_eps, gain_rate):
    depth, cells_x, cells_y, columns = probes.shape
    planes = SLAB + 4
    core = lax.axis_index("sx") & 1
    even_x = core == 0
    even_y = (lax.axis_index("sy") & 1) == 0
    smem = pl.BlockSpec(memory_space=pltpu.SMEM)
    vmem = pl.BlockSpec(memory_space=pltpu.VMEM)
    hbm = pl.BlockSpec(memory_space=pltpu.HBM)
    mib = 1024 * 1024
    shapes = [
        (planes, cells_x * cells_y, columns),
        (PARTS + 16, columns),
        (PARTS, columns),
        (FAR, columns),
        (FAR, columns),
    ]
    own, first, second, third, fourth = pl.pallas_call(
        slab_kernel,
        out_shape=[jax.ShapeDtypeStruct(shape, probes.dtype) for shape in shapes],
        in_specs=[smem, vmem],
        out_specs=[vmem] * 5,
        scratch_shapes=[pltpu.VMEM(((SLAB + 2) * LANES, columns), jnp.float32)] * 2,
        compiler_params=pltpu.CompilerParams(vmem_limit_bytes=8 * mib),
        cost_estimate=pl.CostEstimate(flops=10000000, bytes_accessed=600000, transcendentals=0),
        name="slab",
    )(quad_index, probes.reshape(depth, cells_x * cells_y, columns))

    def corner_rows(at):
        cells = [inner[at : at + SLAB], outer[at : at + SLAB]]
        low, high = jnp.where(even_y, cells[1], cells[0]), jnp.where(even_y, cells[0], cells[1])
        rows = jnp.pad(jnp.stack([low, high], axis=1), ((0, 0), (0, 14), (0, 0)))
        return rows.reshape(SLAB * 16, columns)

    inner = swap(first, dict(quad=1, sy=1))
    parts = first[PARTS:] + inner[PARTS:]
    outer = swap(jnp.concatenate([second, parts], axis=0), dict(quad=3, sy=3))
    parts = parts + outer[PARTS:]
    ylo = jnp.where(even_y, outer, inner)[:CORNERS]
    yhi = jnp.where(even_y, inner, outer)[:CORNERS]
    near = swap(jnp.concatenate([third, corner_rows(CORNERS), parts], axis=0), dict(quad=4, sx=1))
    parts = parts + near[CORNERS:]
    fourth = jnp.concatenate([fourth, corner_rows(CORNERS + SLAB), parts], axis=0)
    beyond = swap(fourth, dict(quad=8, sx=3))
    parts = parts + beyond[CORNERS:]
    xlo = jnp.where(even_x, beyond, near)[:CORNERS]
    xhi = jnp.where(even_x, near, beyond)[:CORNERS]
    weight = jnp.sum(parts[:3].astype(jnp.float32), axis=0, keepdims=True)

    taps = len(TAPS)
    material = pl.pallas_call(
        material_kernel,
        out_shape=jax.ShapeDtypeStruct((3 * taps, 8, LANES), jnp.float32),
        in_specs=[smem, smem, hbm, hbm],
        out_specs=vmem,
        scratch_shapes=[
            pltpu.VMEM((2, planes) + region_label.shape[:0:-1], jnp.int32),
            pltpu.VMEM((len(OFFSETS), 16, LANES), jnp.float32),
            pltpu.SemaphoreType.DMA((2,)),
        ],
        compiler_params=pltpu.CompilerParams(vmem_limit_bytes=8 * mib),
        cost_estimate=pl.CostEstimate(flops=40000000, bytes_accessed=1200000, transcendentals=0),
        name="material",
    )(region_eps, gain_rate, region_label.swapaxes(1, 2), gain_label.swapaxes(1, 2))

    moments, cross = pl.pallas_call(
        moment_kernel,
        out_shape=[
            jax.ShapeDtypeStruct((2, SLAB, columns, LANES), jnp.float32),
            jax.ShapeDtypeStruct((64, 256), jnp.float32),
        ],
        in_specs=[smem] + [vmem] * 7,
        out_specs=[vmem] * 2,
        scratch_shapes=[
            pltpu.VMEM((planes, len(OFFSETS), columns, LANES), jnp.float32),
            pltpu.VMEM((4 * taps, 8, LANES), jnp.float32),
            pltpu.VMEM((6 * taps, 8, LANES), jnp.float32),
        ],
        compiler_params=pltpu.CompilerParams(vmem_limit_bytes=24 * mib),
        cost_estimate=pl.CostEstimate(flops=600000000, bytes_accessed=3000000, transcendentals=0),
        name="moments",
    )(weight, material, own, ylo, yhi, xlo, xhi, jnp.asarray(selector()))

    width = cross.shape[1] // 2
    block = jnp.where(core == 0, cross[:, :width], cross[:, width:])
    block = block + swap(jnp.where(core == 0, cross[:, width:], cross[:, :width]), dict(sx=1))
    for step in (dict(sy=1), dict(sy=3), dict(quad=1), dict(quad=3), dict(quad=4), dict(quad=8)):
        block = block + swap(block, step)
    block, moments = lax.optimization_barrier((block, moments))
    block = block + swap(block, dict(quad=8, sx=2))
    first, second = turn(moments, columns)
    block, first, second = lax.optimization_barrier((block, first, second))
    other = swap(block, dict(sx=1))
    halves = (jnp.where(core == 0, block, other), jnp.where(core == 0, other, block))
    projections = jnp.stack(
        [jnp.stack([half[:, :64], half[:, 64:]], axis=0) for half in halves], axis=0
    )
    shape = (SLAB, cells_x, cells_y, columns)
    return (first.reshape(shape), second.reshape(shape), projections)


def solution(mesh):
    placed = (P(None, "sx", "sy", None), P("quad"), P(), P(), P(), P())
    return jax.shard_map(
        body,
        mesh=mesh,
        in_specs=placed,
        out_specs=(P("quad", "sx", "sy", None), P("quad", "sx", "sy", None), P()),
        check_vma=False,
    )
```

```python
import functools
import math

import jax
import jax.numpy as jnp
import numpy as np
from jax import lax
from jax.experimental import pallas as pl
from jax.experimental.pallas import tpu as pltpu
from jax.sharding import PartitionSpec as P

QUAD = 16
SLAB = 4
CX = 16
CY = 8
LANES = CX * CY

OFFSETS = sorted(
    [(dx, dy) for dx in range(-2, 3) for dy in range(-2, 3) if abs(dx) + abs(dy) <= 2],
    key=lambda o: (abs(o[0]) + abs(o[1]), o),
)
REACH = {0: 13, 1: 5, 2: 1}
TAPS = [(dz, off) for dz in range(-2, 3) for off in range(REACH[abs(dz)])]
TAP_AT = {(dz,) + OFFSETS[off]: i for i, (dz, off) in enumerate(TAPS)}
UNITS = [(1, 0, 0), (-1, 0, 0), (0, 1, 0), (0, -1, 0), (0, 0, 1), (0, 0, -1)]
WIDE = len(OFFSETS) * LANES
FAR = (SLAB + 2) * CX
CORNERS = FAR + SLAB * CX
PARTS = CORNERS + 16


def source_cells():
    cells = [(x, y) for x in range(CX) for y in range(CY)]
    for y in (-1, -2, CY, CY + 1):
        cells += [(x, y) for x in range(CX)]
    for xs, near in (((-2, -1), -1), ((CX, CX + 1), CX)):
        cells += [(x, y) for x in xs for y in range(CY)]
        cells += [(near, -1), (near, CY)] + [None] * 14
    return cells


def selector():
    row_of = {cell: row for row, cell in enumerate(source_cells()) if cell is not None}
    pick = np.zeros((256, WIDE), np.float32)
    for o, (dx, dy) in enumerate(OFFSETS):
        for x in range(CX):
            for y in range(CY):
                pick[row_of[(x + dx, y + dy)], o * LANES + x * CY + y] = 1.0
    return pick.astype(jnp.bfloat16)


def slab_kernel(quad_ref, probes_ref, own_ref, first_ref, second_ref, third_ref, fourth_ref, *whole):
    depth = probes_ref.shape[0]
    me = lax.axis_index("quad")
    even_x = (lax.axis_index("sx") & 1) == 0
    even_y = (lax.axis_index("sy") & 1) == 0

    def plane(slab, p):
        return probes_ref[jnp.clip(slab * SLAB + (p - 2), 0, depth - 1)]

    def x_edge(slab, p, high):
        block = plane(slab, p)
        return jnp.where(high, block[LANES - 16 :].astype(jnp.float32), block[:16].astype(jnp.float32))

    index = jnp.full((1, LANES), quad_ref[0], jnp.int32).astype(jnp.float32)
    angle = 2.0 * math.pi * (index + 0.5) / (4 * QUAD)
    lane = lax.broadcasted_iota(jnp.int32, (1, LANES), 1)
    weight = jnp.where(lane == me, jnp.cos(angle), 0.0)
    weight = jnp.where(lane == me + QUAD, jnp.sin(angle), weight)
    row = lax.broadcasted_iota(jnp.int32, (16, LANES), 0)
    parts = jnp.zeros((16, LANES), jnp.float32)
    for i in range(3):
        part = weight.astype(jnp.bfloat16).astype(jnp.float32)
        parts = jnp.where(row == i, part, parts)
        weight = weight - part
    first_ref[PARTS : PARTS + 16] = parts.astype(jnp.bfloat16)
    second_ref[PARTS : PARTS + 16] = parts.astype(jnp.bfloat16)

    for out_ref, scratch, step, high in (
        (first_ref, whole[0], 1, even_y),
        (second_ref, whole[1], 3, jnp.logical_not(even_y)),
    ):
        target = me ^ step
        for p in range(1, SLAB + 3):
            scratch[(p - 1) * LANES : p * LANES] = plane(target, p).astype(jnp.float32)
        for at, start, count, deep in ((0, 0, SLAB + 2, 0), (FAR, LANES, SLAB, 1)):
            low = scratch[pl.ds(start + deep, count * CX, stride=CY), :]
            top = scratch[pl.ds(start + CY - 1 - deep, count * CX, stride=CY), :]
            out_ref[at : at + count * CX] = jnp.where(high, top, low).astype(jnp.bfloat16)
        corners = jnp.zeros((16, LANES), jnp.float32)
        for i, (bit, edge) in enumerate(((4, even_x), (8, jnp.logical_not(even_x)))):
            cell = jnp.where(edge, CY, 0) + jnp.where(high, CY - 1, 0)
            for p in range(SLAB):
                picked = jnp.where(row == cell, x_edge(target ^ bit, p + 2, edge), 0.0)
                picked = jnp.sum(picked, axis=0, keepdims=True)
                corners = jnp.where(row == i * SLAB + p, picked, corners)
        out_ref[CORNERS : CORNERS + 16] = corners.astype(jnp.bfloat16)

    for out_ref, bit, high in ((third_ref, 4, even_x), (fourth_ref, 8, jnp.logical_not(even_x))):
        for p in range(1, SLAB + 3):
            out_ref[(p - 1) * 16 : p * 16] = x_edge(me ^ bit, p, high).astype(jnp.bfloat16)
    for p in range(SLAB + 4):
        own_ref[p] = plane(me, p)


def material_kernel(eps_ref, gain_ref, region_ref, level_ref, out_ref, labels, codes, sems):
    planes = SLAB + 4
    start = lax.axis_index("quad") * SLAB
    first = jnp.clip(start - 2, 0, region_ref.shape[0] - planes)
    ahead = first - start + 4
    copies = [
        pltpu.make_async_copy(ref.at[pl.ds(first, planes)], labels.at[i], sems.at[i])
        for i, ref in enumerate((region_ref, level_ref))
    ]
    for copy in copies:
        copy.start()
    depth_y, depth_x = labels.shape[2:]
    lane = lax.broadcasted_iota(jnp.int32, (depth_x, LANES), 1)
    x_row = lax.broadcasted_iota(jnp.int32, (depth_x, LANES), 0) - lax.axis_index("sx") * CX
    picks = [
        jnp.where(x_row == lax.shift_right_logical(lane, 3) + dx, 1.0, 0.0) for dx in range(-2, 3)
    ]
    pick = jnp.concatenate(picks, axis=1).astype(jnp.bfloat16)
    y_lane = lax.broadcasted_iota(jnp.int32, (depth_y, LANES), 1) & 7
    y_row = lax.broadcasted_iota(jnp.int32, (depth_y, LANES), 0) - lax.axis_index("sy") * CY
    for copy in copies:
        copy.wait()
    code = labels[0] * 8 + labels[1] + 1
    code = code.astype(jnp.float32).astype(jnp.bfloat16).reshape(planes * depth_y, depth_x)
    spread = jnp.dot(code, pick, preferred_element_type=jnp.float32)
    codes[...] = jnp.zeros(codes.shape, jnp.float32)
    for off, (dx, dy) in enumerate(OFFSETS):
        block = spread[:, (dx + 2) * LANES : (dx + 3) * LANES].reshape(planes, depth_y, LANES)
        picked = jnp.sum(jnp.where((y_row == y_lane + dy)[None], block, 0.0), axis=1)
        codes[off, pl.ds(ahead, planes), :] = picked
    for t, (dz, off) in enumerate(TAPS):
        row = dz + 4
        code = codes[off, row : row + SLAB, :]
        code = jnp.concatenate([code, code], axis=0).astype(jnp.int32)
        inside = code > 0
        code = code - 1
        region = lax.shift_right_logical(code, 3)
        level = code & 7
        real = jnp.zeros((8, LANES), jnp.float32)
        imag = jnp.zeros((8, LANES), jnp.float32)
        for value in range(8):
            real = jnp.where(region == value, eps_ref[value], real)
            imag = jnp.where(level == value, gain_ref[value], imag)
        out_ref[t] = real
        out_ref[len(TAPS) + t] = imag
        out_ref[2 * len(TAPS) + t] = jnp.where(inside, 1.0, 0.0)


def cmul(a, b):
    return (a[0] * b[0] - a[1] * b[1], a[0] * b[1] + a[1] * b[0])


def cadd(a, b):
    return (a[0] + b[0], a[1] + b[1])


def moment_kernel(
    weight_ref,
    material_ref,
    own_ref,
    ylo_ref,
    yhi_ref,
    xlo_ref,
    xhi_ref,
    pick_ref,
    moments_ref,
    cross_ref,
    shifted,
    coef,
    folded,
):
    for plane in range(SLAB + 4):
        near, far = (plane - 1) * 16, 96 + (plane - 2) * 16
        sides = (ylo_ref, yhi_ref, xlo_ref, xhi_ref)
        if 2 <= plane < SLAB + 2:
            reach, starts = 13, (near, far)
        elif plane in (1, SLAB + 2):
            reach, starts = 5, (near, near)
        else:
            reach, starts = 1, ()
        rows = [own_ref[plane]] + [ref[i : i + 16] for ref in sides for i in starts]
        rows = jnp.concatenate(rows, axis=0) if starts else rows[0]
        picked = lax.dot_general(
            rows,
            pick_ref[: rows.shape[0], : reach * LANES],
            (((0,), (0,)), ((), ())),
            preferred_element_type=jnp.float32,
        )
        for off in range(reach):
            shifted[plane, off] = picked[:, off * LANES : (off + 1) * LANES]

    coef[...] = jnp.zeros(coef.shape, jnp.float32)
    first_half = lax.broadcasted_iota(jnp.int32, (8, LANES), 0) < SLAB

    def one_pair(pair, carry):
        weight = (
            jnp.where(first_half, weight_ref[0, 2 * pair], weight_ref[0, 2 * pair + 1]),
            jnp.where(
                first_half, weight_ref[0, QUAD + 2 * pair], weight_ref[0, QUAD + 2 * pair + 1]
            ),
        )
        node = (2.0 + weight[0], weight[1])
        inv = []
        for t in range(len(TAPS)):
            real, imag = material_ref[t], material_ref[len(TAPS) + t]
            diag_real = 6.0 + node[0] * real - node[1] * imag
            diag_imag = node[0] * imag + node[1] * real
            scale = material_ref[2 * len(TAPS) + t] / (diag_real * diag_real + diag_imag * diag_imag)
            inv.append((diag_real * scale, -(diag_imag * scale)))
        centre = inv[TAP_AT[(0, 0, 0)]]
        lead0 = cmul(weight, centre)
        lead1 = cmul(node, lead0)
        for t, (dz, off) in enumerate(TAPS):
            step = (dz,) + OFFSETS[off]
            size = sum(abs(d) for d in step)
            if size == 0:
                near = functools.reduce(cadd, [inv[TAP_AT[u]] for u in UNITS])
                term = cmul(centre, near)
                term = (1.0 + term[0], term[1])
            elif size == 1:
                term = inv[t]
            else:
                mids = [
                    inv[TAP_AT[u]]
                    for u in UNITS
                    if sum(abs(s - d) for s, d in zip(step, u)) == 1
                ]
                term = cmul(inv[t], functools.reduce(cadd, mids))
            for k, lead in enumerate((lead0, lead1)):
                real, imag = cmul(lead, term)
                coef[4 * t + 2 * k] += real
                coef[4 * t + 2 * k + 1] += imag
        return carry

    lax.fori_loop(0, QUAD // 2, one_pair, 0)
    for i in range(2 * len(TAPS)):
        real, imag = coef[2 * i], coef[2 * i + 1]
        real = real + pltpu.roll(real, SLAB, axis=0)
        imag = imag + pltpu.roll(imag, SLAB, axis=0)
        folded[3 * i] = real
        folded[3 * i + 1] = imag - real
        folded[3 * i + 2] = real + imag

    half = 64
    part = 32

    def one_chunk(step, carry):
        z = step // 2
        col = pl.multiple_of((step % 2) * part, part)
        sums = [jnp.zeros((part, LANES), jnp.float32) for _ in range(6)]
        for t, (dz, off) in enumerate(TAPS):
            real = shifted[z + 2 + dz, off, pl.ds(col, part), :]
            imag = shifted[z + 2 + dz, off, pl.ds(half + col, part), :]
            factors = (real + imag, real, imag)
            for i in range(6):
                sums[i] += folded[6 * t + i, pl.ds(z, 1), :] * factors[i % 3]
        for k in range(2):
            both, minus, plus = sums[3 * k : 3 * k + 3]
            moments_ref[k, z, pl.ds(col, part), :] = both - plus
            moments_ref[k, z, pl.ds(half + col, part), :] = both + minus
        return carry

    lax.fori_loop(0, 2 * SLAB, one_chunk, 0)

    cross = jnp.zeros((half, 4 * half), jnp.float32)
    for z in range(SLAB):
        left = jnp.concatenate([shifted[z + 2, 0, :half], shifted[z + 2, 0, half:]], axis=1)
        left = left.astype(jnp.bfloat16)
        rows = []
        for k in range(2):
            real = moments_ref[k, z, :half]
            imag = moments_ref[k, z, half:]
            rows.append(jnp.concatenate([real, imag], axis=1))
            rows.append(jnp.concatenate([imag, -real], axis=1))
        right = jnp.concatenate(rows, axis=0)
        high = right.astype(jnp.bfloat16)
        low = (right - high.astype(jnp.float32)).astype(jnp.bfloat16)
        for piece in (high, low):
            cross += lax.dot_general(
                left, piece, (((1,), (1,)), ((), ())), preferred_element_type=jnp.float32
            )
    cross_ref[...] = cross * (1.0 / 131072)


def turn_kernel(moments_ref, first_ref, second_ref):
    for k, out_ref in enumerate((first_ref, second_ref)):
        for z in range(SLAB):
            out_ref[z] = moments_ref[k, z].T


def turn(moments, columns):
    out = jax.ShapeDtypeStruct((SLAB, LANES, columns), jnp.float32)
    vmem = pl.BlockSpec(memory_space=pltpu.VMEM)
    return pl.pallas_call(
        turn_kernel,
        out_shape=[out] * 2,
        in_specs=[vmem],
        out_specs=[vmem] * 2,
        compiler_params=pltpu.CompilerParams(vmem_limit_bytes=8 * 1024 * 1024),
        cost_estimate=pl.CostEstimate(flops=1000000, bytes_accessed=1000000, transcendentals=0),
        name="turn",
    )(moments)


def swap(block, bits):
    axes = tuple(bits)
    sizes = [lax.axis_size(axis) for axis in axes]
    pairs = []
    for place in np.ndindex(*sizes):
        other = tuple(i ^ bit for i, bit in zip(place, bits.values()))
        pairs.append((int(np.ravel_multi_index(place, sizes)), int(np.ravel_multi_index(other, sizes))))
    return lax.ppermute(block, axes, pairs)


def sum_of_four(block, *steps):
    first, second, third = (swap(block, step) for step in steps)
    return (block + first) + (second + third)


def body(probes, quad_index, region_label, gain_label, region_eps, gain_rate):
    depth, cells_x, cells_y, columns = probes.shape
    planes = SLAB + 4
    core = lax.axis_index("sx") & 1
    even_x = core == 0
    even_y = (lax.axis_index("sy") & 1) == 0
    smem = pl.BlockSpec(memory_space=pltpu.SMEM)
    vmem = pl.BlockSpec(memory_space=pltpu.VMEM)
    hbm = pl.BlockSpec(memory_space=pltpu.HBM)
    mib = 1024 * 1024
    shapes = [
        (planes, cells_x * cells_y, columns),
        (PARTS + 16, columns),
        (PARTS + 16, columns),
        (FAR, columns),
        (FAR, columns),
    ]
    own, first, second, third, fourth = pl.pallas_call(
        slab_kernel,
        out_shape=[jax.ShapeDtypeStruct(shape, probes.dtype) for shape in shapes],
        in_specs=[smem, vmem],
        out_specs=[vmem] * 5,
        scratch_shapes=[pltpu.VMEM(((SLAB + 2) * LANES, columns), jnp.float32)] * 2,
        compiler_params=pltpu.CompilerParams(vmem_limit_bytes=8 * mib),
        cost_estimate=pl.CostEstimate(flops=10000000, bytes_accessed=600000, transcendentals=0),
        name="slab",
    )(quad_index, probes.reshape(depth, cells_x * cells_y, columns))

    def corner_rows(at):
        cells = [inner[at : at + SLAB], outer[at : at + SLAB]]
        low, high = jnp.where(even_y, cells[1], cells[0]), jnp.where(even_y, cells[0], cells[1])
        rows = jnp.pad(jnp.stack([low, high], axis=1), ((0, 0), (0, 14), (0, 0)))
        return rows.reshape(SLAB * 16, columns)

    parts = first[PARTS:]
    inner = swap(first, dict(quad=1, sy=1))
    outer = swap(second, dict(quad=3, sy=3))
    last = swap(parts, dict(quad=2))
    parts = (parts + inner[PARTS:]) + (outer[PARTS:] + last)
    ylo = jnp.where(even_y, outer, inner)[:CORNERS]
    yhi = jnp.where(even_y, inner, outer)[:CORNERS]
    third = jnp.concatenate([third, corner_rows(CORNERS), parts], axis=0)
    fourth = jnp.concatenate([fourth, corner_rows(CORNERS + SLAB), parts], axis=0)
    near = swap(third, dict(quad=4, sx=1))
    beyond = swap(fourth, dict(quad=8, sx=3))
    last = swap(parts, dict(quad=12))
    parts = (parts + near[CORNERS:]) + (beyond[CORNERS:] + last)
    xlo = jnp.where(even_x, beyond, near)[:CORNERS]
    xhi = jnp.where(even_x, near, beyond)[:CORNERS]
    weight = jnp.sum(parts[:3].astype(jnp.float32), axis=0, keepdims=True)

    taps = len(TAPS)
    material = pl.pallas_call(
        material_kernel,
        out_shape=jax.ShapeDtypeStruct((3 * taps, 8, LANES), jnp.float32),
        in_specs=[smem, smem, hbm, hbm],
        out_specs=vmem,
        scratch_shapes=[
            pltpu.VMEM((2, planes) + region_label.shape[:0:-1], jnp.int32),
            pltpu.VMEM((len(OFFSETS), 16, LANES), jnp.float32),
            pltpu.SemaphoreType.DMA((2,)),
        ],
        compiler_params=pltpu.CompilerParams(vmem_limit_bytes=8 * mib),
        cost_estimate=pl.CostEstimate(flops=40000000, bytes_accessed=1200000, transcendentals=0),
        name="material",
    )(region_eps, gain_rate, region_label.swapaxes(1, 2), gain_label.swapaxes(1, 2))

    moments, cross = pl.pallas_call(
        moment_kernel,
        out_shape=[
            jax.ShapeDtypeStruct((2, SLAB, columns, LANES), jnp.float32),
            jax.ShapeDtypeStruct((64, 256), jnp.float32),
        ],
        in_specs=[smem] + [vmem] * 7,
        out_specs=[vmem] * 2,
        scratch_shapes=[
            pltpu.VMEM((planes, len(OFFSETS), columns, LANES), jnp.float32),
            pltpu.VMEM((4 * taps, 8, LANES), jnp.float32),
            pltpu.VMEM((6 * taps, 8, LANES), jnp.float32),
        ],
        compiler_params=pltpu.CompilerParams(vmem_limit_bytes=24 * mib),
        cost_estimate=pl.CostEstimate(flops=600000000, bytes_accessed=3000000, transcendentals=0),
        name="moments",
    )(weight, material, own, ylo, yhi, xlo, xhi, jnp.asarray(selector()))

    width = cross.shape[1] // 2
    block = jnp.where(core == 0, cross[:, :width], cross[:, width:])
    block = block + swap(jnp.where(core == 0, cross[:, width:], cross[:, :width]), dict(sx=1))
    block = sum_of_four(block, dict(sy=1), dict(sy=3), dict(sy=2))
    block = sum_of_four(block, dict(quad=1), dict(quad=3), dict(quad=2))
    for step in (dict(quad=4), dict(quad=8)):
        block = block + swap(block, step)
    block, moments = lax.optimization_barrier((block, moments))
    block = block + swap(block, dict(quad=8, sx=2))
    first, second = turn(moments, columns)
    block, first, second = lax.optimization_barrier((block, first, second))
    other = swap(block, dict(sx=1))
    halves = (jnp.where(core == 0, block, other), jnp.where(core == 0, other, block))
    projections = jnp.stack(
        [jnp.stack([half[:, :64], half[:, 64:]], axis=0) for half in halves], axis=0
    )
    shape = (SLAB, cells_x, cells_y, columns)
    return (first.reshape(shape), second.reshape(shape), projections)


def solution(mesh):
    placed = (P(None, "sx", "sy", None), P("quad"), P(), P(), P(), P())
    return jax.shard_map(
        body,
        mesh=mesh,
        in_specs=placed,
        out_specs=(P("quad", "sx", "sy", None), P("quad", "sx", "sy", None), P()),
        check_vma=False,
    )
```

```python
import functools
import math

import jax
import jax.numpy as jnp
import numpy as np
from jax import lax
from jax.experimental import pallas as pl
from jax.experimental.pallas import tpu as pltpu
from jax.sharding import PartitionSpec as P

QUAD = 16
SLAB = 4
CX = 16
CY = 8
LANES = CX * CY

OFFSETS = sorted(
    [(dx, dy) for dx in range(-2, 3) for dy in range(-2, 3) if abs(dx) + abs(dy) <= 2],
    key=lambda o: (abs(o[0]) + abs(o[1]), o),
)
REACH = {0: 13, 1: 5, 2: 1}
TAPS = [(dz, off) for dz in range(-2, 3) for off in range(REACH[abs(dz)])]
TAP_AT = {(dz,) + OFFSETS[off]: i for i, (dz, off) in enumerate(TAPS)}
UNITS = [(1, 0, 0), (-1, 0, 0), (0, 1, 0), (0, -1, 0), (0, 0, 1), (0, 0, -1)]
WIDE = len(OFFSETS) * LANES
FAR = (SLAB + 2) * CX
CORNERS = FAR + SLAB * CX
PARTS = CORNERS + 16


def source_cells():
    cells = [(x, y) for x in range(CX) for y in range(CY)]
    for y in (-1, -2, CY, CY + 1):
        cells += [(x, y) for x in range(CX)]
    for xs, near in (((-2, -1), -1), ((CX, CX + 1), CX)):
        cells += [(x, y) for x in xs for y in range(CY)]
        cells += [(near, -1), (near, CY)] + [None] * 14
    return cells


def selector():
    row_of = {cell: row for row, cell in enumerate(source_cells()) if cell is not None}
    pick = np.zeros((256, WIDE), np.float32)
    for o, (dx, dy) in enumerate(OFFSETS):
        for x in range(CX):
            for y in range(CY):
                pick[row_of[(x + dx, y + dy)], o * LANES + x * CY + y] = 1.0
    return pick.astype(jnp.bfloat16)


def slab_kernel(
    quad_ref, probes_ref, own_ref, first_ref, second_ref, third_ref, fourth_ref, block, side, rim, sems, *whole
):
    depth = probes_ref.shape[0]
    me = lax.axis_index("quad")
    even_x = (lax.axis_index("sx") & 1) == 0
    even_y = (lax.axis_index("sy") & 1) == 0

    group = 4 * SLAB + 4
    bases = [jnp.clip((me & ~3) * SLAB - 2, 0, depth - group)]
    bases += [jnp.clip((me ^ bit) * SLAB - 2, 0, depth - SLAB - 4) for bit in (4, 8)]
    held = (block, side.at[0], side.at[1])
    copies = [
        pltpu.make_async_copy(probes_ref.at[pl.ds(base, to.shape[0])], to, sems.at[i])
        for i, (base, to) in enumerate(zip(bases, held))
    ]
    edges = ((4, even_x), (8, jnp.logical_not(even_x)))
    for i, step in enumerate((1, 3)):
        for j, (bit, high) in enumerate(edges):
            at = pl.multiple_of(jnp.where(high, LANES - 16, 0), 16)
            start = ((me ^ step) ^ bit) * SLAB
            edge = probes_ref.at[pl.ds(start, SLAB), pl.ds(at, 16)]
            copies.append(pltpu.make_async_copy(edge, rim.at[2 * i + j], sems.at[len(copies)]))
    for copy in copies:
        copy.start()

    def plane(slab, p, bit=0):
        z = jnp.clip(slab * SLAB + (p - 2), 0, depth - 1)
        at = {0: 0, 4: 1, 8: 2}[bit]
        return held[at][z - bases[at]]

    def x_edge(values, high):
        low, top = values[:16].astype(jnp.float32), values[LANES - 16 :].astype(jnp.float32)
        return jnp.where(high, top, low)

    index = jnp.full((1, LANES), quad_ref[0], jnp.int32).astype(jnp.float32)
    angle = 2.0 * math.pi * (index + 0.5) / (4 * QUAD)
    lane = lax.broadcasted_iota(jnp.int32, (1, LANES), 1)
    weight = jnp.where(lane == me, jnp.cos(angle), 0.0)
    weight = jnp.where(lane == me + QUAD, jnp.sin(angle), weight)
    row = lax.broadcasted_iota(jnp.int32, (16, LANES), 0)
    parts = jnp.zeros((16, LANES), jnp.float32)
    for i in range(3):
        part = weight.astype(jnp.bfloat16).astype(jnp.float32)
        parts = jnp.where(row == i, part, parts)
        weight = weight - part
    first_ref[PARTS : PARTS + 16] = parts.astype(jnp.bfloat16)
    second_ref[PARTS : PARTS + 16] = parts.astype(jnp.bfloat16)

    for copy in copies:
        copy.wait()
    sends = ((first_ref, whole[0], 1, even_y), (second_ref, whole[1], 3, jnp.logical_not(even_y)))
    for send, (out_ref, scratch, step, high) in enumerate(sends):
        target = me ^ step
        for p in range(1, SLAB + 3):
            scratch[(p - 1) * LANES : p * LANES] = plane(target, p).astype(jnp.float32)
        for at, start, count, deep in ((0, 0, SLAB + 2, 0), (FAR, LANES, SLAB, 1)):
            low = scratch[pl.ds(start + deep, count * CX, stride=CY), :]
            top = scratch[pl.ds(start + CY - 1 - deep, count * CX, stride=CY), :]
            out_ref[at : at + count * CX] = jnp.where(high, top, low).astype(jnp.bfloat16)
        corners = jnp.zeros((16, LANES), jnp.float32)
        for i, (bit, edge) in enumerate(edges):
            cell = jnp.where(edge, CY, 0) + jnp.where(high, CY - 1, 0)
            for p in range(SLAB):
                picked = jnp.where(row == cell, rim[2 * send + i, p].astype(jnp.float32), 0.0)
                picked = jnp.sum(picked, axis=0, keepdims=True)
                corners = jnp.where(row == i * SLAB + p, picked, corners)
        out_ref[CORNERS : CORNERS + 16] = corners.astype(jnp.bfloat16)

    for out_ref, (bit, high) in zip((third_ref, fourth_ref), edges):
        for p in range(1, SLAB + 3):
            out_ref[(p - 1) * 16 : p * 16] = x_edge(plane(me ^ bit, p, bit), high).astype(jnp.bfloat16)
    for p in range(SLAB + 4):
        own_ref[p] = plane(me, p)


def material_kernel(eps_ref, gain_ref, region_ref, level_ref, out_ref, labels, codes, sems):
    planes = SLAB + 4
    start = lax.axis_index("quad") * SLAB
    first = jnp.clip(start - 2, 0, region_ref.shape[0] - planes)
    ahead = first - start + 4
    copies = [
        pltpu.make_async_copy(ref.at[pl.ds(first, planes)], labels.at[i], sems.at[i])
        for i, ref in enumerate((region_ref, level_ref))
    ]
    for copy in copies:
        copy.start()
    depth_y, depth_x = labels.shape[2:]
    lane = lax.broadcasted_iota(jnp.int32, (depth_x, LANES), 1)
    x_row = lax.broadcasted_iota(jnp.int32, (depth_x, LANES), 0) - lax.axis_index("sx") * CX
    picks = [
        jnp.where(x_row == lax.shift_right_logical(lane, 3) + dx, 1.0, 0.0) for dx in range(-2, 3)
    ]
    pick = jnp.concatenate(picks, axis=1).astype(jnp.bfloat16)
    y_lane = lax.broadcasted_iota(jnp.int32, (depth_y, LANES), 1) & 7
    y_row = lax.broadcasted_iota(jnp.int32, (depth_y, LANES), 0) - lax.axis_index("sy") * CY
    for copy in copies:
        copy.wait()
    code = labels[0] * 8 + labels[1] + 1
    code = code.astype(jnp.float32).astype(jnp.bfloat16).reshape(planes * depth_y, depth_x)
    spread = jnp.dot(code, pick, preferred_element_type=jnp.float32)
    codes[...] = jnp.zeros(codes.shape, jnp.float32)
    for off, (dx, dy) in enumerate(OFFSETS):
        block = spread[:, (dx + 2) * LANES : (dx + 3) * LANES].reshape(planes, depth_y, LANES)
        picked = jnp.sum(jnp.where((y_row == y_lane + dy)[None], block, 0.0), axis=1)
        codes[off, pl.ds(ahead, planes), :] = picked
    for t, (dz, off) in enumerate(TAPS):
        row = dz + 4
        code = codes[off, row : row + SLAB, :]
        code = jnp.concatenate([code, code], axis=0).astype(jnp.int32)
        inside = code > 0
        code = code - 1
        region = lax.shift_right_logical(code, 3)
        level = code & 7
        real = jnp.zeros((8, LANES), jnp.float32)
        imag = jnp.zeros((8, LANES), jnp.float32)
        for value in range(8):
            real = jnp.where(region == value, eps_ref[value], real)
            imag = jnp.where(level == value, gain_ref[value], imag)
        out_ref[t] = real
        out_ref[len(TAPS) + t] = imag
        out_ref[2 * len(TAPS) + t] = jnp.where(inside, 1.0, 0.0)


def cmul(a, b):
    return (a[0] * b[0] - a[1] * b[1], a[0] * b[1] + a[1] * b[0])


def cadd(a, b):
    return (a[0] + b[0], a[1] + b[1])


def moment_kernel(
    weight_ref,
    material_ref,
    own_ref,
    ylo_ref,
    yhi_ref,
    xlo_ref,
    xhi_ref,
    pick_ref,
    moments_ref,
    cross_ref,
    shifted,
    coef,
    folded,
):
    for plane in range(SLAB + 4):
        near, far = (plane - 1) * 16, 96 + (plane - 2) * 16
        sides = (ylo_ref, yhi_ref, xlo_ref, xhi_ref)
        if 2 <= plane < SLAB + 2:
            reach, starts = 13, (near, far)
        elif plane in (1, SLAB + 2):
            reach, starts = 5, (near, near)
        else:
            reach, starts = 1, ()
        rows = [own_ref[plane]] + [ref[i : i + 16] for ref in sides for i in starts]
        rows = jnp.concatenate(rows, axis=0) if starts else rows[0]
        picked = lax.dot_general(
            rows,
            pick_ref[: rows.shape[0], : reach * LANES],
            (((0,), (0,)), ((), ())),
            preferred_element_type=jnp.float32,
        )
        for off in range(reach):
            shifted[plane, off] = picked[:, off * LANES : (off + 1) * LANES]

    coef[...] = jnp.zeros(coef.shape, jnp.float32)
    first_half = lax.broadcasted_iota(jnp.int32, (8, LANES), 0) < SLAB

    def one_pair(pair, carry):
        weight = (
            jnp.where(first_half, weight_ref[0, 2 * pair], weight_ref[0, 2 * pair + 1]),
            jnp.where(
                first_half, weight_ref[0, QUAD + 2 * pair], weight_ref[0, QUAD + 2 * pair + 1]
            ),
        )
        node = (2.0 + weight[0], weight[1])
        inv = []
        for t in range(len(TAPS)):
            real, imag = material_ref[t], material_ref[len(TAPS) + t]
            diag_real = 6.0 + node[0] * real - node[1] * imag
            diag_imag = node[0] * imag + node[1] * real
            scale = material_ref[2 * len(TAPS) + t] / (diag_real * diag_real + diag_imag * diag_imag)
            inv.append((diag_real * scale, -(diag_imag * scale)))
        centre = inv[TAP_AT[(0, 0, 0)]]
        lead0 = cmul(weight, centre)
        lead1 = cmul(node, lead0)
        for t, (dz, off) in enumerate(TAPS):
            step = (dz,) + OFFSETS[off]
            size = sum(abs(d) for d in step)
            if size == 0:
                near = functools.reduce(cadd, [inv[TAP_AT[u]] for u in UNITS])
                term = cmul(centre, near)
                term = (1.0 + term[0], term[1])
            elif size == 1:
                term = inv[t]
            else:
                mids = [
                    inv[TAP_AT[u]]
                    for u in UNITS
                    if sum(abs(s - d) for s, d in zip(step, u)) == 1
                ]
                term = cmul(inv[t], functools.reduce(cadd, mids))
            for k, lead in enumerate((lead0, lead1)):
                real, imag = cmul(lead, term)
                coef[4 * t + 2 * k] += real
                coef[4 * t + 2 * k + 1] += imag
        return carry

    lax.fori_loop(0, QUAD // 2, one_pair, 0)
    for i in range(2 * len(TAPS)):
        real, imag = coef[2 * i], coef[2 * i + 1]
        real = real + pltpu.roll(real, SLAB, axis=0)
        imag = imag + pltpu.roll(imag, SLAB, axis=0)
        folded[3 * i] = real
        folded[3 * i + 1] = imag - real
        folded[3 * i + 2] = real + imag

    half = 64
    part = 32

    def one_chunk(step, carry):
        z = step // 2
        col = pl.multiple_of((step % 2) * part, part)
        sums = [jnp.zeros((part, LANES), jnp.float32) for _ in range(6)]
        for t, (dz, off) in enumerate(TAPS):
            real = shifted[z + 2 + dz, off, pl.ds(col, part), :]
            imag = shifted[z + 2 + dz, off, pl.ds(half + col, part), :]
            factors = (real + imag, real, imag)
            for i in range(6):
                sums[i] += folded[6 * t + i, pl.ds(z, 1), :] * factors[i % 3]
        for k in range(2):
            both, minus, plus = sums[3 * k : 3 * k + 3]
            moments_ref[k, z, pl.ds(col, part), :] = both - plus
            moments_ref[k, z, pl.ds(half + col, part), :] = both + minus
        return carry

    lax.fori_loop(0, 2 * SLAB, one_chunk, 0)

    cross = jnp.zeros((half, 4 * half), jnp.float32)
    for z in range(SLAB):
        left = jnp.concatenate([shifted[z + 2, 0, :half], shifted[z + 2, 0, half:]], axis=1)
        left = left.astype(jnp.bfloat16)
        rows = []
        for k in range(2):
            real = moments_ref[k, z, :half]
            imag = moments_ref[k, z, half:]
            rows.append(jnp.concatenate([real, imag], axis=1))
            rows.append(jnp.concatenate([imag, -real], axis=1))
        right = jnp.concatenate(rows, axis=0)
        high = right.astype(jnp.bfloat16)
        low = (right - high.astype(jnp.float32)).astype(jnp.bfloat16)
        for piece in (high, low):
            cross += lax.dot_general(
                left, piece, (((1,), (1,)), ((), ())), preferred_element_type=jnp.float32
            )
    cross_ref[...] = cross * (1.0 / 131072)


def turn_kernel(moments_ref, first_ref, second_ref):
    for k, out_ref in enumerate((first_ref, second_ref)):
        for z in range(SLAB):
            out_ref[z] = moments_ref[k, z].T


def turn(moments, columns):
    out = jax.ShapeDtypeStruct((SLAB, LANES, columns), jnp.float32)
    vmem = pl.BlockSpec(memory_space=pltpu.VMEM)
    return pl.pallas_call(
        turn_kernel,
        out_shape=[out] * 2,
        in_specs=[vmem],
        out_specs=[vmem] * 2,
        compiler_params=pltpu.CompilerParams(vmem_limit_bytes=8 * 1024 * 1024),
        cost_estimate=pl.CostEstimate(flops=1000000, bytes_accessed=1000000, transcendentals=0),
        name="turn",
    )(moments)


def swap(block, bits):
    axes = tuple(bits)
    sizes = [lax.axis_size(axis) for axis in axes]
    pairs = []
    for place in np.ndindex(*sizes):
        other = tuple(i ^ bit for i, bit in zip(place, bits.values()))
        pairs.append((int(np.ravel_multi_index(place, sizes)), int(np.ravel_multi_index(other, sizes))))
    return lax.ppermute(block, axes, pairs)


def sum_of_four(block, *steps):
    first, second, third = (swap(block, step) for step in steps)
    return (block + first) + (second + third)


def body(probes, quad_index, region_label, gain_label, region_eps, gain_rate):
    depth, cells_x, cells_y, columns = probes.shape
    planes = SLAB + 4
    core = lax.axis_index("sx") & 1
    even_x = core == 0
    even_y = (lax.axis_index("sy") & 1) == 0
    smem = pl.BlockSpec(memory_space=pltpu.SMEM)
    vmem = pl.BlockSpec(memory_space=pltpu.VMEM)
    hbm = pl.BlockSpec(memory_space=pltpu.HBM)
    mib = 1024 * 1024
    shapes = [
        (planes, cells_x * cells_y, columns),
        (PARTS + 16, columns),
        (PARTS + 16, columns),
        (FAR, columns),
        (FAR, columns),
    ]
    own, first, second, third, fourth = pl.pallas_call(
        slab_kernel,
        out_shape=[jax.ShapeDtypeStruct(shape, probes.dtype) for shape in shapes],
        in_specs=[smem, hbm],
        out_specs=[vmem] * 5,
        scratch_shapes=[
            pltpu.VMEM((4 * SLAB + 4, cells_x * cells_y, columns), probes.dtype),
            pltpu.VMEM((2, planes, cells_x * cells_y, columns), probes.dtype),
            pltpu.VMEM((4, SLAB, 16, columns), probes.dtype),
            pltpu.SemaphoreType.DMA((7,)),
        ]
        + [pltpu.VMEM(((SLAB + 2) * LANES, columns), jnp.float32)] * 2,
        compiler_params=pltpu.CompilerParams(vmem_limit_bytes=52 * mib),
        cost_estimate=pl.CostEstimate(flops=10000000, bytes_accessed=600000, transcendentals=0),
        name="slab",
    )(quad_index, probes.reshape(depth, cells_x * cells_y, columns))

    def corner_rows(at):
        cells = [inner[at : at + SLAB], outer[at : at + SLAB]]
        low, high = jnp.where(even_y, cells[1], cells[0]), jnp.where(even_y, cells[0], cells[1])
        rows = jnp.pad(jnp.stack([low, high], axis=1), ((0, 0), (0, 14), (0, 0)))
        return rows.reshape(SLAB * 16, columns)

    parts = first[PARTS:]
    inner = swap(first, dict(quad=1, sy=1))
    outer = swap(second, dict(quad=3, sy=3))
    last = swap(parts, dict(quad=2))
    parts = (parts + inner[PARTS:]) + (outer[PARTS:] + last)
    ylo = jnp.where(even_y, outer, inner)[:CORNERS]
    yhi = jnp.where(even_y, inner, outer)[:CORNERS]
    third = jnp.concatenate([third, corner_rows(CORNERS), parts], axis=0)
    fourth = jnp.concatenate([fourth, corner_rows(CORNERS + SLAB), parts], axis=0)
    near = swap(third, dict(quad=4, sx=1))
    beyond = swap(fourth, dict(quad=8, sx=3))
    last = swap(parts, dict(quad=12))
    parts = (parts + near[CORNERS:]) + (beyond[CORNERS:] + last)
    xlo = jnp.where(even_x, beyond, near)[:CORNERS]
    xhi = jnp.where(even_x, near, beyond)[:CORNERS]
    weight = jnp.sum(parts[:3].astype(jnp.float32), axis=0, keepdims=True)

    taps = len(TAPS)
    material = pl.pallas_call(
        material_kernel,
        out_shape=jax.ShapeDtypeStruct((3 * taps, 8, LANES), jnp.float32),
        in_specs=[smem, smem, hbm, hbm],
        out_specs=vmem,
        scratch_shapes=[
            pltpu.VMEM((2, planes) + region_label.shape[:0:-1], jnp.int32),
            pltpu.VMEM((len(OFFSETS), 16, LANES), jnp.float32),
            pltpu.SemaphoreType.DMA((2,)),
        ],
        compiler_params=pltpu.CompilerParams(vmem_limit_bytes=8 * mib),
        cost_estimate=pl.CostEstimate(flops=40000000, bytes_accessed=1200000, transcendentals=0),
        name="material",
    )(region_eps, gain_rate, region_label.swapaxes(1, 2), gain_label.swapaxes(1, 2))

    moments, cross = pl.pallas_call(
        moment_kernel,
        out_shape=[
            jax.ShapeDtypeStruct((2, SLAB, columns, LANES), jnp.float32),
            jax.ShapeDtypeStruct((64, 256), jnp.float32),
        ],
        in_specs=[smem] + [vmem] * 7,
        out_specs=[vmem] * 2,
        scratch_shapes=[
            pltpu.VMEM((planes, len(OFFSETS), columns, LANES), jnp.float32),
            pltpu.VMEM((4 * taps, 8, LANES), jnp.float32),
            pltpu.VMEM((6 * taps, 8, LANES), jnp.float32),
        ],
        compiler_params=pltpu.CompilerParams(vmem_limit_bytes=24 * mib),
        cost_estimate=pl.CostEstimate(flops=600000000, bytes_accessed=3000000, transcendentals=0),
        name="moments",
    )(weight, material, own, ylo, yhi, xlo, xhi, jnp.asarray(selector()))

    width = cross.shape[1] // 2
    block = jnp.where(core == 0, cross[:, :width], cross[:, width:])
    block = block + swap(jnp.where(core == 0, cross[:, width:], cross[:, :width]), dict(sx=1))
    block = sum_of_four(block, dict(sy=1), dict(sy=3), dict(sy=2))
    block = sum_of_four(block, dict(quad=1), dict(quad=3), dict(quad=2))
    for step in (dict(quad=4), dict(quad=8)):
        block = block + swap(block, step)
    block, moments = lax.optimization_barrier((block, moments))
    block = block + swap(block, dict(quad=8, sx=2))
    first, second = turn(moments, columns)
    block, first, second = lax.optimization_barrier((block, first, second))
    other = swap(block, dict(sx=1))
    halves = (jnp.where(core == 0, block, other), jnp.where(core == 0, other, block))
    projections = jnp.stack(
        [jnp.stack([half[:, :64], half[:, 64:]], axis=0) for half in halves], axis=0
    )
    shape = (SLAB, cells_x, cells_y, columns)
    return (first.reshape(shape), second.reshape(shape), projections)


def solution(mesh):
    placed = (P(None, "sx", "sy", None), P("quad"), P(), P(), P(), P())
    return jax.shard_map(
        body,
        mesh=mesh,
        in_specs=placed,
        out_specs=(P("quad", "sx", "sy", None), P("quad", "sx", "sy", None), P()),
        check_vma=False,
    )
```

```python
import functools
import math

import jax
import jax.numpy as jnp
import numpy as np
from jax import lax
from jax.experimental import pallas as pl
from jax.experimental.pallas import tpu as pltpu
from jax.sharding import PartitionSpec as P

QUAD = 16
SLAB = 4
CX = 16
CY = 8
LANES = CX * CY

OFFSETS = sorted(
    [(dx, dy) for dx in range(-2, 3) for dy in range(-2, 3) if abs(dx) + abs(dy) <= 2],
    key=lambda o: (abs(o[0]) + abs(o[1]), o),
)
REACH = {0: 13, 1: 5, 2: 1}
TAPS = [(dz, off) for dz in range(-2, 3) for off in range(REACH[abs(dz)])]
TAP_AT = {(dz,) + OFFSETS[off]: i for i, (dz, off) in enumerate(TAPS)}
UNITS = [(1, 0, 0), (-1, 0, 0), (0, 1, 0), (0, -1, 0), (0, 0, 1), (0, 0, -1)]
WIDE = len(OFFSETS) * LANES
FAR = (SLAB + 2) * CX
CORNERS = FAR + SLAB * CX
PARTS = CORNERS + 16


def cell_code(x, y):
    return (x + 2) * 32 + y + 2


def write_selector(pick_ref):
    row = lax.broadcasted_iota(jnp.int32, (16, LANES), 0)
    lane = lax.broadcasted_iota(jnp.int32, (16, LANES), 1)
    own = cell_code(lax.shift_right_logical(lane, 3), lane & 7)

    def pair_of_x(x):
        return cell_code(x + lax.shift_right_logical(row, 3), row & 7)

    tiles = [pair_of_x(2 * i) for i in range(CX // 2)]
    tiles += [cell_code(row, y) for y in (-1, -2, CY, CY + 1)]
    for first, near in ((-2, -1), (CX, CX)):
        corners = jnp.where(row == 1, cell_code(near, CY), -1)
        tiles += [pair_of_x(first), jnp.where(row == 0, cell_code(near, -1), corners)]
    for i, tile in enumerate(tiles):
        for off, (dx, dy) in enumerate(OFFSETS):
            hit = jnp.where(tile == own + (dx * 32 + dy), 1.0, 0.0).astype(jnp.bfloat16)
            pick_ref[i * 16 : i * 16 + 16, off * LANES : (off + 1) * LANES] = hit


def slab_kernel(
    quad_ref, probes_ref, own_ref, first_ref, second_ref, third_ref, fourth_ref, block, side, rim, sems, *whole
):
    depth = probes_ref.shape[0]
    me = lax.axis_index("quad")
    even_x = (lax.axis_index("sx") & 1) == 0
    even_y = (lax.axis_index("sy") & 1) == 0

    group = 4 * SLAB + 4
    bases = [jnp.clip((me & ~3) * SLAB - 2, 0, depth - group)]
    bases += [jnp.clip((me ^ bit) * SLAB - 2, 0, depth - SLAB - 4) for bit in (4, 8)]
    held = (block, side.at[0], side.at[1])
    copies = [
        pltpu.make_async_copy(probes_ref.at[pl.ds(base, to.shape[0])], to, sems.at[i])
        for i, (base, to) in enumerate(zip(bases, held))
    ]
    edges = ((4, even_x), (8, jnp.logical_not(even_x)))
    for i, step in enumerate((1, 3)):
        for j, (bit, high) in enumerate(edges):
            at = pl.multiple_of(jnp.where(high, LANES - 16, 0), 16)
            start = ((me ^ step) ^ bit) * SLAB
            edge = probes_ref.at[pl.ds(start, SLAB), pl.ds(at, 16)]
            copies.append(pltpu.make_async_copy(edge, rim.at[2 * i + j], sems.at[len(copies)]))
    for copy in copies:
        copy.start()

    def plane(slab, p, bit=0):
        z = jnp.clip(slab * SLAB + (p - 2), 0, depth - 1)
        at = {0: 0, 4: 1, 8: 2}[bit]
        return held[at][z - bases[at]]

    def x_edge(values, high):
        low, top = values[:16].astype(jnp.float32), values[LANES - 16 :].astype(jnp.float32)
        return jnp.where(high, top, low)

    index = jnp.full((1, LANES), quad_ref[0], jnp.int32).astype(jnp.float32)
    angle = 2.0 * math.pi * (index + 0.5) / (4 * QUAD)
    lane = lax.broadcasted_iota(jnp.int32, (1, LANES), 1)
    weight = jnp.where(lane == me, jnp.cos(angle), 0.0)
    weight = jnp.where(lane == me + QUAD, jnp.sin(angle), weight)
    row = lax.broadcasted_iota(jnp.int32, (16, LANES), 0)
    parts = jnp.zeros((16, LANES), jnp.float32)
    for i in range(3):
        part = weight.astype(jnp.bfloat16).astype(jnp.float32)
        parts = jnp.where(row == i, part, parts)
        weight = weight - part
    first_ref[PARTS : PARTS + 16] = parts.astype(jnp.bfloat16)
    second_ref[PARTS : PARTS + 16] = parts.astype(jnp.bfloat16)

    for copy in copies:
        copy.wait()
    sends = ((first_ref, whole[0], 1, even_y), (second_ref, whole[1], 3, jnp.logical_not(even_y)))
    for send, (out_ref, scratch, step, high) in enumerate(sends):
        target = me ^ step
        for p in range(1, SLAB + 3):
            scratch[(p - 1) * LANES : p * LANES] = plane(target, p).astype(jnp.float32)
        for at, start, count, deep in ((0, 0, SLAB + 2, 0), (FAR, LANES, SLAB, 1)):
            low = scratch[pl.ds(start + deep, count * CX, stride=CY), :]
            top = scratch[pl.ds(start + CY - 1 - deep, count * CX, stride=CY), :]
            out_ref[at : at + count * CX] = jnp.where(high, top, low).astype(jnp.bfloat16)
        corners = jnp.zeros((16, LANES), jnp.float32)
        for i, (bit, edge) in enumerate(edges):
            cell = jnp.where(edge, CY, 0) + jnp.where(high, CY - 1, 0)
            for p in range(SLAB):
                picked = jnp.where(row == cell, rim[2 * send + i, p].astype(jnp.float32), 0.0)
                picked = jnp.sum(picked, axis=0, keepdims=True)
                corners = jnp.where(row == i * SLAB + p, picked, corners)
        out_ref[CORNERS : CORNERS + 16] = corners.astype(jnp.bfloat16)

    for out_ref, (bit, high) in zip((third_ref, fourth_ref), edges):
        for p in range(1, SLAB + 3):
            out_ref[(p - 1) * 16 : p * 16] = x_edge(plane(me ^ bit, p, bit), high).astype(jnp.bfloat16)
    for p in range(SLAB + 4):
        own_ref[p] = plane(me, p)


def material_kernel(eps_ref, gain_ref, region_ref, level_ref, out_ref, pick_ref, labels, codes, sems):
    planes = SLAB + 4
    start = lax.axis_index("quad") * SLAB
    first = jnp.clip(start - 2, 0, region_ref.shape[0] - planes)
    ahead = first - start + 4
    copies = [
        pltpu.make_async_copy(ref.at[pl.ds(first, planes)], labels.at[i], sems.at[i])
        for i, ref in enumerate((region_ref, level_ref))
    ]
    for copy in copies:
        copy.start()
    write_selector(pick_ref)
    depth_y, depth_x = labels.shape[2:]
    lane = lax.broadcasted_iota(jnp.int32, (depth_x, LANES), 1)
    x_row = lax.broadcasted_iota(jnp.int32, (depth_x, LANES), 0) - lax.axis_index("sx") * CX
    picks = [
        jnp.where(x_row == lax.shift_right_logical(lane, 3) + dx, 1.0, 0.0) for dx in range(-2, 3)
    ]
    pick = jnp.concatenate(picks, axis=1).astype(jnp.bfloat16)
    y_lane = lax.broadcasted_iota(jnp.int32, (depth_y, LANES), 1) & 7
    y_row = lax.broadcasted_iota(jnp.int32, (depth_y, LANES), 0) - lax.axis_index("sy") * CY
    for copy in copies:
        copy.wait()
    code = labels[0] * 8 + labels[1] + 1
    code = code.astype(jnp.float32).astype(jnp.bfloat16).reshape(planes * depth_y, depth_x)
    spread = jnp.dot(code, pick, preferred_element_type=jnp.float32)
    codes[...] = jnp.zeros(codes.shape, jnp.float32)
    for off, (dx, dy) in enumerate(OFFSETS):
        block = spread[:, (dx + 2) * LANES : (dx + 3) * LANES].reshape(planes, depth_y, LANES)
        picked = jnp.sum(jnp.where((y_row == y_lane + dy)[None], block, 0.0), axis=1)
        codes[off, pl.ds(ahead, planes), :] = picked
    for t, (dz, off) in enumerate(TAPS):
        row = dz + 4
        code = codes[off, row : row + SLAB, :]
        code = jnp.concatenate([code, code], axis=0).astype(jnp.int32)
        inside = code > 0
        code = code - 1
        region = lax.shift_right_logical(code, 3)
        level = code & 7
        real = jnp.zeros((8, LANES), jnp.float32)
        imag = jnp.zeros((8, LANES), jnp.float32)
        for value in range(8):
            real = jnp.where(region == value, eps_ref[value], real)
            imag = jnp.where(level == value, gain_ref[value], imag)
        out_ref[t] = real
        out_ref[len(TAPS) + t] = imag
        out_ref[2 * len(TAPS) + t] = jnp.where(inside, 1.0, 0.0)


def cmul(a, b):
    return (a[0] * b[0] - a[1] * b[1], a[0] * b[1] + a[1] * b[0])


def cadd(a, b):
    return (a[0] + b[0], a[1] + b[1])


def apply_stencil(moment, folded, shifted, moment_ref, cross_ref):
    half = 64
    part = 32

    def one_chunk(step, carry):
        z = step // 2
        col = pl.multiple_of((step % 2) * part, part)
        sums = [jnp.zeros((part, LANES), jnp.float32) for _ in range(3)]
        for t, (dz, off) in enumerate(TAPS):
            real = shifted[z + 2 + dz, off, pl.ds(col, part), :]
            imag = shifted[z + 2 + dz, off, pl.ds(half + col, part), :]
            factors = (real + imag, real, imag)
            for i in range(3):
                sums[i] += folded[6 * t + 3 * moment + i, pl.ds(z, 1), :] * factors[i]
        both, minus, plus = sums
        moment_ref[z, pl.ds(col, part), :] = both - plus
        moment_ref[z, pl.ds(half + col, part), :] = both + minus
        return carry

    lax.fori_loop(0, 2 * SLAB, one_chunk, 0)

    cross = jnp.zeros((half, 2 * half), jnp.float32)
    for z in range(SLAB):
        left = jnp.concatenate([shifted[z + 2, 0, :half], shifted[z + 2, 0, half:]], axis=1)
        left = left.astype(jnp.bfloat16)
        real = moment_ref[z, :half]
        imag = moment_ref[z, half:]
        rows = [jnp.concatenate([real, imag], axis=1), jnp.concatenate([imag, -real], axis=1)]
        right = jnp.concatenate(rows, axis=0)
        high = right.astype(jnp.bfloat16)
        low = (right - high.astype(jnp.float32)).astype(jnp.bfloat16)
        for piece in (high, low):
            cross += lax.dot_general(
                left, piece, (((1,), (1,)), ((), ())), preferred_element_type=jnp.float32
            )
    cross_ref[...] = cross * (1.0 / 131072)


def moment_kernel(
    weight_ref,
    material_ref,
    own_ref,
    ylo_ref,
    yhi_ref,
    xlo_ref,
    xhi_ref,
    pick_ref,
    moment_ref,
    cross_ref,
    shifted,
    folded,
    coef,
):
    for plane in range(SLAB + 4):
        near, far = (plane - 1) * 16, 96 + (plane - 2) * 16
        sides = (ylo_ref, yhi_ref, xlo_ref, xhi_ref)
        if 2 <= plane < SLAB + 2:
            reach, starts = 13, (near, far)
        elif plane in (1, SLAB + 2):
            reach, starts = 5, (near, near)
        else:
            reach, starts = 1, ()
        rows = [own_ref[plane]] + [ref[i : i + 16] for ref in sides for i in starts]
        rows = jnp.concatenate(rows, axis=0) if starts else rows[0]
        picked = lax.dot_general(
            rows,
            pick_ref[: rows.shape[0], : reach * LANES],
            (((0,), (0,)), ((), ())),
            preferred_element_type=jnp.float32,
        )
        for off in range(reach):
            shifted[plane, off] = picked[:, off * LANES : (off + 1) * LANES]

    coef[...] = jnp.zeros(coef.shape, jnp.float32)
    first_half = lax.broadcasted_iota(jnp.int32, (8, LANES), 0) < SLAB

    def one_pair(pair, carry):
        weight = (
            jnp.where(first_half, weight_ref[0, 2 * pair], weight_ref[0, 2 * pair + 1]),
            jnp.where(
                first_half, weight_ref[0, QUAD + 2 * pair], weight_ref[0, QUAD + 2 * pair + 1]
            ),
        )
        node = (2.0 + weight[0], weight[1])
        inv = []
        for t in range(len(TAPS)):
            real, imag = material_ref[t], material_ref[len(TAPS) + t]
            diag_real = 6.0 + node[0] * real - node[1] * imag
            diag_imag = node[0] * imag + node[1] * real
            scale = material_ref[2 * len(TAPS) + t] / (diag_real * diag_real + diag_imag * diag_imag)
            inv.append((diag_real * scale, -(diag_imag * scale)))
        centre = inv[TAP_AT[(0, 0, 0)]]
        lead0 = cmul(weight, centre)
        lead1 = cmul(node, lead0)
        for t, (dz, off) in enumerate(TAPS):
            step = (dz,) + OFFSETS[off]
            size = sum(abs(d) for d in step)
            if size == 0:
                near = functools.reduce(cadd, [inv[TAP_AT[u]] for u in UNITS])
                term = cmul(centre, near)
                term = (1.0 + term[0], term[1])
            elif size == 1:
                term = inv[t]
            else:
                mids = [
                    inv[TAP_AT[u]]
                    for u in UNITS
                    if sum(abs(s - d) for s, d in zip(step, u)) == 1
                ]
                term = cmul(inv[t], functools.reduce(cadd, mids))
            for k, lead in enumerate((lead0, lead1)):
                real, imag = cmul(lead, term)
                coef[4 * t + 2 * k] += real
                coef[4 * t + 2 * k + 1] += imag
        return carry

    lax.fori_loop(0, QUAD // 2, one_pair, 0)
    for i in range(2 * len(TAPS)):
        real, imag = coef[2 * i], coef[2 * i + 1]
        real = real + pltpu.roll(real, SLAB, axis=0)
        imag = imag + pltpu.roll(imag, SLAB, axis=0)
        folded[3 * i] = real
        folded[3 * i + 1] = imag - real
        folded[3 * i + 2] = real + imag

    apply_stencil(1 - (lax.axis_index("sx") & 1), folded, shifted, moment_ref, cross_ref)


def second_kernel(shifted, folded, moment_ref, cross_ref):
    apply_stencil(lax.axis_index("sx") & 1, folded, shifted, moment_ref, cross_ref)


def turn_kernel(other_ref, mine_ref, first_ref, second_ref):
    even = (lax.axis_index("sx") & 1) == 0
    for z in range(SLAB):
        other, mine = other_ref[z].T, mine_ref[z].T
        first_ref[z] = jnp.where(even, mine, other)
        second_ref[z] = jnp.where(even, other, mine)


def turn(other, mine, columns):
    out = jax.ShapeDtypeStruct((SLAB, LANES, columns), jnp.float32)
    vmem = pl.BlockSpec(memory_space=pltpu.VMEM)
    return pl.pallas_call(
        turn_kernel,
        out_shape=[out] * 2,
        in_specs=[vmem] * 2,
        out_specs=[vmem] * 2,
        compiler_params=pltpu.CompilerParams(vmem_limit_bytes=8 * 1024 * 1024),
        cost_estimate=pl.CostEstimate(flops=1000000, bytes_accessed=1000000, transcendentals=0),
        name="turn",
    )(other, mine)


def swap(block, bits):
    axes = tuple(bits)
    sizes = [lax.axis_size(axis) for axis in axes]
    pairs = []
    for place in np.ndindex(*sizes):
        other = tuple(i ^ bit for i, bit in zip(place, bits.values()))
        pairs.append((int(np.ravel_multi_index(place, sizes)), int(np.ravel_multi_index(other, sizes))))
    return lax.ppermute(block, axes, pairs)


def sum_of_four(block, *steps):
    first, second, third = (swap(block, step) for step in steps)
    return (block + first) + (second + third)


def body(probes, quad_index, region_label, gain_label, region_eps, gain_rate):
    depth, cells_x, cells_y, columns = probes.shape
    planes = SLAB + 4
    core = lax.axis_index("sx") & 1
    even_x = core == 0
    even_y = (lax.axis_index("sy") & 1) == 0
    smem = pl.BlockSpec(memory_space=pltpu.SMEM)
    vmem = pl.BlockSpec(memory_space=pltpu.VMEM)
    hbm = pl.BlockSpec(memory_space=pltpu.HBM)
    mib = 1024 * 1024
    shapes = [
        (planes, cells_x * cells_y, columns),
        (PARTS + 16, columns),
        (PARTS + 16, columns),
        (FAR, columns),
        (FAR, columns),
    ]
    own, first, second, third, fourth = pl.pallas_call(
        slab_kernel,
        out_shape=[jax.ShapeDtypeStruct(shape, probes.dtype) for shape in shapes],
        in_specs=[smem, hbm],
        out_specs=[vmem] * 5,
        scratch_shapes=[
            pltpu.VMEM((4 * SLAB + 4, cells_x * cells_y, columns), probes.dtype),
            pltpu.VMEM((2, planes, cells_x * cells_y, columns), probes.dtype),
            pltpu.VMEM((4, SLAB, 16, columns), probes.dtype),
            pltpu.SemaphoreType.DMA((7,)),
        ]
        + [pltpu.VMEM(((SLAB + 2) * LANES, columns), jnp.float32)] * 2,
        compiler_params=pltpu.CompilerParams(vmem_limit_bytes=52 * mib),
        cost_estimate=pl.CostEstimate(flops=10000000, bytes_accessed=600000, transcendentals=0),
        name="slab",
    )(quad_index, probes.reshape(depth, cells_x * cells_y, columns))

    def corner_rows(at):
        cells = [inner[at : at + SLAB], outer[at : at + SLAB]]
        low, high = jnp.where(even_y, cells[1], cells[0]), jnp.where(even_y, cells[0], cells[1])
        rows = jnp.pad(jnp.stack([low, high], axis=1), ((0, 0), (0, 14), (0, 0)))
        return rows.reshape(SLAB * 16, columns)

    parts = first[PARTS:]
    inner = swap(first, dict(quad=1, sy=1))
    outer = swap(second, dict(quad=3, sy=3))
    last = swap(parts, dict(quad=2))
    parts = (parts + inner[PARTS:]) + (outer[PARTS:] + last)
    ylo = jnp.where(even_y, outer, inner)[:CORNERS]
    yhi = jnp.where(even_y, inner, outer)[:CORNERS]
    third = jnp.concatenate([third, corner_rows(CORNERS), parts], axis=0)
    fourth = jnp.concatenate([fourth, corner_rows(CORNERS + SLAB), parts], axis=0)
    near = swap(third, dict(quad=4, sx=1))
    beyond = swap(fourth, dict(quad=8, sx=3))
    last = swap(parts, dict(quad=12))
    parts = (parts + near[CORNERS:]) + (beyond[CORNERS:] + last)
    xlo = jnp.where(even_x, beyond, near)[:CORNERS]
    xhi = jnp.where(even_x, near, beyond)[:CORNERS]
    weight = jnp.sum(parts[:3].astype(jnp.float32), axis=0, keepdims=True)

    taps = len(TAPS)
    material, pick = pl.pallas_call(
        material_kernel,
        out_shape=[
            jax.ShapeDtypeStruct((3 * taps, 8, LANES), jnp.float32),
            jax.ShapeDtypeStruct((256, WIDE), jnp.bfloat16),
        ],
        in_specs=[smem, smem, hbm, hbm],
        out_specs=[vmem] * 2,
        scratch_shapes=[
            pltpu.VMEM((2, planes) + region_label.shape[:0:-1], jnp.int32),
            pltpu.VMEM((len(OFFSETS), 16, LANES), jnp.float32),
            pltpu.SemaphoreType.DMA((2,)),
        ],
        compiler_params=pltpu.CompilerParams(vmem_limit_bytes=52 * mib),
        cost_estimate=pl.CostEstimate(flops=40000000, bytes_accessed=1200000, transcendentals=0),
        name="material",
    )(region_eps, gain_rate, region_label.swapaxes(1, 2), gain_label.swapaxes(1, 2))

    result = [
        jax.ShapeDtypeStruct((SLAB, columns, LANES), jnp.float32),
        jax.ShapeDtypeStruct((64, LANES), jnp.float32),
    ]
    kept = [
        jax.ShapeDtypeStruct((planes, len(OFFSETS), columns, LANES), jnp.float32),
        jax.ShapeDtypeStruct((6 * taps, 8, LANES), jnp.float32),
    ]
    moment_other, cross_other, shifted, folded = pl.pallas_call(
        moment_kernel,
        out_shape=result + kept,
        in_specs=[smem] + [vmem] * 7,
        out_specs=[vmem] * 4,
        scratch_shapes=[pltpu.VMEM((4 * taps, 8, LANES), jnp.float32)],
        compiler_params=pltpu.CompilerParams(vmem_limit_bytes=16 * mib),
        cost_estimate=pl.CostEstimate(flops=600000000, bytes_accessed=3000000, transcendentals=0),
        name="moments",
    )(weight, material, own, ylo, yhi, xlo, xhi, pick)
    received = swap(cross_other, dict(sx=1))
    moment_mine, cross_mine = pl.pallas_call(
        second_kernel,
        out_shape=result,
        in_specs=[vmem] * 2,
        out_specs=[vmem] * 2,
        compiler_params=pltpu.CompilerParams(vmem_limit_bytes=16 * mib),
        cost_estimate=pl.CostEstimate(flops=100000000, bytes_accessed=1000000, transcendentals=0),
        name="second",
    )(shifted, folded)

    block = cross_mine + received
    block = sum_of_four(block, dict(sy=1), dict(sy=3), dict(sy=2))
    block = sum_of_four(block, dict(quad=1), dict(quad=3), dict(quad=2))
    for step in (dict(quad=4), dict(quad=8)):
        block = block + swap(block, step)
    block, moment_other = lax.optimization_barrier((block, moment_other))
    block = block + swap(block, dict(quad=8, sx=2))
    first, second = turn(moment_other, moment_mine, columns)
    block, first, second = lax.optimization_barrier((block, first, second))
    other = swap(block, dict(sx=1))
    halves = (jnp.where(core == 0, block, other), jnp.where(core == 0, other, block))
    projections = jnp.stack(
        [jnp.stack([half[:, :64], half[:, 64:]], axis=0) for half in halves], axis=0
    )
    shape = (SLAB, cells_x, cells_y, columns)
    return (first.reshape(shape), second.reshape(shape), projections)


def solution(mesh):
    placed = (P(None, "sx", "sy", None), P("quad"), P(), P(), P(), P())
    return jax.shard_map(
        body,
        mesh=mesh,
        in_specs=placed,
        out_specs=(P("quad", "sx", "sy", None), P("quad", "sx", "sy", None), P()),
        check_vma=False,
    )
```

```python
import functools
import math

import jax
import jax.numpy as jnp
import numpy as np
from jax import lax
from jax.experimental import pallas as pl
from jax.experimental.pallas import tpu as pltpu
from jax.sharding import PartitionSpec as P

QUAD = 16
SLAB = 4
CX = 16
CY = 8
LANES = CX * CY

OFFSETS = sorted(
    [(dx, dy) for dx in range(-2, 3) for dy in range(-2, 3) if abs(dx) + abs(dy) <= 2],
    key=lambda o: (abs(o[0]) + abs(o[1]), o),
)
REACH = {0: 13, 1: 5, 2: 1}
TAPS = [(dz, off) for dz in range(-2, 3) for off in range(REACH[abs(dz)])]
TAP_AT = {(dz,) + OFFSETS[off]: i for i, (dz, off) in enumerate(TAPS)}
UNITS = [(1, 0, 0), (-1, 0, 0), (0, 1, 0), (0, -1, 0), (0, 0, 1), (0, 0, -1)]
WIDE = len(OFFSETS) * LANES
FAR = (SLAB + 2) * CX
CORNERS = FAR + SLAB * CX
PARTS = CORNERS + 16


def cell_code(x, y):
    return (x + 2) * 32 + y + 2


def write_selector(pick_ref):
    row = lax.broadcasted_iota(jnp.int32, (16, LANES), 0)
    lane = lax.broadcasted_iota(jnp.int32, (16, LANES), 1)
    own = cell_code(lax.shift_right_logical(lane, 3), lane & 7)

    def pair_of_x(x):
        return cell_code(x + lax.shift_right_logical(row, 3), row & 7)

    tiles = [pair_of_x(2 * i) for i in range(CX // 2)]
    tiles += [cell_code(row, y) for y in (-1, -2, CY, CY + 1)]
    for first, near in ((-2, -1), (CX, CX)):
        corners = jnp.where(row == 1, cell_code(near, CY), -1)
        tiles += [pair_of_x(first), jnp.where(row == 0, cell_code(near, -1), corners)]
    for i, tile in enumerate(tiles):
        for off, (dx, dy) in enumerate(OFFSETS):
            hit = jnp.where(tile == own + (dx * 32 + dy), 1.0, 0.0).astype(jnp.bfloat16)
            pick_ref[i * 16 : i * 16 + 16, off * LANES : (off + 1) * LANES] = hit


def slab_kernel(
    quad_ref, probes_ref, own_ref, first_ref, second_ref, third_ref, fourth_ref, block, side, rim, sems, *whole
):
    depth = probes_ref.shape[0]
    me = lax.axis_index("quad")
    even_x = (lax.axis_index("sx") & 1) == 0
    even_y = (lax.axis_index("sy") & 1) == 0

    group = 4 * SLAB + 4
    bases = [jnp.clip((me & ~3) * SLAB - 2, 0, depth - group)]
    bases += [jnp.clip((me ^ bit) * SLAB - 2, 0, depth - SLAB - 4) for bit in (4, 8)]
    held = (block, side.at[0], side.at[1])
    copies = [
        pltpu.make_async_copy(probes_ref.at[pl.ds(base, to.shape[0])], to, sems.at[i])
        for i, (base, to) in enumerate(zip(bases, held))
    ]
    edges = ((4, even_x), (8, jnp.logical_not(even_x)))
    for i, step in enumerate((1, 3)):
        for j, (bit, high) in enumerate(edges):
            at = pl.multiple_of(jnp.where(high, LANES - 16, 0), 16)
            start = ((me ^ step) ^ bit) * SLAB
            edge = probes_ref.at[pl.ds(start, SLAB), pl.ds(at, 16)]
            copies.append(pltpu.make_async_copy(edge, rim.at[2 * i + j], sems.at[len(copies)]))
    for copy in copies:
        copy.start()

    def plane(slab, p, bit=0):
        z = jnp.clip(slab * SLAB + (p - 2), 0, depth - 1)
        at = {0: 0, 4: 1, 8: 2}[bit]
        return held[at][z - bases[at]]

    def x_edge(values, high):
        low, top = values[:16].astype(jnp.float32), values[LANES - 16 :].astype(jnp.float32)
        return jnp.where(high, top, low)

    index = jnp.full((1, LANES), quad_ref[0], jnp.int32).astype(jnp.float32)
    angle = 2.0 * math.pi * (index + 0.5) / (4 * QUAD)
    lane = lax.broadcasted_iota(jnp.int32, (1, LANES), 1)
    weight = jnp.where(lane == me, jnp.cos(angle), 0.0)
    weight = jnp.where(lane == me + QUAD, jnp.sin(angle), weight)
    row = lax.broadcasted_iota(jnp.int32, (16, LANES), 0)
    parts = jnp.zeros((16, LANES), jnp.float32)
    for i in range(3):
        part = weight.astype(jnp.bfloat16).astype(jnp.float32)
        parts = jnp.where(row == i, part, parts)
        weight = weight - part
    first_ref[PARTS : PARTS + 16] = parts.astype(jnp.bfloat16)
    second_ref[PARTS : PARTS + 16] = parts.astype(jnp.bfloat16)

    for copy in copies:
        copy.wait()
    sends = ((first_ref, whole[0], 1, even_y), (second_ref, whole[1], 3, jnp.logical_not(even_y)))
    for send, (out_ref, scratch, step, high) in enumerate(sends):
        target = me ^ step
        for p in range(1, SLAB + 3):
            scratch[(p - 1) * LANES : p * LANES] = plane(target, p).astype(jnp.float32)
        for at, start, count, deep in ((0, 0, SLAB + 2, 0), (FAR, LANES, SLAB, 1)):
            low = scratch[pl.ds(start + deep, count * CX, stride=CY), :]
            top = scratch[pl.ds(start + CY - 1 - deep, count * CX, stride=CY), :]
            out_ref[at : at + count * CX] = jnp.where(high, top, low).astype(jnp.bfloat16)
        corners = jnp.zeros((16, LANES), jnp.float32)
        for i, (bit, edge) in enumerate(edges):
            cell = jnp.where(edge, CY, 0) + jnp.where(high, CY - 1, 0)
            for p in range(SLAB):
                picked = jnp.where(row == cell, rim[2 * send + i, p].astype(jnp.float32), 0.0)
                picked = jnp.sum(picked, axis=0, keepdims=True)
                corners = jnp.where(row == i * SLAB + p, picked, corners)
        out_ref[CORNERS : CORNERS + 16] = corners.astype(jnp.bfloat16)

    for out_ref, (bit, high) in zip((third_ref, fourth_ref), edges):
        for p in range(1, SLAB + 3):
            out_ref[(p - 1) * 16 : p * 16] = x_edge(plane(me ^ bit, p, bit), high).astype(jnp.bfloat16)
    for p in range(SLAB + 4):
        own_ref[p] = plane(me, p)


def material_kernel(eps_ref, gain_ref, region_ref, level_ref, out_ref, pick_ref, labels, codes, sems):
    planes = SLAB + 4
    start = lax.axis_index("quad") * SLAB
    first = jnp.clip(start - 2, 0, region_ref.shape[0] - planes)
    ahead = first - start + 4
    copies = [
        pltpu.make_async_copy(ref.at[pl.ds(first, planes)], labels.at[i], sems.at[i])
        for i, ref in enumerate((region_ref, level_ref))
    ]
    for copy in copies:
        copy.start()
    write_selector(pick_ref)
    depth_y, depth_x = labels.shape[2:]
    lane = lax.broadcasted_iota(jnp.int32, (depth_x, LANES), 1)
    x_row = lax.broadcasted_iota(jnp.int32, (depth_x, LANES), 0) - lax.axis_index("sx") * CX
    picks = [
        jnp.where(x_row == lax.shift_right_logical(lane, 3) + dx, 1.0, 0.0) for dx in range(-2, 3)
    ]
    pick = jnp.concatenate(picks, axis=1).astype(jnp.bfloat16)
    y_lane = lax.broadcasted_iota(jnp.int32, (depth_y, LANES), 1) & 7
    y_row = lax.broadcasted_iota(jnp.int32, (depth_y, LANES), 0) - lax.axis_index("sy") * CY
    for copy in copies:
        copy.wait()
    code = labels[0] * 8 + labels[1] + 1
    code = code.astype(jnp.float32).astype(jnp.bfloat16).reshape(planes * depth_y, depth_x)
    spread = jnp.dot(code, pick, preferred_element_type=jnp.float32)
    codes[...] = jnp.zeros(codes.shape, jnp.float32)
    for off, (dx, dy) in enumerate(OFFSETS):
        block = spread[:, (dx + 2) * LANES : (dx + 3) * LANES].reshape(planes, depth_y, LANES)
        picked = jnp.sum(jnp.where((y_row == y_lane + dy)[None], block, 0.0), axis=1)
        codes[off, pl.ds(ahead, planes), :] = picked
    for t, (dz, off) in enumerate(TAPS):
        row = dz + 4
        code = codes[off, row : row + SLAB, :]
        code = jnp.concatenate([code, code], axis=0).astype(jnp.int32)
        inside = code > 0
        code = code - 1
        region = lax.shift_right_logical(code, 3)
        level = code & 7
        real = jnp.zeros((8, LANES), jnp.float32)
        imag = jnp.zeros((8, LANES), jnp.float32)
        for value in range(8):
            real = jnp.where(region == value, eps_ref[value], real)
            imag = jnp.where(level == value, gain_ref[value], imag)
        out_ref[t] = real
        out_ref[len(TAPS) + t] = imag
        out_ref[2 * len(TAPS) + t] = jnp.where(inside, 1.0, 0.0)


def cmul(a, b):
    return (a[0] * b[0] - a[1] * b[1], a[0] * b[1] + a[1] * b[0])


def cadd(a, b):
    return (a[0] + b[0], a[1] + b[1])


def moment_kernel(
    weight_ref,
    material_ref,
    own_ref,
    ylo_ref,
    yhi_ref,
    xlo_ref,
    xhi_ref,
    pick_ref,
    moments_ref,
    cross_ref,
    shifted,
    coef,
    folded,
):
    for plane in range(SLAB + 4):
        near, far = (plane - 1) * 16, 96 + (plane - 2) * 16
        sides = (ylo_ref, yhi_ref, xlo_ref, xhi_ref)
        if 2 <= plane < SLAB + 2:
            reach, starts = 13, (near, far)
        elif plane in (1, SLAB + 2):
            reach, starts = 5, (near, near)
        else:
            reach, starts = 1, ()
        rows = [own_ref[plane]] + [ref[i : i + 16] for ref in sides for i in starts]
        rows = jnp.concatenate(rows, axis=0) if starts else rows[0]
        picked = lax.dot_general(
            rows,
            pick_ref[: rows.shape[0], : reach * LANES],
            (((0,), (0,)), ((), ())),
            preferred_element_type=jnp.float32,
        )
        for off in range(reach):
            shifted[plane, off] = picked[:, off * LANES : (off + 1) * LANES]

    coef[...] = jnp.zeros(coef.shape, jnp.float32)
    first_half = lax.broadcasted_iota(jnp.int32, (8, LANES), 0) < SLAB

    def one_pair(pair, carry):
        weight = (
            jnp.where(first_half, weight_ref[0, 2 * pair], weight_ref[0, 2 * pair + 1]),
            jnp.where(
                first_half, weight_ref[0, QUAD + 2 * pair], weight_ref[0, QUAD + 2 * pair + 1]
            ),
        )
        node = (2.0 + weight[0], weight[1])
        inv = []
        for t in range(len(TAPS)):
            real, imag = material_ref[t], material_ref[len(TAPS) + t]
            diag_real = 6.0 + node[0] * real - node[1] * imag
            diag_imag = node[0] * imag + node[1] * real
            scale = material_ref[2 * len(TAPS) + t] / (diag_real * diag_real + diag_imag * diag_imag)
            inv.append((diag_real * scale, -(diag_imag * scale)))
        centre = inv[TAP_AT[(0, 0, 0)]]
        lead0 = cmul(weight, centre)
        lead1 = cmul(node, lead0)
        for t, (dz, off) in enumerate(TAPS):
            step = (dz,) + OFFSETS[off]
            size = sum(abs(d) for d in step)
            if size == 0:
                near = functools.reduce(cadd, [inv[TAP_AT[u]] for u in UNITS])
                term = cmul(centre, near)
                term = (1.0 + term[0], term[1])
            elif size == 1:
                term = inv[t]
            else:
                mids = [
                    inv[TAP_AT[u]]
                    for u in UNITS
                    if sum(abs(s - d) for s, d in zip(step, u)) == 1
                ]
                term = cmul(inv[t], functools.reduce(cadd, mids))
            for k, lead in enumerate((lead0, lead1)):
                real, imag = cmul(lead, term)
                coef[4 * t + 2 * k] += real
                coef[4 * t + 2 * k + 1] += imag
        return carry

    lax.fori_loop(0, QUAD // 2, one_pair, 0)
    for i in range(2 * len(TAPS)):
        real, imag = coef[2 * i], coef[2 * i + 1]
        real = real + pltpu.roll(real, SLAB, axis=0)
        imag = imag + pltpu.roll(imag, SLAB, axis=0)
        folded[3 * i] = real
        folded[3 * i + 1] = imag - real
        folded[3 * i + 2] = real + imag

    half = 64
    part = 32

    def one_chunk(step, carry):
        z = step // 2
        col = pl.multiple_of((step % 2) * part, part)
        sums = [jnp.zeros((part, LANES), jnp.float32) for _ in range(6)]
        for t, (dz, off) in enumerate(TAPS):
            real = shifted[z + 2 + dz, off, pl.ds(col, part), :]
            imag = shifted[z + 2 + dz, off, pl.ds(half + col, part), :]
            factors = (real + imag, real, imag)
            for i in range(6):
                sums[i] += folded[6 * t + i, pl.ds(z, 1), :] * factors[i % 3]
        for k in range(2):
            both, minus, plus = sums[3 * k : 3 * k + 3]
            moments_ref[k, z, pl.ds(col, part), :] = both - plus
            moments_ref[k, z, pl.ds(half + col, part), :] = both + minus
        return carry

    lax.fori_loop(0, 2 * SLAB, one_chunk, 0)

    cross = jnp.zeros((half, 4 * half), jnp.float32)
    for z in range(SLAB):
        left = jnp.concatenate([shifted[z + 2, 0, :half], shifted[z + 2, 0, half:]], axis=1)
        left = left.astype(jnp.bfloat16)
        rows = []
        for k in range(2):
            real = moments_ref[k, z, :half]
            imag = moments_ref[k, z, half:]
            rows.append(jnp.concatenate([real, imag], axis=1))
            rows.append(jnp.concatenate([imag, -real], axis=1))
        right = jnp.concatenate(rows, axis=0)
        high = right.astype(jnp.bfloat16)
        low = (right - high.astype(jnp.float32)).astype(jnp.bfloat16)
        for piece in (high, low):
            cross += lax.dot_general(
                left, piece, (((1,), (1,)), ((), ())), preferred_element_type=jnp.float32
            )
    cross_ref[...] = cross * (1.0 / 131072)


def turn_kernel(moments_ref, first_ref, second_ref):
    for k, out_ref in enumerate((first_ref, second_ref)):
        for z in range(SLAB):
            out_ref[z] = moments_ref[k, z].T


def turn(moments, columns):
    out = jax.ShapeDtypeStruct((SLAB, LANES, columns), jnp.float32)
    vmem = pl.BlockSpec(memory_space=pltpu.VMEM)
    return pl.pallas_call(
        turn_kernel,
        out_shape=[out] * 2,
        in_specs=[vmem],
        out_specs=[vmem] * 2,
        compiler_params=pltpu.CompilerParams(vmem_limit_bytes=8 * 1024 * 1024),
        cost_estimate=pl.CostEstimate(flops=1000000, bytes_accessed=1000000, transcendentals=0),
        name="turn",
    )(moments)


def swap(block, bits):
    axes = tuple(bits)
    sizes = [lax.axis_size(axis) for axis in axes]
    pairs = []
    for place in np.ndindex(*sizes):
        other = tuple(i ^ bit for i, bit in zip(place, bits.values()))
        pairs.append((int(np.ravel_multi_index(place, sizes)), int(np.ravel_multi_index(other, sizes))))
    return lax.ppermute(block, axes, pairs)


def sum_of_four(block, *steps):
    first, second, third = (swap(block, step) for step in steps)
    return (block + first) + (second + third)


def body(probes, quad_index, region_label, gain_label, region_eps, gain_rate):
    depth, cells_x, cells_y, columns = probes.shape
    planes = SLAB + 4
    core = lax.axis_index("sx") & 1
    even_x = core == 0
    even_y = (lax.axis_index("sy") & 1) == 0
    smem = pl.BlockSpec(memory_space=pltpu.SMEM)
    vmem = pl.BlockSpec(memory_space=pltpu.VMEM)
    hbm = pl.BlockSpec(memory_space=pltpu.HBM)
    mib = 1024 * 1024
    shapes = [
        (planes, cells_x * cells_y, columns),
        (PARTS + 16, columns),
        (PARTS + 16, columns),
        (FAR, columns),
        (FAR, columns),
    ]
    own, first, second, third, fourth = pl.pallas_call(
        slab_kernel,
        out_shape=[jax.ShapeDtypeStruct(shape, probes.dtype) for shape in shapes],
        in_specs=[smem, hbm],
        out_specs=[vmem] * 5,
        scratch_shapes=[
            pltpu.VMEM((4 * SLAB + 4, cells_x * cells_y, columns), probes.dtype),
            pltpu.VMEM((2, planes, cells_x * cells_y, columns), probes.dtype),
            pltpu.VMEM((4, SLAB, 16, columns), probes.dtype),
            pltpu.SemaphoreType.DMA((7,)),
        ]
        + [pltpu.VMEM(((SLAB + 2) * LANES, columns), jnp.float32)] * 2,
        compiler_params=pltpu.CompilerParams(vmem_limit_bytes=52 * mib),
        cost_estimate=pl.CostEstimate(flops=10000000, bytes_accessed=600000, transcendentals=0),
        name="slab",
    )(quad_index, probes.reshape(depth, cells_x * cells_y, columns))

    def corner_rows(at):
        cells = [inner[at : at + SLAB], outer[at : at + SLAB]]
        low, high = jnp.where(even_y, cells[1], cells[0]), jnp.where(even_y, cells[0], cells[1])
        rows = jnp.pad(jnp.stack([low, high], axis=1), ((0, 0), (0, 14), (0, 0)))
        return rows.reshape(SLAB * 16, columns)

    parts = first[PARTS:]
    inner = swap(first, dict(quad=1, sy=1))
    outer = swap(second, dict(quad=3, sy=3))
    last = swap(parts, dict(quad=2))
    parts = (parts + inner[PARTS:]) + (outer[PARTS:] + last)
    ylo = jnp.where(even_y, outer, inner)[:CORNERS]
    yhi = jnp.where(even_y, inner, outer)[:CORNERS]
    third = jnp.concatenate([third, corner_rows(CORNERS), parts], axis=0)
    fourth = jnp.concatenate([fourth, corner_rows(CORNERS + SLAB), parts], axis=0)
    near = swap(third, dict(quad=4, sx=1))
    beyond = swap(fourth, dict(quad=8, sx=3))
    last = swap(parts, dict(quad=12))
    parts = (parts + near[CORNERS:]) + (beyond[CORNERS:] + last)
    xlo = jnp.where(even_x, beyond, near)[:CORNERS]
    xhi = jnp.where(even_x, near, beyond)[:CORNERS]
    weight = jnp.sum(parts[:3].astype(jnp.float32), axis=0, keepdims=True)

    taps = len(TAPS)
    material, pick = pl.pallas_call(
        material_kernel,
        out_shape=[
            jax.ShapeDtypeStruct((3 * taps, 8, LANES), jnp.float32),
            jax.ShapeDtypeStruct((256, WIDE), jnp.bfloat16),
        ],
        in_specs=[smem, smem, hbm, hbm],
        out_specs=[vmem] * 2,
        scratch_shapes=[
            pltpu.VMEM((2, planes) + region_label.shape[:0:-1], jnp.int32),
            pltpu.VMEM((len(OFFSETS), 16, LANES), jnp.float32),
            pltpu.SemaphoreType.DMA((2,)),
        ],
        compiler_params=pltpu.CompilerParams(vmem_limit_bytes=52 * mib),
        cost_estimate=pl.CostEstimate(flops=40000000, bytes_accessed=1200000, transcendentals=0),
        name="material",
    )(region_eps, gain_rate, region_label.swapaxes(1, 2), gain_label.swapaxes(1, 2))

    moments, cross = pl.pallas_call(
        moment_kernel,
        out_shape=[
            jax.ShapeDtypeStruct((2, SLAB, columns, LANES), jnp.float32),
            jax.ShapeDtypeStruct((64, 256), jnp.float32),
        ],
        in_specs=[smem] + [vmem] * 7,
        out_specs=[vmem] * 2,
        scratch_shapes=[
            pltpu.VMEM((planes, len(OFFSETS), columns, LANES), jnp.float32),
            pltpu.VMEM((4 * taps, 8, LANES), jnp.float32),
            pltpu.VMEM((6 * taps, 8, LANES), jnp.float32),
        ],
        compiler_params=pltpu.CompilerParams(vmem_limit_bytes=24 * mib),
        cost_estimate=pl.CostEstimate(flops=600000000, bytes_accessed=3000000, transcendentals=0),
        name="moments",
    )(weight, material, own, ylo, yhi, xlo, xhi, pick)

    width = cross.shape[1] // 2
    block = jnp.where(core == 0, cross[:, :width], cross[:, width:])
    block = block + swap(jnp.where(core == 0, cross[:, width:], cross[:, :width]), dict(sx=1))
    block = sum_of_four(block, dict(sy=1), dict(sy=3), dict(sy=2))
    block = sum_of_four(block, dict(quad=1), dict(quad=3), dict(quad=2))
    block = sum_of_four(block, dict(quad=4), dict(quad=8, sx=2), dict(quad=12, sx=2))
    block, moments = lax.optimization_barrier((block, moments))
    block = block + swap(block, dict(quad=8))
    first, second = turn(moments, columns)
    block, first, second = lax.optimization_barrier((block, first, second))
    other = swap(block, dict(sx=1))
    halves = (jnp.where(core == 0, block, other), jnp.where(core == 0, other, block))
    projections = jnp.stack(
        [jnp.stack([half[:, :64], half[:, 64:]], axis=0) for half in halves], axis=0
    )
    shape = (SLAB, cells_x, cells_y, columns)
    return (first.reshape(shape), second.reshape(shape), projections)


def solution(mesh):
    placed = (P(None, "sx", "sy", None), P("quad"), P(), P(), P(), P())
    return jax.shard_map(
        body,
        mesh=mesh,
        in_specs=placed,
        out_specs=(P("quad", "sx", "sy", None), P("quad", "sx", "sy", None), P()),
        check_vma=False,
    )
```

```python
import functools
import math

import jax
import jax.numpy as jnp
import numpy as np
from jax import lax
from jax.experimental import pallas as pl
from jax.experimental.pallas import tpu as pltpu
from jax.sharding import PartitionSpec as P

QUAD = 16
SLAB = 4
CX = 16
CY = 8
LANES = CX * CY

OFFSETS = sorted(
    [(dx, dy) for dx in range(-2, 3) for dy in range(-2, 3) if abs(dx) + abs(dy) <= 2],
    key=lambda o: (abs(o[0]) + abs(o[1]), o),
)
REACH = {0: 13, 1: 5, 2: 1}
TAPS = [(dz, off) for dz in range(-2, 3) for off in range(REACH[abs(dz)])]
TAP_AT = {(dz,) + OFFSETS[off]: i for i, (dz, off) in enumerate(TAPS)}
UNITS = [(1, 0, 0), (-1, 0, 0), (0, 1, 0), (0, -1, 0), (0, 0, 1), (0, 0, -1)]
WIDE = len(OFFSETS) * LANES
FAR = (SLAB + 2) * CX
CORNERS = FAR + SLAB * CX
PARTS = CORNERS + 16


def cell_code(x, y):
    return (x + 2) * 32 + y + 2


def write_selector(pick_ref):
    row = lax.broadcasted_iota(jnp.int32, (16, LANES), 0)
    lane = lax.broadcasted_iota(jnp.int32, (16, LANES), 1)
    own = cell_code(lax.shift_right_logical(lane, 3), lane & 7)

    def pair_of_x(x):
        return cell_code(x + lax.shift_right_logical(row, 3), row & 7)

    tiles = [pair_of_x(2 * i) for i in range(CX // 2)]
    tiles += [cell_code(row, y) for y in (-1, -2, CY, CY + 1)]
    for first, near in ((-2, -1), (CX, CX)):
        corners = jnp.where(row == 1, cell_code(near, CY), -1)
        tiles += [pair_of_x(first), jnp.where(row == 0, cell_code(near, -1), corners)]
    for i, tile in enumerate(tiles):
        for off, (dx, dy) in enumerate(OFFSETS):
            hit = jnp.where(tile == own + (dx * 32 + dy), 1.0, 0.0).astype(jnp.bfloat16)
            pick_ref[i * 16 : i * 16 + 16, off * LANES : (off + 1) * LANES] = hit


def slab_kernel(
    quad_ref, probes_ref, own_ref, first_ref, second_ref, third_ref, fourth_ref, block, side, rim, sems, *whole
):
    depth = probes_ref.shape[0]
    me = lax.axis_index("quad")
    even_x = (lax.axis_index("sx") & 1) == 0
    even_y = (lax.axis_index("sy") & 1) == 0

    group = 4 * SLAB + 4
    bases = [jnp.clip((me & ~3) * SLAB - 2, 0, depth - group)]
    bases += [jnp.clip((me ^ bit) * SLAB - 2, 0, depth - SLAB - 4) for bit in (4, 8)]
    held = (block, side.at[0], side.at[1])
    copies = [
        pltpu.make_async_copy(probes_ref.at[pl.ds(base, to.shape[0])], to, sems.at[i])
        for i, (base, to) in enumerate(zip(bases, held))
    ]
    edges = ((4, even_x), (8, jnp.logical_not(even_x)))
    for i, step in enumerate((1, 3)):
        for j, (bit, high) in enumerate(edges):
            at = pl.multiple_of(jnp.where(high, LANES - 16, 0), 16)
            start = ((me ^ step) ^ bit) * SLAB
            edge = probes_ref.at[pl.ds(start, SLAB), pl.ds(at, 16)]
            copies.append(pltpu.make_async_copy(edge, rim.at[2 * i + j], sems.at[len(copies)]))
    for copy in copies:
        copy.start()

    def plane(slab, p, bit=0):
        z = jnp.clip(slab * SLAB + (p - 2), 0, depth - 1)
        at = {0: 0, 4: 1, 8: 2}[bit]
        return held[at][z - bases[at]]

    def x_edge(values, high):
        low, top = values[:16].astype(jnp.float32), values[LANES - 16 :].astype(jnp.float32)
        return jnp.where(high, top, low)

    index = jnp.full((1, LANES), quad_ref[0], jnp.int32).astype(jnp.float32)
    angle = 2.0 * math.pi * (index + 0.5) / (4 * QUAD)
    lane = lax.broadcasted_iota(jnp.int32, (1, LANES), 1)
    weight = jnp.where(lane == me, jnp.cos(angle), 0.0)
    weight = jnp.where(lane == me + QUAD, jnp.sin(angle), weight)
    row = lax.broadcasted_iota(jnp.int32, (16, LANES), 0)
    parts = jnp.zeros((16, LANES), jnp.float32)
    for i in range(3):
        part = weight.astype(jnp.bfloat16).astype(jnp.float32)
        parts = jnp.where(row == i, part, parts)
        weight = weight - part
    first_ref[PARTS : PARTS + 16] = parts.astype(jnp.bfloat16)
    second_ref[PARTS : PARTS + 16] = parts.astype(jnp.bfloat16)

    for copy in copies:
        copy.wait()
    sends = ((first_ref, whole[0], 1, even_y), (second_ref, whole[1], 3, jnp.logical_not(even_y)))
    for send, (out_ref, scratch, step, high) in enumerate(sends):
        target = me ^ step
        for p in range(1, SLAB + 3):
            scratch[(p - 1) * LANES : p * LANES] = plane(target, p).astype(jnp.float32)
        for at, start, count, deep in ((0, 0, SLAB + 2, 0), (FAR, LANES, SLAB, 1)):
            low = scratch[pl.ds(start + deep, count * CX, stride=CY), :]
            top = scratch[pl.ds(start + CY - 1 - deep, count * CX, stride=CY), :]
            out_ref[at : at + count * CX] = jnp.where(high, top, low).astype(jnp.bfloat16)
        corners = jnp.zeros((16, LANES), jnp.float32)
        for i, (bit, edge) in enumerate(edges):
            cell = jnp.where(edge, CY, 0) + jnp.where(high, CY - 1, 0)
            for p in range(SLAB):
                picked = jnp.where(row == cell, rim[2 * send + i, p].astype(jnp.float32), 0.0)
                picked = jnp.sum(picked, axis=0, keepdims=True)
                corners = jnp.where(row == i * SLAB + p, picked, corners)
        out_ref[CORNERS : CORNERS + 16] = corners.astype(jnp.bfloat16)

    for out_ref, (bit, high) in zip((third_ref, fourth_ref), edges):
        for p in range(1, SLAB + 3):
            out_ref[(p - 1) * 16 : p * 16] = x_edge(plane(me ^ bit, p, bit), high).astype(jnp.bfloat16)
    for p in range(SLAB + 4):
        own_ref[p] = plane(me, p)


def pack_kernel(inner_ref, outer_ref, last_ref, first_ref, third_ref, fourth_ref, near_ref, beyond_ref):
    even_y = (lax.axis_index("sy") & 1) == 0
    inner = inner_ref[CORNERS:].astype(jnp.float32)
    outer = outer_ref[CORNERS:].astype(jnp.float32)
    low, high = jnp.where(even_y, outer, inner), jnp.where(even_y, inner, outer)
    parts = (first_ref[PARTS:].astype(jnp.float32) + inner[16:]) + (
        outer[16:] + last_ref[...].astype(jnp.float32)
    )
    row = lax.broadcasted_iota(jnp.int32, (16, LANES), 0)
    for i, (layers_ref, out_ref) in enumerate(((third_ref, near_ref), (fourth_ref, beyond_ref))):
        out_ref[:FAR] = layers_ref[...]
        for p in range(SLAB):
            at = i * SLAB + p
            corner = jnp.where(row == 1, high[at : at + 1], 0.0)
            corner = jnp.where(row == 0, low[at : at + 1], corner)
            out_ref[FAR + p * 16 : FAR + (p + 1) * 16] = corner.astype(jnp.bfloat16)
        out_ref[CORNERS:] = parts.astype(jnp.bfloat16)


def material_kernel(eps_ref, gain_ref, region_ref, level_ref, out_ref, pick_ref, labels, codes, sems):
    planes = SLAB + 4
    start = lax.axis_index("quad") * SLAB
    first = jnp.clip(start - 2, 0, region_ref.shape[0] - planes)
    ahead = first - start + 4
    copies = [
        pltpu.make_async_copy(ref.at[pl.ds(first, planes)], labels.at[i], sems.at[i])
        for i, ref in enumerate((region_ref, level_ref))
    ]
    for copy in copies:
        copy.start()
    write_selector(pick_ref)
    depth_y, depth_x = labels.shape[2:]
    lane = lax.broadcasted_iota(jnp.int32, (depth_x, LANES), 1)
    x_row = lax.broadcasted_iota(jnp.int32, (depth_x, LANES), 0) - lax.axis_index("sx") * CX
    picks = [
        jnp.where(x_row == lax.shift_right_logical(lane, 3) + dx, 1.0, 0.0) for dx in range(-2, 3)
    ]
    pick = jnp.concatenate(picks, axis=1).astype(jnp.bfloat16)
    y_lane = lax.broadcasted_iota(jnp.int32, (depth_y, LANES), 1) & 7
    y_row = lax.broadcasted_iota(jnp.int32, (depth_y, LANES), 0) - lax.axis_index("sy") * CY
    for copy in copies:
        copy.wait()
    code = labels[0] * 8 + labels[1] + 1
    code = code.astype(jnp.float32).astype(jnp.bfloat16).reshape(planes * depth_y, depth_x)
    spread = jnp.dot(code, pick, preferred_element_type=jnp.float32)
    codes[...] = jnp.zeros(codes.shape, jnp.float32)
    for off, (dx, dy) in enumerate(OFFSETS):
        block = spread[:, (dx + 2) * LANES : (dx + 3) * LANES].reshape(planes, depth_y, LANES)
        picked = jnp.sum(jnp.where((y_row == y_lane + dy)[None], block, 0.0), axis=1)
        codes[off, pl.ds(ahead, planes), :] = picked
    for t, (dz, off) in enumerate(TAPS):
        row = dz + 4
        code = codes[off, row : row + SLAB, :]
        code = jnp.concatenate([code, code], axis=0).astype(jnp.int32)
        inside = code > 0
        code = code - 1
        region = lax.shift_right_logical(code, 3)
        level = code & 7
        real = jnp.zeros((8, LANES), jnp.float32)
        imag = jnp.zeros((8, LANES), jnp.float32)
        for value in range(8):
            real = jnp.where(region == value, eps_ref[value], real)
            imag = jnp.where(level == value, gain_ref[value], imag)
        out_ref[t] = real
        out_ref[len(TAPS) + t] = imag
        out_ref[2 * len(TAPS) + t] = jnp.where(inside, 1.0, 0.0)


def cmul(a, b):
    return (a[0] * b[0] - a[1] * b[1], a[0] * b[1] + a[1] * b[0])


def cadd(a, b):
    return (a[0] + b[0], a[1] + b[1])


def moment_kernel(
    weight_ref,
    material_ref,
    own_ref,
    ylo_ref,
    yhi_ref,
    xlo_ref,
    xhi_ref,
    pick_ref,
    moments_ref,
    cross_ref,
    shifted,
    coef,
    folded,
):
    for plane in range(SLAB + 4):
        near, far = (plane - 1) * 16, 96 + (plane - 2) * 16
        sides = (ylo_ref, yhi_ref, xlo_ref, xhi_ref)
        if 2 <= plane < SLAB + 2:
            reach, starts = 13, (near, far)
        elif plane in (1, SLAB + 2):
            reach, starts = 5, (near, near)
        else:
            reach, starts = 1, ()
        rows = [own_ref[plane]] + [ref[i : i + 16] for ref in sides for i in starts]
        rows = jnp.concatenate(rows, axis=0) if starts else rows[0]
        picked = lax.dot_general(
            rows,
            pick_ref[: rows.shape[0], : reach * LANES],
            (((0,), (0,)), ((), ())),
            preferred_element_type=jnp.float32,
        )
        for off in range(reach):
            shifted[plane, off] = picked[:, off * LANES : (off + 1) * LANES]

    coef[...] = jnp.zeros(coef.shape, jnp.float32)
    first_half = lax.broadcasted_iota(jnp.int32, (8, LANES), 0) < SLAB

    def one_pair(pair, carry):
        weight = (
            jnp.where(first_half, weight_ref[0, 2 * pair], weight_ref[0, 2 * pair + 1]),
            jnp.where(
                first_half, weight_ref[0, QUAD + 2 * pair], weight_ref[0, QUAD + 2 * pair + 1]
            ),
        )
        node = (2.0 + weight[0], weight[1])
        inv = []
        for t in range(len(TAPS)):
            real, imag = material_ref[t], material_ref[len(TAPS) + t]
            diag_real = 6.0 + node[0] * real - node[1] * imag
            diag_imag = node[0] * imag + node[1] * real
            scale = material_ref[2 * len(TAPS) + t] / (diag_real * diag_real + diag_imag * diag_imag)
            inv.append((diag_real * scale, -(diag_imag * scale)))
        centre = inv[TAP_AT[(0, 0, 0)]]
        lead0 = cmul(weight, centre)
        lead1 = cmul(node, lead0)
        for t, (dz, off) in enumerate(TAPS):
            step = (dz,) + OFFSETS[off]
            size = sum(abs(d) for d in step)
            if size == 0:
                near = functools.reduce(cadd, [inv[TAP_AT[u]] for u in UNITS])
                term = cmul(centre, near)
                term = (1.0 + term[0], term[1])
            elif size == 1:
                term = inv[t]
            else:
                mids = [
                    inv[TAP_AT[u]]
                    for u in UNITS
                    if sum(abs(s - d) for s, d in zip(step, u)) == 1
                ]
                term = cmul(inv[t], functools.reduce(cadd, mids))
            for k, lead in enumerate((lead0, lead1)):
                real, imag = cmul(lead, term)
                coef[4 * t + 2 * k] += real
                coef[4 * t + 2 * k + 1] += imag
        return carry

    lax.fori_loop(0, QUAD // 2, one_pair, 0)
    for i in range(2 * len(TAPS)):
        real, imag = coef[2 * i], coef[2 * i + 1]
        real = real + pltpu.roll(real, SLAB, axis=0)
        imag = imag + pltpu.roll(imag, SLAB, axis=0)
        folded[3 * i] = real
        folded[3 * i + 1] = imag - real
        folded[3 * i + 2] = real + imag

    half = 64
    part = 32

    def one_chunk(step, carry):
        z = step // 2
        col = pl.multiple_of((step % 2) * part, part)
        sums = [jnp.zeros((part, LANES), jnp.float32) for _ in range(6)]
        for t, (dz, off) in enumerate(TAPS):
            real = shifted[z + 2 + dz, off, pl.ds(col, part), :]
            imag = shifted[z + 2 + dz, off, pl.ds(half + col, part), :]
            factors = (real + imag, real, imag)
            for i in range(6):
                sums[i] += folded[6 * t + i, pl.ds(z, 1), :] * factors[i % 3]
        for k in range(2):
            both, minus, plus = sums[3 * k : 3 * k + 3]
            moments_ref[k, z, pl.ds(col, part), :] = both - plus
            moments_ref[k, z, pl.ds(half + col, part), :] = both + minus
        return carry

    lax.fori_loop(0, 2 * SLAB, one_chunk, 0)

    cross = jnp.zeros((half, 4 * half), jnp.float32)
    for z in range(SLAB):
        left = jnp.concatenate([shifted[z + 2, 0, :half], shifted[z + 2, 0, half:]], axis=1)
        left = left.astype(jnp.bfloat16)
        rows = []
        for k in range(2):
            real = moments_ref[k, z, :half]
            imag = moments_ref[k, z, half:]
            rows.append(jnp.concatenate([real, imag], axis=1))
            rows.append(jnp.concatenate([imag, -real], axis=1))
        right = jnp.concatenate(rows, axis=0)
        high = right.astype(jnp.bfloat16)
        low = (right - high.astype(jnp.float32)).astype(jnp.bfloat16)
        for piece in (high, low):
            cross += lax.dot_general(
                left, piece, (((1,), (1,)), ((), ())), preferred_element_type=jnp.float32
            )
    cross_ref[...] = cross * (1.0 / 131072)


def turn_kernel(moments_ref, first_ref, second_ref):
    for k, out_ref in enumerate((first_ref, second_ref)):
        for z in range(SLAB):
            out_ref[z] = moments_ref[k, z].T


def turn(moments, columns):
    out = jax.ShapeDtypeStruct((SLAB, LANES, columns), jnp.float32)
    vmem = pl.BlockSpec(memory_space=pltpu.VMEM)
    return pl.pallas_call(
        turn_kernel,
        out_shape=[out] * 2,
        in_specs=[vmem],
        out_specs=[vmem] * 2,
        compiler_params=pltpu.CompilerParams(vmem_limit_bytes=8 * 1024 * 1024),
        cost_estimate=pl.CostEstimate(flops=1000000, bytes_accessed=1000000, transcendentals=0),
        name="turn",
    )(moments)


def swap(block, bits):
    axes = tuple(bits)
    sizes = [lax.axis_size(axis) for axis in axes]
    pairs = []
    for place in np.ndindex(*sizes):
        other = tuple(i ^ bit for i, bit in zip(place, bits.values()))
        pairs.append((int(np.ravel_multi_index(place, sizes)), int(np.ravel_multi_index(other, sizes))))
    return lax.ppermute(block, axes, pairs)


def sum_of_four(block, *steps):
    first, second, third = (swap(block, step) for step in steps)
    return (block + first) + (second + third)


def body(probes, quad_index, region_label, gain_label, region_eps, gain_rate):
    depth, cells_x, cells_y, columns = probes.shape
    planes = SLAB + 4
    core = lax.axis_index("sx") & 1
    even_x = core == 0
    even_y = (lax.axis_index("sy") & 1) == 0
    smem = pl.BlockSpec(memory_space=pltpu.SMEM)
    vmem = pl.BlockSpec(memory_space=pltpu.VMEM)
    hbm = pl.BlockSpec(memory_space=pltpu.HBM)
    mib = 1024 * 1024
    shapes = [
        (planes, cells_x * cells_y, columns),
        (PARTS + 16, columns),
        (PARTS + 16, columns),
        (FAR, columns),
        (FAR, columns),
    ]
    own, first, second, third, fourth = pl.pallas_call(
        slab_kernel,
        out_shape=[jax.ShapeDtypeStruct(shape, probes.dtype) for shape in shapes],
        in_specs=[smem, hbm],
        out_specs=[vmem] * 5,
        scratch_shapes=[
            pltpu.VMEM((4 * SLAB + 4, cells_x * cells_y, columns), probes.dtype),
            pltpu.VMEM((2, planes, cells_x * cells_y, columns), probes.dtype),
            pltpu.VMEM((4, SLAB, 16, columns), probes.dtype),
            pltpu.SemaphoreType.DMA((7,)),
        ]
        + [pltpu.VMEM(((SLAB + 2) * LANES, columns), jnp.float32)] * 2,
        compiler_params=pltpu.CompilerParams(vmem_limit_bytes=52 * mib),
        cost_estimate=pl.CostEstimate(flops=10000000, bytes_accessed=600000, transcendentals=0),
        name="slab",
    )(quad_index, probes.reshape(depth, cells_x * cells_y, columns))

    inner = swap(first, dict(quad=1, sy=1))
    outer = swap(second, dict(quad=3, sy=3))
    last = swap(first[PARTS:], dict(quad=2))
    ylo = jnp.where(even_y, outer, inner)[:CORNERS]
    yhi = jnp.where(even_y, inner, outer)[:CORNERS]
    to_near, to_beyond = pl.pallas_call(
        pack_kernel,
        out_shape=[jax.ShapeDtypeStruct((CORNERS + 16, columns), probes.dtype)] * 2,
        in_specs=[vmem] * 6,
        out_specs=[vmem] * 2,
        compiler_params=pltpu.CompilerParams(vmem_limit_bytes=4 * mib),
        cost_estimate=pl.CostEstimate(flops=100000, bytes_accessed=200000, transcendentals=0),
        name="pack",
    )(inner, outer, last, first, third, fourth)
    beyond = swap(to_beyond, dict(quad=8, sx=3))
    near = swap(to_near, dict(quad=4, sx=1))
    parts = to_near[CORNERS:]
    last = swap(parts, dict(quad=12))
    parts = (parts + near[CORNERS:]) + (beyond[CORNERS:] + last)
    xlo = jnp.where(even_x, beyond, near)[:CORNERS]
    xhi = jnp.where(even_x, near, beyond)[:CORNERS]
    weight = jnp.sum(parts[:3].astype(jnp.float32), axis=0, keepdims=True)

    taps = len(TAPS)
    material, pick = pl.pallas_call(
        material_kernel,
        out_shape=[
            jax.ShapeDtypeStruct((3 * taps, 8, LANES), jnp.float32),
            jax.ShapeDtypeStruct((256, WIDE), jnp.bfloat16),
        ],
        in_specs=[smem, smem, hbm, hbm],
        out_specs=[vmem] * 2,
        scratch_shapes=[
            pltpu.VMEM((2, planes) + region_label.shape[:0:-1], jnp.int32),
            pltpu.VMEM((len(OFFSETS), 16, LANES), jnp.float32),
            pltpu.SemaphoreType.DMA((2,)),
        ],
        compiler_params=pltpu.CompilerParams(vmem_limit_bytes=52 * mib),
        cost_estimate=pl.CostEstimate(flops=40000000, bytes_accessed=1200000, transcendentals=0),
        name="material",
    )(region_eps, gain_rate, region_label.swapaxes(1, 2), gain_label.swapaxes(1, 2))

    moments, cross = pl.pallas_call(
        moment_kernel,
        out_shape=[
            jax.ShapeDtypeStruct((2, SLAB, columns, LANES), jnp.float32),
            jax.ShapeDtypeStruct((64, 256), jnp.float32),
        ],
        in_specs=[smem] + [vmem] * 7,
        out_specs=[vmem] * 2,
        scratch_shapes=[
            pltpu.VMEM((planes, len(OFFSETS), columns, LANES), jnp.float32),
            pltpu.VMEM((4 * taps, 8, LANES), jnp.float32),
            pltpu.VMEM((6 * taps, 8, LANES), jnp.float32),
        ],
        compiler_params=pltpu.CompilerParams(vmem_limit_bytes=24 * mib),
        cost_estimate=pl.CostEstimate(flops=600000000, bytes_accessed=3000000, transcendentals=0),
        name="moments",
    )(weight, material, own, ylo, yhi, xlo, xhi, pick)

    width = cross.shape[1] // 2
    block = jnp.where(core == 0, cross[:, :width], cross[:, width:])
    block = block + swap(jnp.where(core == 0, cross[:, width:], cross[:, :width]), dict(sx=1))
    block = sum_of_four(block, dict(sy=1), dict(sy=3), dict(sy=2))
    block = sum_of_four(block, dict(quad=1), dict(quad=3), dict(quad=2))
    block = sum_of_four(block, dict(quad=4), dict(quad=8, sx=2), dict(quad=12, sx=2))
    block, moments = lax.optimization_barrier((block, moments))
    block = block + swap(block, dict(quad=8))
    first, second = turn(moments, columns)
    block, first, second = lax.optimization_barrier((block, first, second))
    other = swap(block, dict(sx=1))
    halves = (jnp.where(core == 0, block, other), jnp.where(core == 0, other, block))
    projections = jnp.stack(
        [jnp.stack([half[:, :64], half[:, 64:]], axis=0) for half in halves], axis=0
    )
    shape = (SLAB, cells_x, cells_y, columns)
    return (first.reshape(shape), second.reshape(shape), projections)


def solution(mesh):
    placed = (P(None, "sx", "sy", None), P("quad"), P(), P(), P(), P())
    return jax.shard_map(
        body,
        mesh=mesh,
        in_specs=placed,
        out_specs=(P("quad", "sx", "sy", None), P("quad", "sx", "sy", None), P()),
        check_vma=False,
    )
```

```python
import functools
import math

import jax
import jax.numpy as jnp
import numpy as np
from jax import lax
from jax.experimental import pallas as pl
from jax.experimental.pallas import tpu as pltpu
from jax.sharding import PartitionSpec as P

QUAD = 16
SLAB = 4
CX = 16
CY = 8
LANES = CX * CY

OFFSETS = sorted(
    [(dx, dy) for dx in range(-2, 3) for dy in range(-2, 3) if abs(dx) + abs(dy) <= 2],
    key=lambda o: (abs(o[0]) + abs(o[1]), o),
)
REACH = {0: 13, 1: 5, 2: 1}
TAPS = [(dz, off) for dz in range(-2, 3) for off in range(REACH[abs(dz)])]
TAP_AT = {(dz,) + OFFSETS[off]: i for i, (dz, off) in enumerate(TAPS)}
UNITS = [(1, 0, 0), (-1, 0, 0), (0, 1, 0), (0, -1, 0), (0, 0, 1), (0, 0, -1)]
WIDE = len(OFFSETS) * LANES
FAR = (SLAB + 2) * CX
CORNERS = FAR + SLAB * CX
PARTS = CORNERS + 16


def cell_code(x, y):
    return (x + 2) * 32 + y + 2


def write_selector(pick_ref):
    row = lax.broadcasted_iota(jnp.int32, (16, LANES), 0)
    lane = lax.broadcasted_iota(jnp.int32, (16, LANES), 1)
    own = cell_code(lax.shift_right_logical(lane, 3), lane & 7)

    def pair_of_x(x):
        return cell_code(x + lax.shift_right_logical(row, 3), row & 7)

    tiles = [pair_of_x(2 * i) for i in range(CX // 2)]
    tiles += [cell_code(row, y) for y in (-1, -2, CY, CY + 1)]
    for first, near in ((-2, -1), (CX, CX)):
        corners = jnp.where(row == 1, cell_code(near, CY), -1)
        tiles += [pair_of_x(first), jnp.where(row == 0, cell_code(near, -1), corners)]
    for i, tile in enumerate(tiles):
        for off, (dx, dy) in enumerate(OFFSETS):
            hit = jnp.where(tile == own + (dx * 32 + dy), 1.0, 0.0).astype(jnp.bfloat16)
            pick_ref[i * 16 : i * 16 + 16, off * LANES : (off + 1) * LANES] = hit


def slab_kernel(
    quad_ref, probes_ref, own_ref, first_ref, second_ref, third_ref, fourth_ref, block, side, rim, sems, *whole
):
    depth = probes_ref.shape[0]
    me = lax.axis_index("quad")
    even_x = (lax.axis_index("sx") & 1) == 0
    even_y = (lax.axis_index("sy") & 1) == 0

    group = 4 * SLAB + 4
    bases = [jnp.clip((me & ~3) * SLAB - 2, 0, depth - group)]
    bases += [jnp.clip((me ^ bit) * SLAB - 2, 0, depth - SLAB - 4) for bit in (4, 8)]
    held = (block, side.at[0], side.at[1])
    copies = [
        pltpu.make_async_copy(probes_ref.at[pl.ds(base, to.shape[0])], to, sems.at[i])
        for i, (base, to) in enumerate(zip(bases, held))
    ]
    edges = ((1, even_x), (8, jnp.logical_not(even_x)))
    for i, step in enumerate((4, 3)):
        for j, (bit, high) in enumerate(edges):
            at = pl.multiple_of(jnp.where(high, LANES - 16, 0), 16)
            start = ((me ^ step) ^ bit) * SLAB
            edge = probes_ref.at[pl.ds(start, SLAB), pl.ds(at, 16)]
            copies.append(pltpu.make_async_copy(edge, rim.at[2 * i + j], sems.at[len(copies)]))
    for copy in copies:
        copy.start()

    def plane(slab, p, bit=0):
        z = jnp.clip(slab * SLAB + (p - 2), 0, depth - 1)
        at = {4: 1, 8: 2}.get(bit, 0)
        return held[at][z - bases[at]]

    def x_edge(values, high):
        low, top = values[:16].astype(jnp.float32), values[LANES - 16 :].astype(jnp.float32)
        return jnp.where(high, top, low)

    index = jnp.full((1, LANES), quad_ref[0], jnp.int32).astype(jnp.float32)
    angle = 2.0 * math.pi * (index + 0.5) / (4 * QUAD)
    lane = lax.broadcasted_iota(jnp.int32, (1, LANES), 1)
    weight = jnp.where(lane == me, jnp.cos(angle), 0.0)
    weight = jnp.where(lane == me + QUAD, jnp.sin(angle), weight)
    row = lax.broadcasted_iota(jnp.int32, (16, LANES), 0)
    parts = jnp.zeros((16, LANES), jnp.float32)
    for i in range(3):
        part = weight.astype(jnp.bfloat16).astype(jnp.float32)
        parts = jnp.where(row == i, part, parts)
        weight = weight - part
    first_ref[PARTS : PARTS + 16] = parts.astype(jnp.bfloat16)
    second_ref[PARTS : PARTS + 16] = parts.astype(jnp.bfloat16)

    for copy in copies:
        copy.wait()
    sends = ((first_ref, whole[0], 4, even_y), (second_ref, whole[1], 3, jnp.logical_not(even_y)))
    for send, (out_ref, scratch, step, high) in enumerate(sends):
        target = me ^ step
        for p in range(1, SLAB + 3):
            scratch[(p - 1) * LANES : p * LANES] = plane(target, p, step).astype(jnp.float32)
        for at, start, count, deep in ((0, 0, SLAB + 2, 0), (FAR, LANES, SLAB, 1)):
            low = scratch[pl.ds(start + deep, count * CX, stride=CY), :]
            top = scratch[pl.ds(start + CY - 1 - deep, count * CX, stride=CY), :]
            out_ref[at : at + count * CX] = jnp.where(high, top, low).astype(jnp.bfloat16)
        corners = jnp.zeros((16, LANES), jnp.float32)
        for i, (bit, edge) in enumerate(edges):
            cell = jnp.where(edge, CY, 0) + jnp.where(high, CY - 1, 0)
            for p in range(SLAB):
                picked = jnp.where(row == cell, rim[2 * send + i, p].astype(jnp.float32), 0.0)
                picked = jnp.sum(picked, axis=0, keepdims=True)
                corners = jnp.where(row == i * SLAB + p, picked, corners)
        out_ref[CORNERS : CORNERS + 16] = corners.astype(jnp.bfloat16)

    for out_ref, (bit, high) in zip((third_ref, fourth_ref), edges):
        for p in range(1, SLAB + 3):
            out_ref[(p - 1) * 16 : p * 16] = x_edge(plane(me ^ bit, p, bit), high).astype(jnp.bfloat16)
    for p in range(SLAB + 4):
        own_ref[p] = plane(me, p)


def pack_kernel(inner_ref, outer_ref, last_ref, first_ref, third_ref, fourth_ref, near_ref, beyond_ref):
    even_y = (lax.axis_index("sy") & 1) == 0
    inner = inner_ref[CORNERS:].astype(jnp.float32)
    outer = outer_ref[CORNERS:].astype(jnp.float32)
    low, high = jnp.where(even_y, outer, inner), jnp.where(even_y, inner, outer)
    parts = (first_ref[PARTS:].astype(jnp.float32) + inner[16:]) + (
        outer[16:] + last_ref[...].astype(jnp.float32)
    )
    row = lax.broadcasted_iota(jnp.int32, (16, LANES), 0)
    for i, (layers_ref, out_ref) in enumerate(((third_ref, near_ref), (fourth_ref, beyond_ref))):
        out_ref[:FAR] = layers_ref[...]
        for p in range(SLAB):
            at = i * SLAB + p
            corner = jnp.where(row == 1, high[at : at + 1], 0.0)
            corner = jnp.where(row == 0, low[at : at + 1], corner)
            out_ref[FAR + p * 16 : FAR + (p + 1) * 16] = corner.astype(jnp.bfloat16)
        out_ref[CORNERS:] = parts.astype(jnp.bfloat16)


def material_kernel(eps_ref, gain_ref, region_ref, level_ref, out_ref, pick_ref, labels, codes, sems):
    planes = SLAB + 4
    start = lax.axis_index("quad") * SLAB
    first = jnp.clip(start - 2, 0, region_ref.shape[0] - planes)
    ahead = first - start + 4
    copies = [
        pltpu.make_async_copy(ref.at[pl.ds(first, planes)], labels.at[i], sems.at[i])
        for i, ref in enumerate((region_ref, level_ref))
    ]
    for copy in copies:
        copy.start()
    write_selector(pick_ref)
    depth_y, depth_x = labels.shape[2:]
    lane = lax.broadcasted_iota(jnp.int32, (depth_x, LANES), 1)
    x_row = lax.broadcasted_iota(jnp.int32, (depth_x, LANES), 0) - lax.axis_index("sx") * CX
    picks = [
        jnp.where(x_row == lax.shift_right_logical(lane, 3) + dx, 1.0, 0.0) for dx in range(-2, 3)
    ]
    pick = jnp.concatenate(picks, axis=1).astype(jnp.bfloat16)
    y_lane = lax.broadcasted_iota(jnp.int32, (depth_y, LANES), 1) & 7
    y_row = lax.broadcasted_iota(jnp.int32, (depth_y, LANES), 0) - lax.axis_index("sy") * CY
    for copy in copies:
        copy.wait()
    code = labels[0] * 8 + labels[1] + 1
    code = code.astype(jnp.float32).astype(jnp.bfloat16).reshape(planes * depth_y, depth_x)
    spread = jnp.dot(code, pick, preferred_element_type=jnp.float32)
    codes[...] = jnp.zeros(codes.shape, jnp.float32)
    for off, (dx, dy) in enumerate(OFFSETS):
        block = spread[:, (dx + 2) * LANES : (dx + 3) * LANES].reshape(planes, depth_y, LANES)
        picked = jnp.sum(jnp.where((y_row == y_lane + dy)[None], block, 0.0), axis=1)
        codes[off, pl.ds(ahead, planes), :] = picked
    for t, (dz, off) in enumerate(TAPS):
        row = dz + 4
        code = codes[off, row : row + SLAB, :]
        code = jnp.concatenate([code, code], axis=0).astype(jnp.int32)
        inside = code > 0
        code = code - 1
        region = lax.shift_right_logical(code, 3)
        level = code & 7
        real = jnp.zeros((8, LANES), jnp.float32)
        imag = jnp.zeros((8, LANES), jnp.float32)
        for value in range(8):
            real = jnp.where(region == value, eps_ref[value], real)
            imag = jnp.where(level == value, gain_ref[value], imag)
        out_ref[t] = real
        out_ref[len(TAPS) + t] = imag
        out_ref[2 * len(TAPS) + t] = jnp.where(inside, 1.0, 0.0)


def cmul(a, b):
    return (a[0] * b[0] - a[1] * b[1], a[0] * b[1] + a[1] * b[0])


def cadd(a, b):
    return (a[0] + b[0], a[1] + b[1])


def moment_kernel(
    weight_ref,
    material_ref,
    own_ref,
    ylo_ref,
    yhi_ref,
    xlo_ref,
    xhi_ref,
    pick_ref,
    moments_ref,
    cross_ref,
    shifted,
    coef,
    folded,
):
    for plane in range(SLAB + 4):
        near, far = (plane - 1) * 16, 96 + (plane - 2) * 16
        sides = (ylo_ref, yhi_ref, xlo_ref, xhi_ref)
        if 2 <= plane < SLAB + 2:
            reach, starts = 13, (near, far)
        elif plane in (1, SLAB + 2):
            reach, starts = 5, (near, near)
        else:
            reach, starts = 1, ()
        rows = [own_ref[plane]] + [ref[i : i + 16] for ref in sides for i in starts]
        rows = jnp.concatenate(rows, axis=0) if starts else rows[0]
        picked = lax.dot_general(
            rows,
            pick_ref[: rows.shape[0], : reach * LANES],
            (((0,), (0,)), ((), ())),
            preferred_element_type=jnp.float32,
        )
        for off in range(reach):
            shifted[plane, off] = picked[:, off * LANES : (off + 1) * LANES]

    coef[...] = jnp.zeros(coef.shape, jnp.float32)
    first_half = lax.broadcasted_iota(jnp.int32, (8, LANES), 0) < SLAB

    def one_pair(pair, carry):
        weight = (
            jnp.where(first_half, weight_ref[0, 2 * pair], weight_ref[0, 2 * pair + 1]),
            jnp.where(
                first_half, weight_ref[0, QUAD + 2 * pair], weight_ref[0, QUAD + 2 * pair + 1]
            ),
        )
        node = (2.0 + weight[0], weight[1])
        inv = []
        for t in range(len(TAPS)):
            real, imag = material_ref[t], material_ref[len(TAPS) + t]
            diag_real = 6.0 + node[0] * real - node[1] * imag
            diag_imag = node[0] * imag + node[1] * real
            scale = material_ref[2 * len(TAPS) + t] / (diag_real * diag_real + diag_imag * diag_imag)
            inv.append((diag_real * scale, -(diag_imag * scale)))
        centre = inv[TAP_AT[(0, 0, 0)]]
        lead0 = cmul(weight, centre)
        lead1 = cmul(node, lead0)
        for t, (dz, off) in enumerate(TAPS):
            step = (dz,) + OFFSETS[off]
            size = sum(abs(d) for d in step)
            if size == 0:
                near = functools.reduce(cadd, [inv[TAP_AT[u]] for u in UNITS])
                term = cmul(centre, near)
                term = (1.0 + term[0], term[1])
            elif size == 1:
                term = inv[t]
            else:
                mids = [
                    inv[TAP_AT[u]]
                    for u in UNITS
                    if sum(abs(s - d) for s, d in zip(step, u)) == 1
                ]
                term = cmul(inv[t], functools.reduce(cadd, mids))
            for k, lead in enumerate((lead0, lead1)):
                real, imag = cmul(lead, term)
                coef[4 * t + 2 * k] += real
                coef[4 * t + 2 * k + 1] += imag
        return carry

    lax.fori_loop(0, QUAD // 2, one_pair, 0)
    for i in range(2 * len(TAPS)):
        real, imag = coef[2 * i], coef[2 * i + 1]
        real = real + pltpu.roll(real, SLAB, axis=0)
        imag = imag + pltpu.roll(imag, SLAB, axis=0)
        folded[3 * i] = real
        folded[3 * i + 1] = imag - real
        folded[3 * i + 2] = real + imag

    half = 64
    part = 32

    def one_chunk(step, carry):
        z = step // 2
        col = pl.multiple_of((step % 2) * part, part)
        sums = [jnp.zeros((part, LANES), jnp.float32) for _ in range(6)]
        for t, (dz, off) in enumerate(TAPS):
            real = shifted[z + 2 + dz, off, pl.ds(col, part), :]
            imag = shifted[z + 2 + dz, off, pl.ds(half + col, part), :]
            factors = (real + imag, real, imag)
            for i in range(6):
                sums[i] += folded[6 * t + i, pl.ds(z, 1), :] * factors[i % 3]
        for k in range(2):
            both, minus, plus = sums[3 * k : 3 * k + 3]
            moments_ref[k, z, pl.ds(col, part), :] = both - plus
            moments_ref[k, z, pl.ds(half + col, part), :] = both + minus
        return carry

    lax.fori_loop(0, 2 * SLAB, one_chunk, 0)

    cross = jnp.zeros((half, 4 * half), jnp.float32)
    for z in range(SLAB):
        left = jnp.concatenate([shifted[z + 2, 0, :half], shifted[z + 2, 0, half:]], axis=1)
        left = left.astype(jnp.bfloat16)
        rows = []
        for k in range(2):
            real = moments_ref[k, z, :half]
            imag = moments_ref[k, z, half:]
            rows.append(jnp.concatenate([real, imag], axis=1))
            rows.append(jnp.concatenate([imag, -real], axis=1))
        right = jnp.concatenate(rows, axis=0)
        high = right.astype(jnp.bfloat16)
        low = (right - high.astype(jnp.float32)).astype(jnp.bfloat16)
        for piece in (high, low):
            cross += lax.dot_general(
                left, piece, (((1,), (1,)), ((), ())), preferred_element_type=jnp.float32
            )
    cross_ref[...] = cross * (1.0 / 131072)


def turn_kernel(moments_ref, first_ref, second_ref):
    for k, out_ref in enumerate((first_ref, second_ref)):
        for z in range(SLAB):
            out_ref[z] = moments_ref[k, z].T


def turn(moments, columns):
    out = jax.ShapeDtypeStruct((SLAB, LANES, columns), jnp.float32)
    vmem = pl.BlockSpec(memory_space=pltpu.VMEM)
    return pl.pallas_call(
        turn_kernel,
        out_shape=[out] * 2,
        in_specs=[vmem],
        out_specs=[vmem] * 2,
        compiler_params=pltpu.CompilerParams(vmem_limit_bytes=8 * 1024 * 1024),
        cost_estimate=pl.CostEstimate(flops=1000000, bytes_accessed=1000000, transcendentals=0),
        name="turn",
    )(moments)


def swap(block, bits):
    axes = tuple(bits)
    sizes = [lax.axis_size(axis) for axis in axes]
    pairs = []
    for place in np.ndindex(*sizes):
        other = tuple(i ^ bit for i, bit in zip(place, bits.values()))
        pairs.append((int(np.ravel_multi_index(place, sizes)), int(np.ravel_multi_index(other, sizes))))
    return lax.ppermute(block, axes, pairs)


def sum_of_four(block, *steps):
    first, second, third = (swap(block, step) for step in steps)
    return (block + first) + (second + third)


def body(probes, quad_index, region_label, gain_label, region_eps, gain_rate):
    depth, cells_x, cells_y, columns = probes.shape
    planes = SLAB + 4
    core = lax.axis_index("sx") & 1
    even_x = core == 0
    even_y = (lax.axis_index("sy") & 1) == 0
    smem = pl.BlockSpec(memory_space=pltpu.SMEM)
    vmem = pl.BlockSpec(memory_space=pltpu.VMEM)
    hbm = pl.BlockSpec(memory_space=pltpu.HBM)
    mib = 1024 * 1024
    shapes = [
        (planes, cells_x * cells_y, columns),
        (PARTS + 16, columns),
        (PARTS + 16, columns),
        (FAR, columns),
        (FAR, columns),
    ]
    own, first, second, third, fourth = pl.pallas_call(
        slab_kernel,
        out_shape=[jax.ShapeDtypeStruct(shape, probes.dtype) for shape in shapes],
        in_specs=[smem, hbm],
        out_specs=[vmem] * 5,
        scratch_shapes=[
            pltpu.VMEM((4 * SLAB + 4, cells_x * cells_y, columns), probes.dtype),
            pltpu.VMEM((2, planes, cells_x * cells_y, columns), probes.dtype),
            pltpu.VMEM((4, SLAB, 16, columns), probes.dtype),
            pltpu.SemaphoreType.DMA((7,)),
        ]
        + [pltpu.VMEM(((SLAB + 2) * LANES, columns), jnp.float32)] * 2,
        compiler_params=pltpu.CompilerParams(vmem_limit_bytes=52 * mib),
        cost_estimate=pl.CostEstimate(flops=10000000, bytes_accessed=600000, transcendentals=0),
        name="slab",
    )(quad_index, probes.reshape(depth, cells_x * cells_y, columns))

    inner = swap(first, dict(quad=4, sy=1))
    outer = swap(second, dict(quad=3, sy=3))
    last = swap(first[PARTS:], dict(quad=7))
    ylo = jnp.where(even_y, outer, inner)[:CORNERS]
    yhi = jnp.where(even_y, inner, outer)[:CORNERS]
    to_near, to_beyond = pl.pallas_call(
        pack_kernel,
        out_shape=[jax.ShapeDtypeStruct((CORNERS + 16, columns), probes.dtype)] * 2,
        in_specs=[vmem] * 6,
        out_specs=[vmem] * 2,
        compiler_params=pltpu.CompilerParams(vmem_limit_bytes=4 * mib),
        cost_estimate=pl.CostEstimate(flops=100000, bytes_accessed=200000, transcendentals=0),
        name="pack",
    )(inner, outer, last, first, third, fourth)
    beyond = swap(to_beyond, dict(quad=8, sx=3))
    near = swap(to_near, dict(quad=1, sx=1))
    parts = to_near[CORNERS:]
    last = swap(parts, dict(quad=9))
    parts = (parts + near[CORNERS:]) + (beyond[CORNERS:] + last)
    xlo = jnp.where(even_x, beyond, near)[:CORNERS]
    xhi = jnp.where(even_x, near, beyond)[:CORNERS]
    weight = jnp.sum(parts[:3].astype(jnp.float32), axis=0, keepdims=True)

    taps = len(TAPS)
    material, pick = pl.pallas_call(
        material_kernel,
        out_shape=[
            jax.ShapeDtypeStruct((3 * taps, 8, LANES), jnp.float32),
            jax.ShapeDtypeStruct((256, WIDE), jnp.bfloat16),
        ],
        in_specs=[smem, smem, hbm, hbm],
        out_specs=[vmem] * 2,
        scratch_shapes=[
            pltpu.VMEM((2, planes) + region_label.shape[:0:-1], jnp.int32),
            pltpu.VMEM((len(OFFSETS), 16, LANES), jnp.float32),
            pltpu.SemaphoreType.DMA((2,)),
        ],
        compiler_params=pltpu.CompilerParams(vmem_limit_bytes=52 * mib),
        cost_estimate=pl.CostEstimate(flops=40000000, bytes_accessed=1200000, transcendentals=0),
        name="material",
    )(region_eps, gain_rate, region_label.swapaxes(1, 2), gain_label.swapaxes(1, 2))

    moments, cross = pl.pallas_call(
        moment_kernel,
        out_shape=[
            jax.ShapeDtypeStruct((2, SLAB, columns, LANES), jnp.float32),
            jax.ShapeDtypeStruct((64, 256), jnp.float32),
        ],
        in_specs=[smem] + [vmem] * 7,
        out_specs=[vmem] * 2,
        scratch_shapes=[
            pltpu.VMEM((planes, len(OFFSETS), columns, LANES), jnp.float32),
            pltpu.VMEM((4 * taps, 8, LANES), jnp.float32),
            pltpu.VMEM((6 * taps, 8, LANES), jnp.float32),
        ],
        compiler_params=pltpu.CompilerParams(vmem_limit_bytes=24 * mib),
        cost_estimate=pl.CostEstimate(flops=600000000, bytes_accessed=3000000, transcendentals=0),
        name="moments",
    )(weight, material, own, ylo, yhi, xlo, xhi, pick)

    width = cross.shape[1] // 2
    block = jnp.where(core == 0, cross[:, :width], cross[:, width:])
    block = block + swap(jnp.where(core == 0, cross[:, width:], cross[:, :width]), dict(sx=1))
    block = sum_of_four(block, dict(sy=1), dict(sy=3), dict(sy=2))
    block = sum_of_four(block, dict(quad=1), dict(quad=3), dict(quad=2))
    block = sum_of_four(block, dict(quad=4), dict(quad=8, sx=2), dict(quad=12, sx=2))
    block, moments = lax.optimization_barrier((block, moments))
    block = block + swap(block, dict(quad=8))
    first, second = turn(moments, columns)
    block, first, second = lax.optimization_barrier((block, first, second))
    other = swap(block, dict(sx=1))
    halves = (jnp.where(core == 0, block, other), jnp.where(core == 0, other, block))
    projections = jnp.stack(
        [jnp.stack([half[:, :64], half[:, 64:]], axis=0) for half in halves], axis=0
    )
    shape = (SLAB, cells_x, cells_y, columns)
    return (first.reshape(shape), second.reshape(shape), projections)


def solution(mesh):
    placed = (P(None, "sx", "sy", None), P("quad"), P(), P(), P(), P())
    return jax.shard_map(
        body,
        mesh=mesh,
        in_specs=placed,
        out_specs=(P("quad", "sx", "sy", None), P("quad", "sx", "sy", None), P()),
        check_vma=False,
    )
```

```python
import functools
import math

import jax
import jax.numpy as jnp
import numpy as np
from jax import lax
from jax.experimental import pallas as pl
from jax.experimental.pallas import tpu as pltpu
from jax.sharding import PartitionSpec as P

QUAD = 16
SLAB = 4
CX = 16
CY = 8
LANES = CX * CY

OFFSETS = sorted(
    [(dx, dy) for dx in range(-2, 3) for dy in range(-2, 3) if abs(dx) + abs(dy) <= 2],
    key=lambda o: (abs(o[0]) + abs(o[1]), o),
)
REACH = {0: 13, 1: 5, 2: 1}
TAPS = [(dz, off) for dz in range(-2, 3) for off in range(REACH[abs(dz)])]
TAP_AT = {(dz,) + OFFSETS[off]: i for i, (dz, off) in enumerate(TAPS)}
UNITS = [(1, 0, 0), (-1, 0, 0), (0, 1, 0), (0, -1, 0), (0, 0, 1), (0, 0, -1)]
WIDE = len(OFFSETS) * LANES
FAR = (SLAB + 2) * CX
CORNERS = FAR + SLAB * CX
PARTS = CORNERS + 16


def cell_code(x, y):
    return (x + 2) * 32 + y + 2


def write_selector(pick_ref):
    row = lax.broadcasted_iota(jnp.int32, (16, LANES), 0)
    lane = lax.broadcasted_iota(jnp.int32, (16, LANES), 1)
    own = cell_code(lax.shift_right_logical(lane, 3), lane & 7)

    def pair_of_x(x):
        return cell_code(x + lax.shift_right_logical(row, 3), row & 7)

    tiles = [pair_of_x(2 * i) for i in range(CX // 2)]
    tiles += [cell_code(row, y) for y in (-1, -2, CY, CY + 1)]
    for first, near in ((-2, -1), (CX, CX)):
        corners = jnp.where(row == 1, cell_code(near, CY), -1)
        tiles += [pair_of_x(first), jnp.where(row == 0, cell_code(near, -1), corners)]
    for i, tile in enumerate(tiles):
        for off, (dx, dy) in enumerate(OFFSETS):
            hit = jnp.where(tile == own + (dx * 32 + dy), 1.0, 0.0).astype(jnp.bfloat16)
            pick_ref[i * 16 : i * 16 + 16, off * LANES : (off + 1) * LANES] = hit


def slab_kernel(
    quad_ref, probes_ref, own_ref, first_ref, second_ref, third_ref, fourth_ref, block, side, rim, sems, *whole
):
    depth = probes_ref.shape[0]
    me = lax.axis_index("quad")
    even_x = (lax.axis_index("sx") & 1) == 0
    even_y = (lax.axis_index("sy") & 1) == 0

    group = 4 * SLAB + 4
    bases = [jnp.clip((me & ~3) * SLAB - 2, 0, depth - group)]
    bases += [jnp.clip((me ^ bit) * SLAB - 2, 0, depth - SLAB - 4) for bit in (4, 8)]
    held = (block, side.at[0], side.at[1])
    copies = [
        pltpu.make_async_copy(probes_ref.at[pl.ds(base, to.shape[0])], to, sems.at[i])
        for i, (base, to) in enumerate(zip(bases, held))
    ]
    edges = ((4, even_x), (8, jnp.logical_not(even_x)))
    for i, step in enumerate((1, 3)):
        for j, (bit, high) in enumerate(edges):
            at = pl.multiple_of(jnp.where(high, LANES - 16, 0), 16)
            start = ((me ^ step) ^ bit) * SLAB
            edge = probes_ref.at[pl.ds(start, SLAB), pl.ds(at, 16)]
            copies.append(pltpu.make_async_copy(edge, rim.at[2 * i + j], sems.at[len(copies)]))
    for copy in copies:
        copy.start()

    def plane(slab, p, bit=0):
        z = jnp.clip(slab * SLAB + (p - 2), 0, depth - 1)
        at = {0: 0, 4: 1, 8: 2}[bit]
        return held[at][z - bases[at]]

    def x_edge(values, high):
        low, top = values[:16].astype(jnp.float32), values[LANES - 16 :].astype(jnp.float32)
        return jnp.where(high, top, low)

    index = jnp.full((1, LANES), quad_ref[0], jnp.int32).astype(jnp.float32)
    angle = 2.0 * math.pi * (index + 0.5) / (4 * QUAD)
    lane = lax.broadcasted_iota(jnp.int32, (1, LANES), 1)
    weight = jnp.where(lane == me, jnp.cos(angle), 0.0)
    weight = jnp.where(lane == me + QUAD, jnp.sin(angle), weight)
    row = lax.broadcasted_iota(jnp.int32, (16, LANES), 0)
    parts = jnp.zeros((16, LANES), jnp.float32)
    for i in range(3):
        part = weight.astype(jnp.bfloat16).astype(jnp.float32)
        parts = jnp.where(row == i, part, parts)
        weight = weight - part
    first_ref[PARTS : PARTS + 16] = parts.astype(jnp.bfloat16)
    second_ref[PARTS : PARTS + 16] = parts.astype(jnp.bfloat16)

    for copy in copies:
        copy.wait()
    sends = ((first_ref, whole[0], 1, even_y), (second_ref, whole[1], 3, jnp.logical_not(even_y)))
    for send, (out_ref, scratch, step, high) in enumerate(sends):
        target = me ^ step
        for p in range(1, SLAB + 3):
            scratch[(p - 1) * LANES : p * LANES] = plane(target, p).astype(jnp.float32)
        for at, start, count, deep in ((0, 0, SLAB + 2, 0), (FAR, LANES, SLAB, 1)):
            low = scratch[pl.ds(start + deep, count * CX, stride=CY), :]
            top = scratch[pl.ds(start + CY - 1 - deep, count * CX, stride=CY), :]
            out_ref[at : at + count * CX] = jnp.where(high, top, low).astype(jnp.bfloat16)
        corners = jnp.zeros((16, LANES), jnp.float32)
        for i, (bit, edge) in enumerate(edges):
            cell = jnp.where(edge, CY, 0) + jnp.where(high, CY - 1, 0)
            for p in range(SLAB):
                picked = jnp.where(row == cell, rim[2 * send + i, p].astype(jnp.float32), 0.0)
                picked = jnp.sum(picked, axis=0, keepdims=True)
                corners = jnp.where(row == i * SLAB + p, picked, corners)
        out_ref[CORNERS : CORNERS + 16] = corners.astype(jnp.bfloat16)

    for out_ref, (bit, high) in zip((third_ref, fourth_ref), edges):
        for p in range(1, SLAB + 3):
            out_ref[(p - 1) * 16 : p * 16] = x_edge(plane(me ^ bit, p, bit), high).astype(jnp.bfloat16)
    for p in range(SLAB + 4):
        own_ref[p] = plane(me, p)


def material_kernel(eps_ref, gain_ref, region_ref, level_ref, out_ref, pick_ref, labels, codes, sems):
    planes = SLAB + 4
    start = lax.axis_index("quad") * SLAB
    first = jnp.clip(start - 2, 0, region_ref.shape[0] - planes)
    ahead = first - start + 4
    copies = [
        pltpu.make_async_copy(ref.at[pl.ds(first, planes)], labels.at[i], sems.at[i])
        for i, ref in enumerate((region_ref, level_ref))
    ]
    for copy in copies:
        copy.start()
    write_selector(pick_ref)
    depth_y, depth_x = labels.shape[2:]
    lane = lax.broadcasted_iota(jnp.int32, (depth_x, LANES), 1)
    x_row = lax.broadcasted_iota(jnp.int32, (depth_x, LANES), 0) - lax.axis_index("sx") * CX
    picks = [
        jnp.where(x_row == lax.shift_right_logical(lane, 3) + dx, 1.0, 0.0) for dx in range(-2, 3)
    ]
    pick = jnp.concatenate(picks, axis=1).astype(jnp.bfloat16)
    y_lane = lax.broadcasted_iota(jnp.int32, (depth_y, LANES), 1) & 7
    y_row = lax.broadcasted_iota(jnp.int32, (depth_y, LANES), 0) - lax.axis_index("sy") * CY
    for copy in copies:
        copy.wait()
    code = labels[0] * 8 + labels[1] + 1
    code = code.astype(jnp.float32).astype(jnp.bfloat16).reshape(planes * depth_y, depth_x)
    spread = jnp.dot(code, pick, preferred_element_type=jnp.float32)
    codes[...] = jnp.zeros(codes.shape, jnp.float32)
    for off, (dx, dy) in enumerate(OFFSETS):
        block = spread[:, (dx + 2) * LANES : (dx + 3) * LANES].reshape(planes, depth_y, LANES)
        picked = jnp.sum(jnp.where((y_row == y_lane + dy)[None], block, 0.0), axis=1)
        codes[off, pl.ds(ahead, planes), :] = picked
    for t, (dz, off) in enumerate(TAPS):
        row = dz + 4
        code = codes[off, row : row + SLAB, :]
        code = jnp.concatenate([code, code], axis=0).astype(jnp.int32)
        inside = code > 0
        code = code - 1
        region = lax.shift_right_logical(code, 3)
        level = code & 7
        real = jnp.zeros((8, LANES), jnp.float32)
        imag = jnp.zeros((8, LANES), jnp.float32)
        for value in range(8):
            real = jnp.where(region == value, eps_ref[value], real)
            imag = jnp.where(level == value, gain_ref[value], imag)
        out_ref[t] = real
        out_ref[len(TAPS) + t] = imag
        out_ref[2 * len(TAPS) + t] = jnp.where(inside, 1.0, 0.0)


def cmul(a, b):
    return (a[0] * b[0] - a[1] * b[1], a[0] * b[1] + a[1] * b[0])


def cadd(a, b):
    return (a[0] + b[0], a[1] + b[1])


def moment_kernel(
    weight_ref,
    material_ref,
    own_ref,
    ylo_ref,
    yhi_ref,
    xlo_ref,
    xhi_ref,
    pick_ref,
    moments_ref,
    cross_ref,
    shifted,
    coef,
    folded,
):
    for plane in range(SLAB + 4):
        near, far = (plane - 1) * 16, 96 + (plane - 2) * 16
        sides = (ylo_ref, yhi_ref, xlo_ref, xhi_ref)
        if 2 <= plane < SLAB + 2:
            reach, starts = 13, (near, far)
        elif plane in (1, SLAB + 2):
            reach, starts = 5, (near, near)
        else:
            reach, starts = 1, ()
        rows = [own_ref[plane]] + [ref[i : i + 16] for ref in sides for i in starts]
        rows = jnp.concatenate(rows, axis=0) if starts else rows[0]
        picked = lax.dot_general(
            rows,
            pick_ref[: rows.shape[0], : reach * LANES],
            (((0,), (0,)), ((), ())),
            preferred_element_type=jnp.float32,
        )
        for off in range(reach):
            shifted[plane, off] = picked[:, off * LANES : (off + 1) * LANES]

    coef[...] = jnp.zeros(coef.shape, jnp.float32)
    first_half = lax.broadcasted_iota(jnp.int32, (8, LANES), 0) < SLAB

    def one_pair(pair, carry):
        weight = (
            jnp.where(first_half, weight_ref[0, 2 * pair], weight_ref[0, 2 * pair + 1]),
            jnp.where(
                first_half, weight_ref[0, QUAD + 2 * pair], weight_ref[0, QUAD + 2 * pair + 1]
            ),
        )
        node = (2.0 + weight[0], weight[1])
        inv = []
        for t in range(len(TAPS)):
            real, imag = material_ref[t], material_ref[len(TAPS) + t]
            diag_real = 6.0 + node[0] * real - node[1] * imag
            diag_imag = node[0] * imag + node[1] * real
            scale = material_ref[2 * len(TAPS) + t] / (diag_real * diag_real + diag_imag * diag_imag)
            inv.append((diag_real * scale, -(diag_imag * scale)))
        centre = inv[TAP_AT[(0, 0, 0)]]
        lead0 = cmul(weight, centre)
        lead1 = cmul(node, lead0)
        for t, (dz, off) in enumerate(TAPS):
            step = (dz,) + OFFSETS[off]
            size = sum(abs(d) for d in step)
            if size == 0:
                near = functools.reduce(cadd, [inv[TAP_AT[u]] for u in UNITS])
                term = cmul(centre, near)
                term = (1.0 + term[0], term[1])
            elif size == 1:
                term = inv[t]
            else:
                mids = [
                    inv[TAP_AT[u]]
                    for u in UNITS
                    if sum(abs(s - d) for s, d in zip(step, u)) == 1
                ]
                term = cmul(inv[t], functools.reduce(cadd, mids))
            for k, lead in enumerate((lead0, lead1)):
                real, imag = cmul(lead, term)
                coef[4 * t + 2 * k] += real
                coef[4 * t + 2 * k + 1] += imag
        return carry

    lax.fori_loop(0, QUAD // 2, one_pair, 0, unroll=2)
    for i in range(2 * len(TAPS)):
        real, imag = coef[2 * i], coef[2 * i + 1]
        real = real + pltpu.roll(real, SLAB, axis=0)
        imag = imag + pltpu.roll(imag, SLAB, axis=0)
        folded[3 * i] = real
        folded[3 * i + 1] = imag - real
        folded[3 * i + 2] = real + imag

    half = 64
    part = 32

    def one_chunk(step, carry):
        z = step // 2
        col = pl.multiple_of((step % 2) * part, part)
        sums = [jnp.zeros((part, LANES), jnp.float32) for _ in range(6)]
        for t, (dz, off) in enumerate(TAPS):
            real = shifted[z + 2 + dz, off, pl.ds(col, part), :]
            imag = shifted[z + 2 + dz, off, pl.ds(half + col, part), :]
            factors = (real + imag, real, imag)
            for i in range(6):
                sums[i] += folded[6 * t + i, pl.ds(z, 1), :] * factors[i % 3]
        for k in range(2):
            both, minus, plus = sums[3 * k : 3 * k + 3]
            moments_ref[k, z, pl.ds(col, part), :] = both - plus
            moments_ref[k, z, pl.ds(half + col, part), :] = both + minus
        return carry

    lax.fori_loop(0, 2 * SLAB, one_chunk, 0)

    cross = jnp.zeros((half, 4 * half), jnp.float32)
    for z in range(SLAB):
        left = jnp.concatenate([shifted[z + 2, 0, :half], shifted[z + 2, 0, half:]], axis=1)
        left = left.astype(jnp.bfloat16)
        rows = []
        for k in range(2):
            real = moments_ref[k, z, :half]
            imag = moments_ref[k, z, half:]
            rows.append(jnp.concatenate([real, imag], axis=1))
            rows.append(jnp.concatenate([imag, -real], axis=1))
        right = jnp.concatenate(rows, axis=0)
        high = right.astype(jnp.bfloat16)
        low = (right - high.astype(jnp.float32)).astype(jnp.bfloat16)
        for piece in (high, low):
            cross += lax.dot_general(
                left, piece, (((1,), (1,)), ((), ())), preferred_element_type=jnp.float32
            )
    cross_ref[...] = cross * (1.0 / 131072)


def turn_kernel(moments_ref, first_ref, second_ref):
    for k, out_ref in enumerate((first_ref, second_ref)):
        for z in range(SLAB):
            out_ref[z] = moments_ref[k, z].T


def turn(moments, columns):
    out = jax.ShapeDtypeStruct((SLAB, LANES, columns), jnp.float32)
    vmem = pl.BlockSpec(memory_space=pltpu.VMEM)
    return pl.pallas_call(
        turn_kernel,
        out_shape=[out] * 2,
        in_specs=[vmem],
        out_specs=[vmem] * 2,
        compiler_params=pltpu.CompilerParams(vmem_limit_bytes=8 * 1024 * 1024),
        cost_estimate=pl.CostEstimate(flops=1000000, bytes_accessed=1000000, transcendentals=0),
        name="turn",
    )(moments)


def swap(block, bits):
    axes = tuple(bits)
    sizes = [lax.axis_size(axis) for axis in axes]
    pairs = []
    for place in np.ndindex(*sizes):
        other = tuple(i ^ bit for i, bit in zip(place, bits.values()))
        pairs.append((int(np.ravel_multi_index(place, sizes)), int(np.ravel_multi_index(other, sizes))))
    return lax.ppermute(block, axes, pairs)


def sum_of_four(block, *steps):
    first, second, third = (swap(block, step) for step in steps)
    return (block + first) + (second + third)


def body(probes, quad_index, region_label, gain_label, region_eps, gain_rate):
    depth, cells_x, cells_y, columns = probes.shape
    planes = SLAB + 4
    core = lax.axis_index("sx") & 1
    even_x = core == 0
    even_y = (lax.axis_index("sy") & 1) == 0
    smem = pl.BlockSpec(memory_space=pltpu.SMEM)
    vmem = pl.BlockSpec(memory_space=pltpu.VMEM)
    hbm = pl.BlockSpec(memory_space=pltpu.HBM)
    mib = 1024 * 1024
    shapes = [
        (planes, cells_x * cells_y, columns),
        (PARTS + 16, columns),
        (PARTS + 16, columns),
        (FAR, columns),
        (FAR, columns),
    ]
    own, first, second, third, fourth = pl.pallas_call(
        slab_kernel,
        out_shape=[jax.ShapeDtypeStruct(shape, probes.dtype) for shape in shapes],
        in_specs=[smem, hbm],
        out_specs=[vmem] * 5,
        scratch_shapes=[
            pltpu.VMEM((4 * SLAB + 4, cells_x * cells_y, columns), probes.dtype),
            pltpu.VMEM((2, planes, cells_x * cells_y, columns), probes.dtype),
            pltpu.VMEM((4, SLAB, 16, columns), probes.dtype),
            pltpu.SemaphoreType.DMA((7,)),
        ]
        + [pltpu.VMEM(((SLAB + 2) * LANES, columns), jnp.float32)] * 2,
        compiler_params=pltpu.CompilerParams(vmem_limit_bytes=52 * mib),
        cost_estimate=pl.CostEstimate(flops=10000000, bytes_accessed=600000, transcendentals=0),
        name="slab",
    )(quad_index, probes.reshape(depth, cells_x * cells_y, columns))

    def corner_rows(at):
        cells = [inner[at : at + SLAB], outer[at : at + SLAB]]
        low, high = jnp.where(even_y, cells[1], cells[0]), jnp.where(even_y, cells[0], cells[1])
        rows = jnp.pad(jnp.stack([low, high], axis=1), ((0, 0), (0, 14), (0, 0)))
        return rows.reshape(SLAB * 16, columns)

    parts = first[PARTS:]
    inner = swap(first, dict(quad=1, sy=1))
    outer = swap(second, dict(quad=3, sy=3))
    last = swap(parts, dict(quad=2))
    parts = (parts + inner[PARTS:]) + (outer[PARTS:] + last)
    ylo = jnp.where(even_y, outer, inner)[:CORNERS]
    yhi = jnp.where(even_y, inner, outer)[:CORNERS]
    third = jnp.concatenate([third, corner_rows(CORNERS), parts], axis=0)
    fourth = jnp.concatenate([fourth, corner_rows(CORNERS + SLAB), parts], axis=0)
    near = swap(third, dict(quad=4, sx=1))
    beyond = swap(fourth, dict(quad=8, sx=3))
    last = swap(parts, dict(quad=12))
    parts = (parts + near[CORNERS:]) + (beyond[CORNERS:] + last)
    xlo = jnp.where(even_x, beyond, near)[:CORNERS]
    xhi = jnp.where(even_x, near, beyond)[:CORNERS]
    weight = jnp.sum(parts[:3].astype(jnp.float32), axis=0, keepdims=True)

    taps = len(TAPS)
    material, pick = pl.pallas_call(
        material_kernel,
        out_shape=[
            jax.ShapeDtypeStruct((3 * taps, 8, LANES), jnp.float32),
            jax.ShapeDtypeStruct((256, WIDE), jnp.bfloat16),
        ],
        in_specs=[smem, smem, hbm, hbm],
        out_specs=[vmem] * 2,
        scratch_shapes=[
            pltpu.VMEM((2, planes) + region_label.shape[:0:-1], jnp.int32),
            pltpu.VMEM((len(OFFSETS), 16, LANES), jnp.float32),
            pltpu.SemaphoreType.DMA((2,)),
        ],
        compiler_params=pltpu.CompilerParams(vmem_limit_bytes=52 * mib),
        cost_estimate=pl.CostEstimate(flops=40000000, bytes_accessed=1200000, transcendentals=0),
        name="material",
    )(region_eps, gain_rate, region_label.swapaxes(1, 2), gain_label.swapaxes(1, 2))

    moments, cross = pl.pallas_call(
        moment_kernel,
        out_shape=[
            jax.ShapeDtypeStruct((2, SLAB, columns, LANES), jnp.float32),
            jax.ShapeDtypeStruct((64, 256), jnp.float32),
        ],
        in_specs=[smem] + [vmem] * 7,
        out_specs=[vmem] * 2,
        scratch_shapes=[
            pltpu.VMEM((planes, len(OFFSETS), columns, LANES), jnp.float32),
            pltpu.VMEM((4 * taps, 8, LANES), jnp.float32),
            pltpu.VMEM((6 * taps, 8, LANES), jnp.float32),
        ],
        compiler_params=pltpu.CompilerParams(vmem_limit_bytes=24 * mib),
        cost_estimate=pl.CostEstimate(flops=600000000, bytes_accessed=3000000, transcendentals=0),
        name="moments",
    )(weight, material, own, ylo, yhi, xlo, xhi, pick)

    width = cross.shape[1] // 2
    block = jnp.where(core == 0, cross[:, :width], cross[:, width:])
    block = block + swap(jnp.where(core == 0, cross[:, width:], cross[:, :width]), dict(sx=1))
    block = sum_of_four(block, dict(sy=1), dict(sy=3), dict(sy=2))
    block = sum_of_four(block, dict(quad=1), dict(quad=3), dict(quad=2))
    block = sum_of_four(block, dict(quad=4), dict(quad=8, sx=2), dict(quad=12, sx=2))
    block, moments = lax.optimization_barrier((block, moments))
    block = block + swap(block, dict(quad=8))
    first, second = turn(moments, columns)
    block, first, second = lax.optimization_barrier((block, first, second))
    other = swap(block, dict(sx=1))
    halves = (jnp.where(core == 0, block, other), jnp.where(core == 0, other, block))
    projections = jnp.stack(
        [jnp.stack([half[:, :64], half[:, 64:]], axis=0) for half in halves], axis=0
    )
    shape = (SLAB, cells_x, cells_y, columns)
    return (first.reshape(shape), second.reshape(shape), projections)


def solution(mesh):
    placed = (P(None, "sx", "sy", None), P("quad"), P(), P(), P(), P())
    return jax.shard_map(
        body,
        mesh=mesh,
        in_specs=placed,
        out_specs=(P("quad", "sx", "sy", None), P("quad", "sx", "sy", None), P()),
        check_vma=False,
    )
```
